32 devices in a mesh: dp: 2 (over y), expert: 16 (over z, x, core).
Axes of the slice: x: 2, y: 2, z: 4, core: 2. Of those that a mesh axis runs over, the one named last changes fastest.
Arguments:
- tokens: bfloat16 [4096, 4096], P(('dp', 'expert')), may hold values from -6 to 6
- expert_ids: int32 [4096, 2], P(('dp', 'expert')), may hold values from 0 to 63, as said below
- gate_values: float32 [4096, 2], P(('dp', 'expert')), may hold values from 0.2 to 1
- w_gate: bfloat16 [4096, 14336], P('dp', 'expert'), may hold values from -0.09375 to 0.09375
- w_up: bfloat16 [4096, 14336], P('dp', 'expert'), may hold values from -0.09375 to 0.09375
- w_down: bfloat16 [14336, 4096], P('expert', 'dp'), may hold values from -0.046875 to 0.046875
- target: bfloat16 [4096, 4096], P(('dp', 'expert')), may hold values from -6 to 6
Outputs:
- token_grad: bfloat16 [4096, 4096], P(('dp', 'expert'))
- gate_grad: bfloat16 [4096, 14336], P('dp', 'expert')
- up_grad: bfloat16 [4096, 14336], P('dp', 'expert')
The draws below stay inside these ranges and needn't reach their ends.
Inputs may be any that keep to these rules, and one draw needn't show every extreme that they name: `expert_ids`: A token's two expert ids differ, and no token names two experts below 1. Among the 128 tokens of one device each expert below 1 is named by 1 to 3 tokens, and in every draw some device names each of them exactly 3 times.
All inputs are finite; a program needn't handle non-finite values.
Results may differ from the reference program's by a relative error of at most 0.008.
Values may be sent and summed in bfloat16 or wider, within the bound.
No kernel may reach another device: no remote copies, remote signals or barrier semaphores. Data moves between devices by JAX's collectives and lax.ppermute only.
A program may use at most 128 MiB of HBM per device.

```python
import math
import jax
import jax.numpy as jnp
from jax import lax

D = 4096
HID = 14336
ROUTED = 64
EXPERTS = 1
TOK_DEV = 128
GROUP = 16
CAP = 3
TOKENS = 4096
N_DP = 2
N_EXPERT = 16


def draw_expert_ids(key, part):
    blocks = N_DP * N_EXPERT
    key_counts, key_full, key_perm, key_first, key_second, key_order = jax.random.split(key, 6)
    counts = jax.random.randint(key_counts, (blocks, EXPERTS), 1, CAP + 1)
    full_block = jax.random.randint(key_full, (), 0, blocks)
    counts = jnp.where(jnp.arange(blocks)[:, None] == full_block, CAP, counts)
    count_ends = jnp.cumsum(counts, axis=1)
    permuted = jax.vmap(lambda one_key: jax.random.permutation(one_key, TOK_DEV))(jax.random.split(key_perm, blocks))
    token_rank = jnp.argsort(permuted, axis=1)
    window_expert = jnp.sum((token_rank[:, :, None] >= count_ends[:, None, :]).astype(jnp.int32), axis=2)
    in_window = window_expert < EXPERTS
    outside = ROUTED - EXPERTS
    first_choice = EXPERTS + jax.random.randint(key_first, (blocks, TOK_DEV), 0, outside)
    second = EXPERTS + (first_choice - EXPERTS + jax.random.randint(key_second, (blocks, TOK_DEV), 1, outside)) % outside
    chosen = jnp.where(in_window, window_expert, second)
    swap_order = jax.random.randint(key_order, (blocks, TOK_DEV), 0, 2)
    column_zero = jnp.where(swap_order == 1, chosen, first_choice)
    column_one = jnp.where(swap_order == 1, first_choice, chosen)
    return jnp.stack([column_zero, column_one], axis=-1).reshape(blocks * TOK_DEV, 2).astype(jnp.int32)


def block_scale(key, dims, cuts, smallest, high):
    level = 1.0
    for dim, shards_of in cuts:
        draws = jax.random.uniform(jax.random.fold_in(jax.random.fold_in(key, 6), dim), (shards_of,), jnp.float32, smallest / len(cuts), high / len(cuts))
        level = level * jnp.repeat(jnp.exp(draws), dims[dim] // shards_of).reshape((-1,) + (1,) * (len(dims) - 1 - dim))
    return level


def centred(own_key, extent, spread, limit, cuts=(), kind=jnp.bfloat16):
    drawn = jax.random.normal(own_key, extent, jnp.float32) * spread
    if len(cuts) > 0:
        drawn = block_scale(own_key, extent, cuts, -0.22, 0.18) * drawn
    return jnp.clip(drawn, min=-limit, max=limit).astype(kind)


def setup_inputs(seed: int = 0) -> dict:
    seeds = jax.random.split(jax.random.key(seed), 8)
    tokens = centred(seeds[0], (TOKENS, D), 1.0, 6.0, ((0, 32),))
    expert_ids = draw_expert_ids(jax.random.fold_in(seeds[7], 71), 0)
    gate_values = jnp.clip(jnp.exp(math.log(1.0) - 1.609438 * jax.random.uniform(seeds[2], (TOKENS, 2), jnp.float32) ** block_scale(seeds[2], (TOKENS, 2), ((0, 32),), -0.2, 0.2)), 0.2, 1.0)
    w_gate = centred(seeds[3], (D, EXPERTS * HID), D ** -0.5, 0.09375, ((0, 2), (1, 16)))
    w_up = centred(seeds[4], (D, EXPERTS * HID), D ** -0.5, 0.09375, ((0, 2), (1, 16)))
    w_down = centred(seeds[5], (EXPERTS * HID, D), HID ** -0.5, 0.046875, ((0, 16), (1, 2)))
    target = centred(seeds[6], (TOKENS, D), 1.0, 6.0, ((0, 32),))
    return dict(tokens=tokens, expert_ids=expert_ids, gate_values=gate_values, w_gate=w_gate, w_up=w_up, w_down=w_down, target=target)


def slot_tables(expert_ids, gate_values):
    blocks = N_DP * N_EXPERT
    pair_count = 2 * TOK_DEV
    route_ids = expert_ids.reshape(blocks, pair_count).astype(jnp.int32)
    onehot = (route_ids[:, :, None] == jnp.arange(EXPERTS, dtype=jnp.int32)[None, None, :]).astype(jnp.int32)
    slot_index = jnp.sum((jnp.cumsum(onehot, axis=1) - onehot) * onehot, axis=2).astype(jnp.int32)
    window = route_ids < EXPERTS
    position = jnp.where(window, route_ids * CAP + slot_index, EXPERTS * CAP).astype(jnp.int32)
    block_index = jnp.arange(blocks, dtype=jnp.int32)[:, None]
    owning = (block_index * TOK_DEV + jnp.arange(pair_count, dtype=jnp.int32)[None, :] // 2).astype(jnp.int32)
    table_width = EXPERTS * CAP + 1
    slot_token = jnp.zeros((blocks, table_width), jnp.int32).at[block_index, position].set(owning)[:, :-1]
    slot_live = jnp.zeros((blocks, table_width), jnp.float32).at[block_index, position].set(1.0)[:, :-1]
    slot_gate = jnp.zeros((blocks, table_width), jnp.float32).at[block_index, position].set(
        gate_values.astype(jnp.float32).reshape(blocks, pair_count))[:, :-1]
    return route_ids, window, position, slot_token, slot_live, slot_gate


def by_receiver(table):
    shaped = table.reshape(N_DP, N_EXPERT, EXPERTS, CAP)
    return jnp.transpose(shaped, (0, 2, 1, 3)).reshape(N_DP, EXPERTS, N_EXPERT * CAP)


def reference(tokens, expert_ids, gate_values, w_gate, w_up, w_down, target):
    route_ids, window, position, slot_token, slot_live, slot_gate = slot_tables(expert_ids, gate_values)
    recv_token = by_receiver(slot_token)
    recv_live = by_receiver(slot_live)
    recv_gate = by_receiver(slot_gate)
    rows_count = N_EXPERT * CAP
    hid_local = HID // GROUP

    def rows_for(dp_index, expert_index):
        token_index = recv_token[dp_index, expert_index]
        live_mask = recv_live[dp_index, expert_index]
        return jnp.where(live_mask[:, None] > 0, tokens[token_index], jnp.zeros((), tokens.dtype))

    def slices(expert_index, slice_index):
        column_start = (expert_index * HID + slice_index * hid_local).astype(jnp.int32)
        gate_slice = lax.dynamic_slice_in_dim(w_gate, column_start, hid_local, 1)
        up_slice = lax.dynamic_slice_in_dim(w_up, column_start, hid_local, 1)
        down_slice = lax.dynamic_slice_in_dim(w_down, column_start, hid_local, 0)
        return gate_slice, up_slice, down_slice

    def forward_item(item_index):
        dp_index = item_index // EXPERTS
        expert_index = item_index % EXPERTS
        rows_in = rows_for(dp_index, expert_index)

        def slice_step(running, slice_index):
            gate_slice, up_slice, down_slice = slices(expert_index, slice_index)
            gate_pre = jnp.dot(rows_in, gate_slice, preferred_element_type=jnp.float32)
            up_pre = jnp.dot(rows_in, up_slice, preferred_element_type=jnp.float32)
            hidden = (jax.nn.sigmoid(gate_pre) * gate_pre * up_pre).astype(jnp.bfloat16)
            partial_value = jnp.dot(hidden, down_slice, preferred_element_type=jnp.float32).astype(jnp.bfloat16)
            return running + partial_value.astype(jnp.float32), None

        running, _ = lax.scan(slice_step, jnp.zeros((rows_count, D), jnp.float32), jnp.arange(GROUP, dtype=jnp.int32))
        return running

    outputs_all = lax.map(forward_item, jnp.arange(N_DP * EXPERTS, dtype=jnp.int32))
    blocks = N_DP * N_EXPERT
    block_index = jnp.arange(blocks, dtype=jnp.int32)[:, None]
    dp_of = block_index // N_EXPERT
    source = block_index % N_EXPERT
    safe_ids = jnp.where(window, route_ids, 0).astype(jnp.int32)
    slot_part = (jnp.where(window, position, 0) % CAP).astype(jnp.int32)
    fwd_rows = ((dp_of * EXPERTS + safe_ids) * rows_count + source * CAP + slot_part).reshape(TOKENS, 2).astype(jnp.int32)
    bwd_rows = ((safe_ids * N_DP + dp_of) * rows_count + source * CAP + slot_part).reshape(TOKENS, 2).astype(jnp.int32)
    live_pair = window.reshape(TOKENS, 2)
    flat_out = outputs_all.reshape(-1, D)
    gate_f = gate_values.astype(jnp.float32)
    first_pick = jnp.where(live_pair[:, 0:1], flat_out[fwd_rows[:, 0]], 0.0)
    second_pick = jnp.where(live_pair[:, 1:2], flat_out[fwd_rows[:, 1]], 0.0)
    combined = gate_f[:, 0:1] * first_pick + gate_f[:, 1:2] * second_pick
    residual = combined - target.astype(jnp.float32)

    def backward_expert(expert_index):
        def dp_step(accumulated, dp_index):
            gate_acc, up_acc = accumulated
            rows_in = rows_for(dp_index, expert_index)
            token_index = recv_token[dp_index, expert_index]
            live_mask = recv_live[dp_index, expert_index]
            gate_row = recv_gate[dp_index, expert_index]
            cotangent = jnp.where(live_mask[:, None] > 0, gate_row[:, None] * residual[token_index], 0.0).astype(jnp.bfloat16)

            def slice_step(carry, slice_index):
                row_acc, gate_inner, up_inner = carry
                gate_slice, up_slice, down_slice = slices(expert_index, slice_index)
                gate_pre = jnp.dot(rows_in, gate_slice, preferred_element_type=jnp.float32)
                up_pre = jnp.dot(rows_in, up_slice, preferred_element_type=jnp.float32)
                sigmoid_gate = jax.nn.sigmoid(gate_pre)
                activated = sigmoid_gate * gate_pre
                grad_hidden = jnp.dot(cotangent, down_slice.T, preferred_element_type=jnp.float32)
                derivative = sigmoid_gate * (1.0 + gate_pre * (1.0 - sigmoid_gate))
                grad_gate_pre = (grad_hidden * up_pre * derivative).astype(jnp.bfloat16)
                grad_up_pre = (grad_hidden * activated).astype(jnp.bfloat16)
                row_part = (jnp.dot(grad_gate_pre, gate_slice.T, preferred_element_type=jnp.float32)
                            + jnp.dot(grad_up_pre, up_slice.T, preferred_element_type=jnp.float32)).astype(jnp.bfloat16)
                gate_term = lax.optimization_barrier(jnp.dot(rows_in.T, grad_gate_pre, preferred_element_type=jnp.float32).astype(jnp.bfloat16))
                up_term = lax.optimization_barrier(jnp.dot(rows_in.T, grad_up_pre, preferred_element_type=jnp.float32).astype(jnp.bfloat16))
                column = (slice_index * hid_local).astype(jnp.int32)
                gate_inner = lax.dynamic_update_slice_in_dim(
                    gate_inner, lax.dynamic_slice_in_dim(gate_inner, column, hid_local, 1) + gate_term.astype(jnp.float32), column, 1)
                up_inner = lax.dynamic_update_slice_in_dim(
                    up_inner, lax.dynamic_slice_in_dim(up_inner, column, hid_local, 1) + up_term.astype(jnp.float32), column, 1)
                return (row_acc + row_part.astype(jnp.float32), gate_inner, up_inner), None

            start_rows = jnp.zeros((rows_count, D), jnp.float32)
            (row_acc, gate_acc, up_acc), _ = lax.scan(slice_step, (start_rows, gate_acc, up_acc), jnp.arange(GROUP, dtype=jnp.int32))
            return (gate_acc, up_acc), row_acc

        start_grads = (jnp.zeros((D, HID), jnp.float32), jnp.zeros((D, HID), jnp.float32))
        (gate_acc, up_acc), row_sums = lax.scan(dp_step, start_grads, jnp.arange(N_DP, dtype=jnp.int32))
        return gate_acc, up_acc, row_sums

    gate_all, up_all, row_all = lax.map(backward_expert, jnp.arange(EXPERTS, dtype=jnp.int32))
    flat_rows = row_all.reshape(-1, D)
    first_grad = jnp.where(live_pair[:, 0:1], flat_rows[bwd_rows[:, 0]], 0.0)
    second_grad = jnp.where(live_pair[:, 1:2], flat_rows[bwd_rows[:, 1]], 0.0)
    token_grad = (first_grad + second_grad).astype(jnp.bfloat16)
    gate_grad = jnp.transpose(gate_all, (1, 0, 2)).reshape(D, EXPERTS * HID).astype(jnp.bfloat16)
    up_grad = jnp.transpose(up_all, (1, 0, 2)).reshape(D, EXPERTS * HID).astype(jnp.bfloat16)
    return (token_grad, gate_grad, up_grad)
```

```python
import functools

import jax
import jax.numpy as jnp
from jax import lax
from jax.experimental import pallas as pl
from jax.experimental.pallas import tpu as pltpu
from jax.sharding import PartitionSpec as P

EXPERTS = 1
LANES = 128
GATE_PIECES = 3
BF = jnp.bfloat16
F32 = jnp.float32
VMEM = pl.BlockSpec(memory_space=pltpu.VMEM)
SMEM = pl.BlockSpec(memory_space=pltpu.SMEM)


def sds(shape, dtype):
    return jax.ShapeDtypeStruct(shape, dtype)


def dot_nn(a, b):
    return lax.dot_general(a, b, (((1,), (0,)), ((), ())), preferred_element_type=F32)


def dot_nt(a, b):
    return lax.dot_general(a, b, (((1,), (1,)), ((), ())), preferred_element_type=F32)


def dot_tn(a, b):
    return lax.dot_general(a, b, (((0,), (0,)), ((), ())), preferred_element_type=F32)


def call(body, outs, args, specs, scratch=(), limit=16, flops=0, moved=0, name=None):
    return pl.pallas_call(
        body,
        out_shape=outs,
        in_specs=specs,
        out_specs=jax.tree.map(lambda _: VMEM, outs),
        scratch_shapes=list(scratch),
        compiler_params=pltpu.CompilerParams(vmem_limit_bytes=limit << 20),
        cost_estimate=pl.CostEstimate(flops=flops, bytes_accessed=moved, transcendentals=0),
        name=name,
    )(*args)


def select_rows(ids_ref):
    tok_rows = ids_ref.shape[1]
    live = jnp.sum((ids_ref[...] < EXPERTS).astype(F32), axis=0, keepdims=True)
    before = lax.broadcasted_iota(jnp.int32, (tok_rows, tok_rows), 0)
    after = lax.broadcasted_iota(jnp.int32, (tok_rows, tok_rows), 1)
    earlier = (before < after).astype(BF)
    wide = jnp.broadcast_to(live, (16, tok_rows))
    slot = dot_nn(wide.astype(BF), earlier)
    wanted = lax.broadcasted_iota(jnp.int32, (16, tok_rows), 0).astype(F32)
    return jnp.where(slot == wanted, wide, 0.0)


def route_kernel(dims, ids_ref, gates_ref, tokens_ref, target_ref, out_ref, tok, tgt, head, tail):
    n_dp, half, cap, blocks, unit = dims
    chosen = select_rows(ids_ref)
    live_gates = jnp.sum(jnp.where(ids_ref[...] < EXPERTS, gates_ref[...], 0.0), axis=0, keepdims=True)
    gate = jnp.sum(chosen * live_gates, axis=1, keepdims=True)
    pick = chosen.astype(BF)
    tok[...] = dot_nn(pick, tokens_ref[...])
    tgt[...] = dot_nn(pick, target_ref[...])
    tail[...] = jnp.zeros_like(tail)
    rest = gate
    for piece in range(GATE_PIECES):
        part = rest.astype(BF).astype(F32)
        rest = rest - part
        at = (2 + piece) * cap
        tail[at : at + cap, :] = jnp.broadcast_to(part[0:cap], (cap, LANES))
    width = blocks * LANES
    for d in range(n_dp):
        for q in range(blocks):
            lo = d * width + q * LANES
            head[q * cap : (q + 1) * cap, :] = tok[0:cap, lo : lo + LANES]
        packed = head[...].astype(BF)
        for h in range(half):
            for core in range(2):
                lo = d * width + (core * half + h) * LANES
                tail[core * cap : (core + 1) * cap, :] = tgt[0:cap, lo : lo + LANES]
            base = (d * half + h) * unit
            out_ref[base : base + blocks * cap, :] = packed
            out_ref[base + blocks * cap : base + unit, :] = tail[...].astype(BF)


def both_cores(core_ref, own_ref, other_ref, wide):
    size = own_ref.shape[0]
    core = core_ref[0]
    wide[pl.ds(pl.multiple_of(core * size, size), size), :] = own_ref[...].astype(wide.dtype)
    wide[pl.ds(pl.multiple_of((1 - core) * size, size), size), :] = other_ref[...].astype(wide.dtype)


def pre_kernel(dims, core_ref, own_ref, other_ref, gate_w, up_w,
               rows_ref, target_ref, gates_ref, own_pre, send_pre, wide):
    n_dp, half, cap, blocks, unit = dims
    sources = 2 * n_dp * half
    both_cores(core_ref, own_ref, other_ref, wide)
    core = core_ref[0]

    def one(k):
        return wide[pl.ds(k, sources, stride=unit), :]

    for c in range(cap):
        rows = slice(c * sources, (c + 1) * sources)
        for q in range(blocks):
            rows_ref[rows, q * LANES : (q + 1) * LANES] = one(q * cap + c).astype(BF)
        base = blocks * cap
        target_ref[rows, :] = jnp.where(core == 0, one(base + c), one(base + cap + c))
        gates_ref[rows, :] = sum(one(base + (2 + piece) * cap + c) for piece in range(GATE_PIECES))
    hid = gate_w.shape[1]

    def column(j, _):
        cols = pl.ds(pl.multiple_of(j * LANES, LANES), LANES)
        pair = jnp.concatenate([gate_w[:, cols], up_w[:, cols]], axis=1)
        both = dot_nn(rows_ref[...], pair)
        for side in range(2):
            value = both[:, side * LANES : (side + 1) * LANES]
            own_pre[side, :, cols] = value
            send_pre[side, :, cols] = value.astype(BF)
        return 0

    lax.fori_loop(0, hid // LANES, column, 0)


def down_kernel(dims, core_ref, own_ref, got_ref, down_w, up_deriv, act_ref, keep_ref, send_ref, hidden):
    n_dp, half, cap, blocks, unit = dims
    gate_pre = own_ref[0] + got_ref[0].astype(F32)
    up_pre = own_ref[1] + got_ref[1].astype(F32)
    sig = jax.nn.sigmoid(gate_pre)
    act = sig * gate_pre
    act_ref[...] = act
    up_deriv[...] = up_pre * (sig * (1.0 + gate_pre * (1.0 - sig)))
    hidden[...] = (act * up_pre).astype(BF)
    rows = hidden.shape[0]
    core = core_ref[0]
    for side, ref in ((core, keep_ref), (1 - core, send_ref)):

        def column(j, _, side=side, ref=ref):
            start = (side * half + 2 * j) * LANES
            cols = pl.ds(pl.multiple_of(start, 2 * LANES), 2 * LANES)
            value = dot_nn(hidden[...], down_w[:, cols]).astype(ref.dtype)
            for k in range(2):
                base = pl.multiple_of((2 * j + k) * rows, rows)
                ref[pl.ds(base, rows), :] = value[:, k * LANES : (k + 1) * LANES]
            return 0

        lax.fori_loop(0, half // 2, column, 0)


def cotangent_kernel(parts, got_ref, gates_ref, target_ref, out_ref):
    rows = target_ref.shape[0]
    total = got_ref[0:rows, :].astype(F32)
    for h in range(1, parts):
        total = total + got_ref[h * rows : (h + 1) * rows, :].astype(F32)
    gate = gates_ref[...]
    value = (gate * (gate * total - target_ref[...])).astype(BF)
    for h in range(parts):
        out_ref[h * rows : (h + 1) * rows, :] = value


def grad_hidden_kernel(rows, core_ref, own_ref, other_ref, down_w, own_out, send_out, cot):
    size = own_ref.shape[0]
    core = core_ref[0]
    for ref, side in ((own_ref, core), (other_ref, 1 - core)):
        for h in range(size // rows):
            start = (side * (size // rows) + h) * LANES
            cot[:, pl.ds(pl.multiple_of(start, LANES), LANES)] = ref[h * rows : (h + 1) * rows, :]
    hid = down_w.shape[0]

    def column(j, _):
        cols = pl.ds(pl.multiple_of(j * LANES, LANES), LANES)
        value = dot_nt(cot[...], down_w[cols, :])
        own_out[:, cols] = value
        send_out[:, cols] = value.astype(BF)
        return 0

    lax.fori_loop(0, hid // LANES, column, 0)


def row_grad_kernel(dims, core_ref, own_ref, got_ref, up_deriv, act_ref, gate_w, up_w,
                    gate_out, up_out, keep_ref, send_ref, wide):
    n_dp, half, cap, blocks, unit = dims
    sources = 2 * n_dp * half
    grad_hidden = own_ref[...] + got_ref[...].astype(F32)
    gate_out[...] = (grad_hidden * up_deriv[...]).astype(BF)
    up_out[...] = (grad_hidden * act_ref[...]).astype(BF)

    def column(j, _):
        at = pl.ds(pl.multiple_of(j * 2 * LANES, 2 * LANES), 2 * LANES)
        value = dot_nt(gate_out[...], gate_w[at, :]) + dot_nt(up_out[...], up_w[at, :])
        for k in range(2):
            for c in range(cap):
                piece = value[c * sources : (c + 1) * sources, k * LANES : (k + 1) * LANES]
                wide[pl.ds((2 * j + k) * cap + c, sources, stride=blocks * cap), :] = piece
        return 0

    lax.fori_loop(0, blocks // 2, column, 0)
    size = keep_ref.shape[0]
    core = core_ref[0]
    keep_ref[...] = wide[pl.ds(pl.multiple_of(core * size, size), size), :]
    send_ref[...] = wide[pl.ds(pl.multiple_of((1 - core) * size, size), size), :].astype(BF)


def weight_grad_kernel(rows_ref, gate_ref, up_ref, gate_out, up_out):
    gate_out[...] = dot_tn(rows_ref[...], gate_ref[...]).astype(BF)
    up_out[...] = dot_tn(rows_ref[...], up_ref[...]).astype(BF)


def token_grad_kernel(dims, ids_ref, got_ref, out_ref, rows):
    n_dp, half, cap, blocks, unit = dims
    size = blocks * cap
    rows[...] = jnp.zeros_like(rows)
    for d in range(n_dp):
        total = got_ref[d * half * size : (d * half + 1) * size, :].astype(F32)
        for h in range(1, half):
            base = (d * half + h) * size
            total = total + got_ref[base : base + size, :].astype(F32)
        for q in range(blocks):
            lo = (d * blocks + q) * LANES
            rows[0:cap, lo : lo + LANES] = total[q * cap : (q + 1) * cap, :]
    pick = select_rows(ids_ref).astype(BF)
    out_ref[...] = dot_tn(pick, rows[...].astype(BF)).astype(out_ref.dtype)


def fast_shards(n_dp, n_expert, cap, tokens, expert_ids, gate_values, w_gate, w_up, w_down, target):
    tok_rows, features = tokens.shape
    width, hid = w_gate.shape
    half = n_expert // 2
    blocks = width // LANES
    peers = n_dp * half
    sources = 2 * peers
    rows = cap * sources
    unit = -(-(blocks + 2 + GATE_PIECES) * cap // 16) * 16
    dims = (n_dp, half, cap, blocks, unit)
    core = (lax.axis_index("expert") % 2).astype(jnp.int32).reshape(1)
    ids = expert_ids.T
    plane = [[2 * h + c for h in range(half)] for c in range(2)]
    slice_groups = [
        [d * n_expert + 2 * h + c for d in range(n_dp) for h in range(half)] for c in range(2)
    ]

    def other_core(x):
        return lax.ppermute(x, "expert", [(i, i ^ 1) for i in range(n_expert)])

    def other_dp(x):
        return lax.ppermute(x, "dp", [(0, 1), (1, 0)])

    def over_plane(x):
        return lax.all_to_all(x, "expert", 0, 0, axis_index_groups=plane, tiled=True)

    def over_slice(x):
        return lax.all_to_all(x, ("dp", "expert"), 0, 0, axis_index_groups=slice_groups, tiled=True)

    outgoing = call(
        functools.partial(route_kernel, dims),
        sds((peers * unit, LANES), BF),
        (ids, gate_values.T, tokens, target),
        [VMEM] * 4,
        [
            pltpu.VMEM((16, features), F32),
            pltpu.VMEM((16, features), F32),
            pltpu.VMEM((blocks * cap, LANES), F32),
            pltpu.VMEM((unit - blocks * cap, LANES), F32),
        ],
        name="route",
    )
    own = over_slice(outgoing)
    other = other_core(own)
    all_rows, all_target, all_gates, own_pre, send_pre = call(
        functools.partial(pre_kernel, dims),
        (
            sds((rows, width), BF),
            sds((rows, LANES), F32),
            sds((rows, LANES), F32),
            sds((2, rows, hid), F32),
            sds((2, rows, hid), BF),
        ),
        (core, own, other, w_gate, w_up),
        [SMEM] + [VMEM] * 4,
        [pltpu.VMEM((sources * unit, LANES), F32)],
        name="pre_activations",
    )
    got_pre = other_dp(send_pre)
    up_deriv, act, keep, send = call(
        functools.partial(down_kernel, dims),
        (
            sds((rows, hid), F32),
            sds((rows, hid), F32),
            sds((half * rows, LANES), F32),
            sds((half * rows, LANES), BF),
        ),
        (core, own_pre, got_pre, w_down),
        [SMEM] + [VMEM] * 3,
        [pltpu.VMEM((rows, hid), BF)],
        name="down",
    )
    chip_out = (keep + other_core(send).astype(F32)).astype(BF)
    cot = call(
        functools.partial(cotangent_kernel, half),
        sds((half * rows, LANES), BF),
        (over_plane(chip_out), all_gates, all_target),
        [VMEM] * 3,
        name="cotangent",
    )
    own = over_plane(cot)
    other = other_core(own)
    own_gh, send_gh = call(
        functools.partial(grad_hidden_kernel, rows),
        (sds((rows, hid), F32), sds((rows, hid), BF)),
        (core, own, other, w_down),
        [SMEM] + [VMEM] * 3,
        [pltpu.VMEM((rows, width), BF)],
        name="grad_hidden",
    )
    got_gh = other_dp(send_gh)
    gate_pre_grad, up_pre_grad, keep, send = call(
        functools.partial(row_grad_kernel, dims),
        (
            sds((rows, hid), BF),
            sds((rows, hid), BF),
            sds((peers * blocks * cap, LANES), F32),
            sds((peers * blocks * cap, LANES), BF),
        ),
        (core, own_gh, got_gh, up_deriv, act, w_gate, w_up),
        [SMEM] + [VMEM] * 6,
        [pltpu.VMEM((sources * blocks * cap, LANES), F32)],
        name="row_grad",
    )
    chip_rows = (keep + other_core(send).astype(F32)).astype(BF)
    got_rows = over_slice(chip_rows)
    tile = 256
    gate_grad, up_grad = pl.pallas_call(
        weight_grad_kernel,
        out_shape=(sds((width, hid), BF), sds((width, hid), BF)),
        grid=(width // tile,),
        in_specs=[
            pl.BlockSpec((rows, tile), lambda i: (0, i)),
            pl.BlockSpec((rows, hid), lambda i: (0, 0)),
            pl.BlockSpec((rows, hid), lambda i: (0, 0)),
        ],
        out_specs=(pl.BlockSpec((tile, hid), lambda i: (i, 0)), pl.BlockSpec((tile, hid), lambda i: (i, 0))),
        compiler_params=pltpu.CompilerParams(vmem_limit_bytes=16 << 20),
        cost_estimate=pl.CostEstimate(
            flops=4 * rows * width * hid, bytes_accessed=4 * width * hid, transcendentals=0
        ),
        name="weight_grads",
    )(all_rows, gate_pre_grad, up_pre_grad)
    token_grad = call(
        functools.partial(token_grad_kernel, dims),
        sds((tok_rows, features), tokens.dtype),
        (ids, got_rows),
        [VMEM] * 2,
        [pltpu.VMEM((16, features), F32)],
        name="token_grad",
    )
    return token_grad, gate_grad, up_grad


def contract_last(matrix_a, matrix_b):
    return lax.dot_general(
        matrix_a, matrix_b, (((1,), (1,)), ((), ())), preferred_element_type=jnp.float32
    )


def rounded_terms(column_blocks, grad_blocks):
    terms = jnp.einsum(
        "krd,krh->kdh", column_blocks, grad_blocks, preferred_element_type=jnp.float32
    )
    terms = lax.optimization_barrier(terms.astype(jnp.bfloat16))
    return jnp.sum(terms.astype(jnp.float32), axis=0)


def spread_rows(rows, group_size, capacity, features):
    flat = rows.reshape(EXPERTS, 1, capacity * features)
    wide = jnp.broadcast_to(flat, (EXPERTS, group_size, capacity * features))
    return wide.reshape(EXPERTS * group_size * capacity, features)


def fold_group(rows, group_size, capacity, features):
    shaped = rows.reshape(EXPERTS, group_size, capacity * features).astype(jnp.float32)
    return jnp.sum(shaped, axis=1).reshape(EXPERTS * capacity, features)


def general_shards(tokens, expert_ids, gate_values, w_gate, w_up, w_down, target):
    devices_along = lax.axis_size("expert")
    group_size = devices_along // EXPERTS
    tok_rows = tokens.shape[0]
    features = tokens.shape[1]
    hid_local = w_gate.shape[1]
    capacity = max(2, 3 * tok_rows // 128)
    slot_total = EXPERTS * capacity
    flat_ids = expert_ids.reshape(-1)
    pair_count = flat_ids.shape[0]
    window = flat_ids < EXPERTS
    onehot = (flat_ids[:, None] == jnp.arange(EXPERTS, dtype=jnp.int32)[None, :]).astype(jnp.int32)
    slot_index = jnp.sum((jnp.cumsum(onehot, axis=0) - onehot) * onehot, axis=1)
    position = jnp.where(window, flat_ids * capacity + slot_index, slot_total)
    owning = jnp.arange(pair_count, dtype=jnp.int32) // 2
    slot_token = jnp.zeros((slot_total + 1,), jnp.int32).at[position].set(owning)[:slot_total]
    slot_live = jnp.zeros((slot_total + 1,), jnp.bool_).at[position].set(True)[:slot_total]
    slot_gate = (
        jnp.zeros((slot_total + 1,), jnp.float32)
        .at[position]
        .set(gate_values.reshape(-1))[:slot_total]
    )
    safe_pairs = jnp.minimum(position, slot_total - 1).reshape(tok_rows, 2)
    live_pairs = window.reshape(tok_rows, 2)

    def pick(table, column):
        return jnp.where(live_pairs[:, column : column + 1], table[safe_pairs[:, column]], 0.0)

    outgoing = jnp.where(slot_live[:, None], tokens[slot_token], jnp.zeros((), tokens.dtype))
    outgoing = spread_rows(outgoing, group_size, capacity, features)
    received = lax.all_to_all(outgoing, "expert", split_axis=0, concat_axis=0, tiled=True)
    rows_count = received.shape[0]
    full_gate, full_up, full_down = (
        lax.all_gather(w_gate, "dp", axis=0, tiled=True),
        lax.all_gather(w_up, "dp", axis=0, tiled=True),
        lax.all_gather(w_down, "dp", axis=1, tiled=True),
    )
    gate_pre = jnp.dot(received, full_gate, preferred_element_type=jnp.float32)
    up_pre = jnp.dot(received, full_up, preferred_element_type=jnp.float32)
    sigmoid_gate = jax.nn.sigmoid(gate_pre)
    activated = sigmoid_gate * gate_pre
    hidden = (activated * up_pre).astype(jnp.bfloat16)
    partial_out = jnp.dot(hidden, full_down, preferred_element_type=jnp.float32).astype(
        jnp.bfloat16
    )
    returned_out = lax.all_to_all(partial_out, "expert", split_axis=0, concat_axis=0, tiled=True)
    expert_out = fold_group(returned_out, group_size, capacity, features)
    combined = gate_values[:, 0:1] * pick(expert_out, 0) + gate_values[:, 1:2] * pick(expert_out, 1)
    residual = combined - target.astype(jnp.float32)
    outgoing_grad = jnp.where(
        slot_live[:, None], slot_gate[:, None] * residual[slot_token], 0.0
    ).astype(jnp.bfloat16)
    outgoing_grad = spread_rows(outgoing_grad, group_size, capacity, features)
    cotangent = lax.all_to_all(outgoing_grad, "expert", split_axis=0, concat_axis=0, tiled=True)
    grad_hidden = contract_last(cotangent, full_down)
    derivative = sigmoid_gate * (1.0 + gate_pre * (1.0 - sigmoid_gate))
    grad_gate_pre = (grad_hidden * up_pre * derivative).astype(jnp.bfloat16)
    grad_up_pre = (grad_hidden * activated).astype(jnp.bfloat16)
    row_part = (
        contract_last(grad_gate_pre, full_gate) + contract_last(grad_up_pre, full_up)
    ).astype(jnp.bfloat16)
    back_rows = lax.all_to_all(row_part, "expert", split_axis=0, concat_axis=0, tiled=True)
    row_grad = fold_group(back_rows, group_size, capacity, features)
    token_grad = (pick(row_grad, 0) + pick(row_grad, 1)).astype(jnp.bfloat16)
    shard_columns = lax.all_to_all(received, "dp", split_axis=1, concat_axis=0, tiled=True)
    shard_width = shard_columns.shape[1]
    dp_count = lax.axis_size("dp")
    every_gate, every_up = (
        lax.all_gather(grad_gate_pre, "dp", axis=0, tiled=True),
        lax.all_gather(grad_up_pre, "dp", axis=0, tiled=True),
    )
    column_blocks = shard_columns.reshape(dp_count, rows_count, shard_width)
    gate_sum = rounded_terms(column_blocks, every_gate.reshape(dp_count, rows_count, hid_local))
    up_sum = rounded_terms(column_blocks, every_up.reshape(dp_count, rows_count, hid_local))
    return (token_grad, gate_sum.astype(jnp.bfloat16), up_sum.astype(jnp.bfloat16))


def solution(mesh):
    n_dp, n_expert = mesh.shape["dp"], mesh.shape["expert"]

    def shards(*args):
        tok_rows, features = args[0].shape
        width, hid = args[3].shape
        cap = max(2, 3 * tok_rows // 128)
        whole_blocks = (
            n_dp == 2
            and n_expert % 4 == 0
            and width == n_expert * LANES
            and hid % LANES == 0
            and n_dp * n_expert % 16 == 0
            and cap <= 8
            and tok_rows % LANES == 0
        )
        if whole_blocks:
            return fast_shards(n_dp, n_expert, cap, *args)
        return general_shards(*args)

    placed = (
        P(("dp", "expert"), None),
        P(("dp", "expert"), None),
        P(("dp", "expert"), None),
        P("dp", "expert"),
        P("dp", "expert"),
        P("expert", "dp"),
        P(("dp", "expert"), None),
    )
    return jax.shard_map(
        shards,
        mesh=mesh,
        in_specs=placed,
        out_specs=(P(("dp", "expert"), None), P("dp", "expert"), P("dp", "expert")),
        check_vma=False,
    )
```

```python
import functools

import jax
import jax.numpy as jnp
from jax import lax
from jax.experimental import pallas as pl
from jax.experimental.pallas import tpu as pltpu
from jax.sharding import PartitionSpec as P

EXPERTS = 1
LANES = 128
GATE_PIECES = 3
BF = jnp.bfloat16
F32 = jnp.float32
VMEM = pl.BlockSpec(memory_space=pltpu.VMEM)
HBM = pl.BlockSpec(memory_space=pltpu.HBM)
SMEM = pl.BlockSpec(memory_space=pltpu.SMEM)


def sds(shape, dtype):
    return jax.ShapeDtypeStruct(shape, dtype)


def dot_nn(a, b):
    return lax.dot_general(a, b, (((1,), (0,)), ((), ())), preferred_element_type=F32)


def dot_nt(a, b):
    return lax.dot_general(a, b, (((1,), (1,)), ((), ())), preferred_element_type=F32)


def dot_tn(a, b):
    return lax.dot_general(a, b, (((0,), (0,)), ((), ())), preferred_element_type=F32)


def call(body, outs, args, specs, scratch=(), limit=16, flops=0, moved=0, name=None):
    return pl.pallas_call(
        body,
        out_shape=outs,
        in_specs=specs,
        out_specs=jax.tree.map(lambda _: VMEM, outs),
        scratch_shapes=list(scratch),
        compiler_params=pltpu.CompilerParams(vmem_limit_bytes=limit << 20),
        cost_estimate=pl.CostEstimate(flops=flops, bytes_accessed=moved, transcendentals=0),
        name=name,
    )(*args)


def select_rows(ids_ref):
    tok_rows = ids_ref.shape[1]
    live = jnp.sum((ids_ref[...] < EXPERTS).astype(F32), axis=0, keepdims=True)
    before = lax.broadcasted_iota(jnp.int32, (tok_rows, tok_rows), 0)
    after = lax.broadcasted_iota(jnp.int32, (tok_rows, tok_rows), 1)
    earlier = (before < after).astype(BF)
    wide = jnp.broadcast_to(live, (16, tok_rows))
    slot = dot_nn(wide.astype(BF), earlier)
    wanted = lax.broadcasted_iota(jnp.int32, (16, tok_rows), 0).astype(F32)
    return jnp.where(slot == wanted, wide, 0.0)


def route_kernel(dims, ids_hbm, gates_hbm, tokens_hbm, target_hbm, out_ref,
                 ids_ref, gates_ref, tokens_ref, target_ref, tok, tgt, head, tail, sems):
    n_dp, half, cap, blocks, unit = dims
    pairs = (
        (ids_hbm, ids_ref),
        (gates_hbm, gates_ref),
        (tokens_hbm, tokens_ref),
        (target_hbm, target_ref),
    )
    copies = [pltpu.make_async_copy(src, dst, sems.at[i]) for i, (src, dst) in enumerate(pairs)]
    for copy in copies:
        copy.start()
    tail[...] = jnp.zeros_like(tail)
    copies[0].wait()
    copies[1].wait()
    chosen = select_rows(ids_ref)
    live_gates = jnp.sum(jnp.where(ids_ref[...] < EXPERTS, gates_ref[...], 0.0), axis=0, keepdims=True)
    gate = jnp.sum(chosen * live_gates, axis=1, keepdims=True)
    pick = chosen.astype(BF)
    copies[2].wait()
    tok[...] = dot_nn(pick, tokens_ref[...])
    copies[3].wait()
    tgt[...] = dot_nn(pick, target_ref[...])
    rest = gate
    for piece in range(GATE_PIECES):
        part = rest.astype(BF).astype(F32)
        rest = rest - part
        at = (2 + piece) * cap
        tail[at : at + cap, :] = jnp.broadcast_to(part[0:cap], (cap, LANES))
    width = blocks * LANES
    for d in range(n_dp):
        for q in range(blocks):
            lo = d * width + q * LANES
            head[q * cap : (q + 1) * cap, :] = tok[0:cap, lo : lo + LANES]
        packed = head[...].astype(BF)
        for h in range(half):
            for core in range(2):
                lo = d * width + (core * half + h) * LANES
                tail[core * cap : (core + 1) * cap, :] = tgt[0:cap, lo : lo + LANES]
            base = (d * half + h) * unit
            out_ref[base : base + blocks * cap, :] = packed
            out_ref[base + blocks * cap : base + unit, :] = tail[...].astype(BF)


def both_cores(core_ref, own_ref, other_ref, wide):
    size = own_ref.shape[0]
    core = core_ref[0]
    wide[pl.ds(pl.multiple_of(core * size, size), size), :] = own_ref[...].astype(wide.dtype)
    wide[pl.ds(pl.multiple_of((1 - core) * size, size), size), :] = other_ref[...].astype(wide.dtype)


def partial_pre(rows_ref, gate_w, up_w, start, own_pre, send_pre):
    def column(j, _):
        cols = pl.ds(pl.multiple_of(j * LANES, LANES), LANES)
        at = pl.ds(pl.multiple_of(start + j * LANES, LANES), LANES)
        pair = jnp.concatenate([gate_w[:, at], up_w[:, at]], axis=1)
        both = dot_nn(rows_ref[...], pair)
        for side in range(2):
            value = both[:, side * LANES : (side + 1) * LANES]
            own_pre[side, :, cols] = value
            send_pre[side, :, cols] = value.astype(BF)
        return 0

    lax.fori_loop(0, own_pre.shape[2] // LANES, column, 0)


def first_pre_kernel(dims, size, core_ref, own_ref, other_ref, gate_hbm, up_hbm,
                     rows_ref, target_ref, gates_ref, gate_w, up_w, own_pre, send_pre, wide, sems):
    n_dp, half, cap, blocks, unit = dims
    sources = 2 * n_dp * half
    hid = gate_w.shape[1]
    copies = []
    for k, cols in enumerate((pl.ds(0, size), pl.ds(size, hid - size))):
        for side, (src, dst) in enumerate(((gate_hbm, gate_w), (up_hbm, up_w))):
            copies.append(pltpu.make_async_copy(src.at[:, cols], dst.at[:, cols], sems.at[k, side]))
    for copy in copies:
        copy.start()
    both_cores(core_ref, own_ref, other_ref, wide)
    core = core_ref[0]

    def one(k):
        return wide[pl.ds(k, sources, stride=unit), :]

    for c in range(cap):
        rows = slice(c * sources, (c + 1) * sources)
        for q in range(blocks):
            rows_ref[rows, q * LANES : (q + 1) * LANES] = one(q * cap + c).astype(BF)
        base = blocks * cap
        target_ref[rows, :] = jnp.where(core == 0, one(base + c), one(base + cap + c))
        gates_ref[rows, :] = sum(one(base + (2 + piece) * cap + c) for piece in range(GATE_PIECES))
    copies[0].wait()
    copies[1].wait()
    partial_pre(rows_ref, gate_w, up_w, 0, own_pre, send_pre)
    copies[2].wait()
    copies[3].wait()


def more_pre_kernel(start, rows_ref, gate_w, up_w, own_pre, send_pre):
    partial_pre(rows_ref, gate_w, up_w, start, own_pre, send_pre)


def down_kernel(dims, start, last, core_ref, own_ref, got_ref, down_w, *refs):
    n_dp, half, cap, blocks, unit = dims
    refs = list(refs)
    total_ref = refs.pop(0) if start > 0 else None
    up_deriv, act_ref, *out_refs, hidden = refs
    gate_pre = own_ref[0] + got_ref[0].astype(F32)
    up_pre = own_ref[1] + got_ref[1].astype(F32)
    sig = jax.nn.sigmoid(gate_pre)
    act = sig * gate_pre
    act_ref[...] = act
    up_deriv[...] = up_pre * (sig * (1.0 + gate_pre * (1.0 - sig)))
    hidden[...] = (act * up_pre).astype(BF)
    rows, hid = hidden.shape
    core = core_ref[0]
    for side in range(2):

        def column(j, _, side=side):
            shown = core if side == 0 else 1 - core
            lo = (shown * half + 2 * j) * LANES
            cols = pl.ds(pl.multiple_of(lo, 2 * LANES), 2 * LANES)
            value = dot_nn(hidden[...], down_w[start : start + hid, cols])
            for k in range(2):
                part = value[:, k * LANES : (k + 1) * LANES]
                mine = pl.ds(pl.multiple_of((2 * j + k) * rows, rows), rows)
                both = pl.ds(pl.multiple_of((side * half + 2 * j + k) * rows, rows), rows)
                if total_ref is not None:
                    part = part + total_ref[both, :]
                if last:
                    out_refs[side][mine, :] = part.astype(out_refs[side].dtype)
                else:
                    out_refs[0][both, :] = part
            return 0

        lax.fori_loop(0, half // 2, column, 0)


def cotangent_kernel(parts, got_ref, gates_ref, target_ref, out_ref):
    rows = target_ref.shape[0]
    total = got_ref[0:rows, :].astype(F32)
    for h in range(1, parts):
        total = total + got_ref[h * rows : (h + 1) * rows, :].astype(F32)
    gate = gates_ref[...]
    value = (gate * (gate * total - target_ref[...])).astype(BF)
    for h in range(parts):
        out_ref[h * rows : (h + 1) * rows, :] = value


def partial_grad_hidden(cot, down_w, start, own_out, send_out):
    def column(j, _):
        cols = pl.ds(pl.multiple_of(j * LANES, LANES), LANES)
        at = pl.ds(pl.multiple_of(start + j * LANES, LANES), LANES)
        value = dot_nt(cot[...], down_w[at, :])
        own_out[:, cols] = value
        send_out[:, cols] = value.astype(BF)
        return 0

    lax.fori_loop(0, own_out.shape[1] // LANES, column, 0)


def first_grad_hidden_kernel(start, core_ref, own_ref, other_ref, down_w, cot, own_out, send_out):
    rows = cot.shape[0]
    parts = own_ref.shape[0] // rows
    core = core_ref[0]
    for ref, side in ((own_ref, core), (other_ref, 1 - core)):
        for h in range(parts):
            lo = (side * parts + h) * LANES
            cot[:, pl.ds(pl.multiple_of(lo, LANES), LANES)] = ref[h * rows : (h + 1) * rows, :]
    partial_grad_hidden(cot, down_w, start, own_out, send_out)


def more_grad_hidden_kernel(start, cot, down_w, own_out, send_out):
    partial_grad_hidden(cot, down_w, start, own_out, send_out)


def row_grad_kernel(dims, start, last, core_ref, own_ref, got_ref, up_deriv, act_ref, gate_w, up_w, *refs):
    n_dp, half, cap, blocks, unit = dims
    sources = 2 * n_dp * half
    refs = list(refs)
    total_ref = refs.pop(0) if start > 0 else None
    gate_out, up_out, *out_refs = refs
    grad_hidden = own_ref[...] + got_ref[...].astype(F32)
    gate_out[...] = (grad_hidden * up_deriv[...]).astype(BF)
    up_out[...] = (grad_hidden * act_ref[...]).astype(BF)
    hid = gate_out.shape[1]
    wide = out_refs[-1]

    def column(j, _):
        at = pl.ds(pl.multiple_of(j * 2 * LANES, 2 * LANES), 2 * LANES)
        value = dot_nt(gate_out[...], gate_w[at, start : start + hid])
        value = value + dot_nt(up_out[...], up_w[at, start : start + hid])
        if total_ref is not None:
            value = value + total_ref[:, at]
        if not last:
            wide[:, at] = value
            return 0
        for k in range(2):
            for c in range(cap):
                piece = value[c * sources : (c + 1) * sources, k * LANES : (k + 1) * LANES]
                wide[pl.ds((2 * j + k) * cap + c, sources, stride=blocks * cap), :] = piece
        return 0

    lax.fori_loop(0, blocks // 2, column, 0)
    if last:
        keep_ref, send_ref, _ = out_refs
        size = keep_ref.shape[0]
        core = core_ref[0]
        keep_ref[...] = wide[pl.ds(pl.multiple_of(core * size, size), size), :]
        send_ref[...] = wide[pl.ds(pl.multiple_of((1 - core) * size, size), size), :].astype(BF)


def weight_grad_kernel(parts, rows_ref, *refs):
    gate_out, up_out = refs[-2:]
    rows = rows_ref[...]
    lo = 0
    for k in range(parts):
        size = refs[k].shape[1]
        gate_out[:, lo : lo + size] = dot_tn(rows, refs[k][...]).astype(BF)
        up_out[:, lo : lo + size] = dot_tn(rows, refs[parts + k][...]).astype(BF)
        lo += size


def token_grad_kernel(dims, ids_ref, got_ref, out_ref, rows):
    n_dp, half, cap, blocks, unit = dims
    size = blocks * cap
    rows[...] = jnp.zeros_like(rows)
    for d in range(n_dp):
        total = got_ref[d * half * size : (d * half + 1) * size, :].astype(F32)
        for h in range(1, half):
            base = (d * half + h) * size
            total = total + got_ref[base : base + size, :].astype(F32)
        for q in range(blocks):
            lo = (d * blocks + q) * LANES
            rows[0:cap, lo : lo + LANES] = total[q * cap : (q + 1) * cap, :]
    pick = select_rows(ids_ref).astype(BF)
    out_ref[...] = dot_tn(pick, rows[...].astype(BF)).astype(out_ref.dtype)


def fast_shards(n_dp, n_expert, cap, tokens, expert_ids, gate_values, w_gate, w_up, w_down, target):
    tok_rows, features = tokens.shape
    width, hid = w_gate.shape
    half = n_expert // 2
    blocks = width // LANES
    peers = n_dp * half
    sources = 2 * peers
    rows = cap * sources
    unit = -(-(blocks + 2 + GATE_PIECES) * cap // 16) * 16
    dims = (n_dp, half, cap, blocks, unit)
    core = (lax.axis_index("expert") % 2).astype(jnp.int32).reshape(1)
    ids = expert_ids.T
    plane = [[2 * h + c for h in range(half)] for c in range(2)]
    slice_groups = [
        [d * n_expert + 2 * h + c for d in range(n_dp) for h in range(half)] for c in range(2)
    ]

    def other_core(x):
        return lax.ppermute(x, "expert", [(i, i ^ 1) for i in range(n_expert)])

    def other_dp(x):
        return lax.ppermute(x, "dp", [(0, 1), (1, 0)])

    def over_plane(x):
        return lax.all_to_all(x, "expert", 0, 0, axis_index_groups=plane, tiled=True)

    def over_slice(x):
        return lax.all_to_all(x, ("dp", "expert"), 0, 0, axis_index_groups=slice_groups, tiled=True)

    outgoing = call(
        functools.partial(route_kernel, dims),
        sds((peers * unit, LANES), BF),
        (ids, gate_values.T, tokens, target),
        [HBM] * 4,
        [
            pltpu.VMEM(ids.shape, ids.dtype),
            pltpu.VMEM(ids.shape, F32),
            pltpu.VMEM(tokens.shape, tokens.dtype),
            pltpu.VMEM(target.shape, target.dtype),
            pltpu.VMEM((16, features), F32),
            pltpu.VMEM((16, features), F32),
            pltpu.VMEM((blocks * cap, LANES), F32),
            pltpu.VMEM((unit - blocks * cap, LANES), F32),
            pltpu.SemaphoreType.DMA((4,)),
        ],
        limit=60,
        name="route",
    )
    own = over_slice(outgoing)
    other = other_core(own)
    first = -(-hid // (2 * LANES)) * LANES
    chunks = [(0, first), (first, hid - first)]
    last = len(chunks) - 1
    pres = []
    for start, size in chunks:
        outs = (sds((2, rows, size), F32), sds((2, rows, size), BF))
        cost = dict(flops=8 * rows * width * size, moved=4 * width * size)
        if start == 0:
            all_rows, all_target, all_gates, gate_w, up_w, *pre = call(
                functools.partial(first_pre_kernel, dims, size),
                (
                    sds((rows, width), BF),
                    sds((rows, LANES), F32),
                    sds((rows, LANES), F32),
                    sds(w_gate.shape, w_gate.dtype),
                    sds(w_up.shape, w_up.dtype),
                    *outs,
                ),
                (core, own, other, w_gate, w_up),
                [SMEM] + [VMEM] * 2 + [HBM] * 2,
                [
                    pltpu.VMEM((sources * unit, LANES), F32),
                    pltpu.SemaphoreType.DMA((2, 2)),
                ],
                limit=44,
                name="pre_activations",
                **cost,
            )
        else:
            pre = call(
                functools.partial(more_pre_kernel, start),
                outs,
                (all_rows, gate_w, up_w),
                [VMEM] * 3,
                name="pre_activations",
                **cost,
            )
        pres.append((pre[0], other_dp(pre[1])))
    saved = []
    total = ()
    for k, (start, size) in enumerate(chunks):
        outs = (sds((2 * half * rows, LANES), F32),)
        if k == last:
            outs = (sds((half * rows, LANES), F32), sds((half * rows, LANES), BF))
        up_deriv, act, *total = call(
            functools.partial(down_kernel, dims, start, k == last),
            (sds((rows, size), F32), sds((rows, size), F32), *outs),
            (core, *pres[k], w_down, *total),
            [SMEM] + [VMEM] * (3 + len(total)),
            [pltpu.VMEM((rows, size), BF)],
            flops=4 * rows * width * size,
            moved=2 * width * size,
            name="down",
        )
        saved.append((up_deriv, act))
    keep, send = total
    chip_out = (keep + other_core(send).astype(F32)).astype(BF)
    cot = call(
        functools.partial(cotangent_kernel, half),
        sds((half * rows, LANES), BF),
        (over_plane(chip_out), all_gates, all_target),
        [VMEM] * 3,
        name="cotangent",
    )
    own = over_plane(cot)
    other = other_core(own)
    grads = []
    for start, size in chunks:
        outs = (sds((rows, size), F32), sds((rows, size), BF))
        cost = dict(flops=4 * rows * width * size, moved=2 * width * size)
        if start == 0:
            cot, *grad = call(
                functools.partial(first_grad_hidden_kernel, start),
                (sds((rows, width), BF), *outs),
                (core, own, other, w_down),
                [SMEM] + [VMEM] * 3,
                name="grad_hidden",
                **cost,
            )
        else:
            grad = call(
                functools.partial(more_grad_hidden_kernel, start),
                outs,
                (cot, w_down),
                [VMEM] * 2,
                name="grad_hidden",
                **cost,
            )
        grads.append((grad[0], other_dp(grad[1])))
    pre_grads = []
    total = ()
    peer_rows = peers * blocks * cap
    for k, (start, size) in enumerate(chunks):
        outs, scratch = (sds((rows, width), F32),), []
        if k == last:
            outs = (sds((peer_rows, LANES), F32), sds((peer_rows, LANES), BF))
            scratch = [pltpu.VMEM((2 * peer_rows, LANES), F32)]
        gate_pre_grad, up_pre_grad, *total = call(
            functools.partial(row_grad_kernel, dims, start, k == last),
            (sds((rows, size), BF), sds((rows, size), BF), *outs),
            (core, *grads[k], *saved[k], gate_w, up_w, *total),
            [SMEM] + [VMEM] * (6 + len(total)),
            scratch,
            flops=8 * rows * width * size,
            moved=4 * width * size,
            name="row_grad",
        )
        pre_grads.append((gate_pre_grad, up_pre_grad))
    keep, send = total
    chip_rows = (keep + other_core(send).astype(F32)).astype(BF)
    got_rows = over_slice(chip_rows)
    pre_grads = [pair[0] for pair in pre_grads] + [pair[1] for pair in pre_grads]
    tile = 256
    gate_grad, up_grad = pl.pallas_call(
        functools.partial(weight_grad_kernel, len(chunks)),
        out_shape=(sds((width, hid), BF), sds((width, hid), BF)),
        grid=(width // tile,),
        in_specs=[pl.BlockSpec((rows, tile), lambda i: (0, i))]
        + [pl.BlockSpec(grad.shape, lambda i: (0, 0)) for grad in pre_grads],
        out_specs=(pl.BlockSpec((tile, hid), lambda i: (i, 0)), pl.BlockSpec((tile, hid), lambda i: (i, 0))),
        compiler_params=pltpu.CompilerParams(vmem_limit_bytes=16 << 20),
        cost_estimate=pl.CostEstimate(
            flops=4 * rows * width * hid, bytes_accessed=4 * width * hid, transcendentals=0
        ),
        name="weight_grads",
    )(all_rows, *pre_grads)
    token_grad = call(
        functools.partial(token_grad_kernel, dims),
        sds((tok_rows, features), tokens.dtype),
        (ids, got_rows),
        [VMEM] * 2,
        [pltpu.VMEM((16, features), F32)],
        name="token_grad",
    )
    return token_grad, gate_grad, up_grad


def contract_last(matrix_a, matrix_b):
    return lax.dot_general(
        matrix_a, matrix_b, (((1,), (1,)), ((), ())), preferred_element_type=jnp.float32
    )


def rounded_terms(column_blocks, grad_blocks):
    terms = jnp.einsum(
        "krd,krh->kdh", column_blocks, grad_blocks, preferred_element_type=jnp.float32
    )
    terms = lax.optimization_barrier(terms.astype(jnp.bfloat16))
    return jnp.sum(terms.astype(jnp.float32), axis=0)


def spread_rows(rows, group_size, capacity, features):
    flat = rows.reshape(EXPERTS, 1, capacity * features)
    wide = jnp.broadcast_to(flat, (EXPERTS, group_size, capacity * features))
    return wide.reshape(EXPERTS * group_size * capacity, features)


def fold_group(rows, group_size, capacity, features):
    shaped = rows.reshape(EXPERTS, group_size, capacity * features).astype(jnp.float32)
    return jnp.sum(shaped, axis=1).reshape(EXPERTS * capacity, features)


def general_shards(tokens, expert_ids, gate_values, w_gate, w_up, w_down, target):
    devices_along = lax.axis_size("expert")
    group_size = devices_along // EXPERTS
    tok_rows = tokens.shape[0]
    features = tokens.shape[1]
    hid_local = w_gate.shape[1]
    capacity = max(2, 3 * tok_rows // 128)
    slot_total = EXPERTS * capacity
    flat_ids = expert_ids.reshape(-1)
    pair_count = flat_ids.shape[0]
    window = flat_ids < EXPERTS
    onehot = (flat_ids[:, None] == jnp.arange(EXPERTS, dtype=jnp.int32)[None, :]).astype(jnp.int32)
    slot_index = jnp.sum((jnp.cumsum(onehot, axis=0) - onehot) * onehot, axis=1)
    position = jnp.where(window, flat_ids * capacity + slot_index, slot_total)
    owning = jnp.arange(pair_count, dtype=jnp.int32) // 2
    slot_token = jnp.zeros((slot_total + 1,), jnp.int32).at[position].set(owning)[:slot_total]
    slot_live = jnp.zeros((slot_total + 1,), jnp.bool_).at[position].set(True)[:slot_total]
    slot_gate = (
        jnp.zeros((slot_total + 1,), jnp.float32)
        .at[position]
        .set(gate_values.reshape(-1))[:slot_total]
    )
    safe_pairs = jnp.minimum(position, slot_total - 1).reshape(tok_rows, 2)
    live_pairs = window.reshape(tok_rows, 2)

    def pick(table, column):
        return jnp.where(live_pairs[:, column : column + 1], table[safe_pairs[:, column]], 0.0)

    outgoing = jnp.where(slot_live[:, None], tokens[slot_token], jnp.zeros((), tokens.dtype))
    outgoing = spread_rows(outgoing, group_size, capacity, features)
    received = lax.all_to_all(outgoing, "expert", split_axis=0, concat_axis=0, tiled=True)
    rows_count = received.shape[0]
    full_gate, full_up, full_down = (
        lax.all_gather(w_gate, "dp", axis=0, tiled=True),
        lax.all_gather(w_up, "dp", axis=0, tiled=True),
        lax.all_gather(w_down, "dp", axis=1, tiled=True),
    )
    gate_pre = jnp.dot(received, full_gate, preferred_element_type=jnp.float32)
    up_pre = jnp.dot(received, full_up, preferred_element_type=jnp.float32)
    sigmoid_gate = jax.nn.sigmoid(gate_pre)
    activated = sigmoid_gate * gate_pre
    hidden = (activated * up_pre).astype(jnp.bfloat16)
    partial_out = jnp.dot(hidden, full_down, preferred_element_type=jnp.float32).astype(
        jnp.bfloat16
    )
    returned_out = lax.all_to_all(partial_out, "expert", split_axis=0, concat_axis=0, tiled=True)
    expert_out = fold_group(returned_out, group_size, capacity, features)
    combined = gate_values[:, 0:1] * pick(expert_out, 0) + gate_values[:, 1:2] * pick(expert_out, 1)
    residual = combined - target.astype(jnp.float32)
    outgoing_grad = jnp.where(
        slot_live[:, None], slot_gate[:, None] * residual[slot_token], 0.0
    ).astype(jnp.bfloat16)
    outgoing_grad = spread_rows(outgoing_grad, group_size, capacity, features)
    cotangent = lax.all_to_all(outgoing_grad, "expert", split_axis=0, concat_axis=0, tiled=True)
    grad_hidden = contract_last(cotangent, full_down)
    derivative = sigmoid_gate * (1.0 + gate_pre * (1.0 - sigmoid_gate))
    grad_gate_pre = (grad_hidden * up_pre * derivative).astype(jnp.bfloat16)
    grad_up_pre = (grad_hidden * activated).astype(jnp.bfloat16)
    row_part = (
        contract_last(grad_gate_pre, full_gate) + contract_last(grad_up_pre, full_up)
    ).astype(jnp.bfloat16)
    back_rows = lax.all_to_all(row_part, "expert", split_axis=0, concat_axis=0, tiled=True)
    row_grad = fold_group(back_rows, group_size, capacity, features)
    token_grad = (pick(row_grad, 0) + pick(row_grad, 1)).astype(jnp.bfloat16)
    shard_columns = lax.all_to_all(received, "dp", split_axis=1, concat_axis=0, tiled=True)
    shard_width = shard_columns.shape[1]
    dp_count = lax.axis_size("dp")
    every_gate, every_up = (
        lax.all_gather(grad_gate_pre, "dp", axis=0, tiled=True),
        lax.all_gather(grad_up_pre, "dp", axis=0, tiled=True),
    )
    column_blocks = shard_columns.reshape(dp_count, rows_count, shard_width)
    gate_sum = rounded_terms(column_blocks, every_gate.reshape(dp_count, rows_count, hid_local))
    up_sum = rounded_terms(column_blocks, every_up.reshape(dp_count, rows_count, hid_local))
    return (token_grad, gate_sum.astype(jnp.bfloat16), up_sum.astype(jnp.bfloat16))


def solution(mesh):
    n_dp, n_expert = mesh.shape["dp"], mesh.shape["expert"]

    def shards(*args):
        tok_rows, features = args[0].shape
        width, hid = args[3].shape
        cap = max(2, 3 * tok_rows // 128)
        whole_blocks = (
            n_dp == 2
            and n_expert % 4 == 0
            and width == n_expert * LANES
            and hid % LANES == 0
            and n_dp * n_expert % 16 == 0
            and cap <= 8
            and tok_rows % LANES == 0
        )
        if whole_blocks:
            return fast_shards(n_dp, n_expert, cap, *args)
        return general_shards(*args)

    placed = (
        P(("dp", "expert"), None),
        P(("dp", "expert"), None),
        P(("dp", "expert"), None),
        P("dp", "expert"),
        P("dp", "expert"),
        P("expert", "dp"),
        P(("dp", "expert"), None),
    )
    return jax.shard_map(
        shards,
        mesh=mesh,
        in_specs=placed,
        out_specs=(P(("dp", "expert"), None), P("dp", "expert"), P("dp", "expert")),
        check_vma=False,
    )
```

```python
import functools

import jax
import jax.numpy as jnp
from jax import lax
from jax.experimental import pallas as pl
from jax.experimental.pallas import tpu as pltpu
from jax.sharding import PartitionSpec as P

EXPERTS = 1
LANES = 128
GATE_PIECES = 3
BF = jnp.bfloat16
F32 = jnp.float32
VMEM = pl.BlockSpec(memory_space=pltpu.VMEM)
HBM = pl.BlockSpec(memory_space=pltpu.HBM)
SMEM = pl.BlockSpec(memory_space=pltpu.SMEM)


def sds(shape, dtype):
    return jax.ShapeDtypeStruct(shape, dtype)


def dot_nn(a, b):
    return lax.dot_general(a, b, (((1,), (0,)), ((), ())), preferred_element_type=F32)


def dot_nt(a, b):
    return lax.dot_general(a, b, (((1,), (1,)), ((), ())), preferred_element_type=F32)


def dot_tn(a, b):
    return lax.dot_general(a, b, (((0,), (0,)), ((), ())), preferred_element_type=F32)


def call(body, outs, args, specs, scratch=(), limit=16, flops=0, moved=0, name=None, out_spec=VMEM):
    return pl.pallas_call(
        body,
        out_shape=outs,
        in_specs=specs,
        out_specs=jax.tree.map(lambda _: out_spec, outs),
        scratch_shapes=list(scratch),
        compiler_params=pltpu.CompilerParams(vmem_limit_bytes=limit << 20),
        cost_estimate=pl.CostEstimate(flops=flops, bytes_accessed=moved, transcendentals=0),
        name=name,
    )(*args)


def select_rows(ids_ref):
    tok_rows = ids_ref.shape[1]
    live = jnp.sum((ids_ref[...] < EXPERTS).astype(F32), axis=0, keepdims=True)
    before = lax.broadcasted_iota(jnp.int32, (tok_rows, tok_rows), 0)
    after = lax.broadcasted_iota(jnp.int32, (tok_rows, tok_rows), 1)
    earlier = (before < after).astype(BF)
    wide = jnp.broadcast_to(live, (16, tok_rows))
    slot = dot_nn(wide.astype(BF), earlier)
    wanted = lax.broadcasted_iota(jnp.int32, (16, tok_rows), 0).astype(F32)
    return jnp.where(slot == wanted, wide, 0.0)


def add_kernel(own_ref, got_ref, out_ref):
    out_ref[...] = (own_ref[...] + got_ref[...].astype(F32)).astype(out_ref.dtype)


def add_cores(own, got):
    return call(add_kernel, sds(got.shape, got.dtype), (own, got), [VMEM] * 2, name="add_cores")


def route_kernel(dims, ids_hbm, gates_hbm, tokens_hbm, target_hbm, out_ref,
                 ids_ref, gates_ref, tokens_ref, target_ref, tok, tgt, head, tail, sems):
    n_dp, half, cap, blocks, unit = dims
    pairs = (
        (ids_hbm, ids_ref),
        (gates_hbm, gates_ref),
        (tokens_hbm, tokens_ref),
        (target_hbm, target_ref),
    )
    copies = [pltpu.make_async_copy(src, dst, sems.at[i]) for i, (src, dst) in enumerate(pairs)]
    for copy in copies:
        copy.start()
    tail[...] = jnp.zeros_like(tail)
    copies[0].wait()
    copies[1].wait()
    chosen = select_rows(ids_ref)
    live_gates = jnp.sum(jnp.where(ids_ref[...] < EXPERTS, gates_ref[...], 0.0), axis=0, keepdims=True)
    gate = jnp.sum(chosen * live_gates, axis=1, keepdims=True)
    pick = chosen.astype(BF)
    copies[2].wait()
    tok[...] = dot_nn(pick, tokens_ref[...])
    copies[3].wait()
    tgt[...] = dot_nn(pick, target_ref[...])
    rest = gate
    for piece in range(GATE_PIECES):
        part = rest.astype(BF).astype(F32)
        rest = rest - part
        at = (2 + piece) * cap
        tail[at : at + cap, :] = jnp.broadcast_to(part[0:cap], (cap, LANES))
    width = blocks * LANES
    for d in range(n_dp):
        for q in range(blocks):
            lo = d * width + q * LANES
            head[q * cap : (q + 1) * cap, :] = tok[0:cap, lo : lo + LANES]
        packed = head[...].astype(BF)
        for h in range(half):
            for core in range(2):
                lo = d * width + (core * half + h) * LANES
                tail[core * cap : (core + 1) * cap, :] = tgt[0:cap, lo : lo + LANES]
            base = (d * half + h) * unit
            out_ref[base : base + blocks * cap, :] = packed
            out_ref[base + blocks * cap : base + unit, :] = tail[...].astype(BF)


def both_cores(core_ref, own_ref, other_ref, wide):
    size = own_ref.shape[0]
    core = core_ref[0]
    wide[pl.ds(pl.multiple_of(core * size, size), size), :] = own_ref[...].astype(wide.dtype)
    wide[pl.ds(pl.multiple_of((1 - core) * size, size), size), :] = other_ref[...].astype(wide.dtype)


def fetch_columns(starts, gate_hbm, up_hbm, gate_w, up_w, sems):
    lo, hi = starts
    copies = []
    for k, at in enumerate(range(lo, hi, 2 * LANES)):
        count = min(2 * LANES, hi - at)
        pair = []
        for side, (src, dst) in enumerate(((gate_hbm, gate_w), (up_hbm, up_w))):
            part = src.at[:, pl.ds(at, count)]
            pair.append(pltpu.make_async_copy(part, dst.at[:, pl.ds(at - lo, count)], sems.at[k, side]))
            pair[-1].start()
        copies.append(pair)
    return copies


def load_kernel(start, gate_hbm, up_hbm, *refs):
    done_ref, gate_w, up_w, sems = refs[-4:]
    stop = start + gate_w.shape[1]
    copies = fetch_columns((start, stop), gate_hbm, up_hbm, gate_w, up_w, sems)
    done_ref[...] = jnp.zeros_like(done_ref)
    for pair in copies:
        for copy in pair:
            copy.wait()


def partial_pre(rows_ref, gate_w, up_w, copies, first, own_pre, send_pre):
    for j in range(gate_w.shape[1] // LANES):
        if copies and j % 2 == 0:
            for copy in copies[j // 2]:
                copy.wait()
        here = slice(j * LANES, (j + 1) * LANES)
        cols = slice(first + j * LANES, first + (j + 1) * LANES)
        pair = jnp.concatenate([gate_w[:, here], up_w[:, here]], axis=1)
        both = dot_nn(rows_ref[...], pair)
        for side in range(2):
            value = both[:, side * LANES : (side + 1) * LANES]
            own_pre[side, :, cols] = value
            send_pre[side, :, cols] = value.astype(BF)


def first_pre_kernel(dims, core_ref, loaded_ref, own_ref, other_ref, gate_head, up_head, gate_rest, up_rest,
                     rows_ref, target_ref, gates_ref, own_pre, send_pre, wide):
    n_dp, half, cap, blocks, unit = dims
    sources = 2 * n_dp * half
    both_cores(core_ref, own_ref, other_ref, wide)
    core = core_ref[0]

    def one(k):
        return wide[pl.ds(k, sources, stride=unit), :]

    for c in range(cap):
        rows = slice(c * sources, (c + 1) * sources)
        for q in range(blocks):
            rows_ref[rows, q * LANES : (q + 1) * LANES] = one(q * cap + c).astype(BF)
        base = blocks * cap
        target_ref[rows, :] = jnp.where(core == 0, one(base + c), one(base + cap + c))
        gates_ref[rows, :] = sum(one(base + (2 + piece) * cap + c) for piece in range(GATE_PIECES))
    partial_pre(rows_ref, gate_head, up_head, (), 0, own_pre, send_pre)
    partial_pre(rows_ref, gate_rest, up_rest, (), gate_head.shape[1], own_pre, send_pre)


def more_pre_kernel(start, rows_ref, gate_hbm, up_hbm, own_pre, send_pre, gate_w, up_w, sems):
    copies = fetch_columns((start, start + own_pre.shape[2]), gate_hbm, up_hbm, gate_w, up_w, sems)
    partial_pre(rows_ref, gate_w, up_w, copies, 0, own_pre, send_pre)


def down_kernel(dims, start, last, core_ref, own_ref, got_ref, down_w, *refs):
    n_dp, half, cap, blocks, unit = dims
    refs = list(refs)
    total_ref = refs.pop(0) if start > 0 else None
    up_deriv, act_ref, *out_refs, hidden = refs
    gate_pre = own_ref[0] + got_ref[0].astype(F32)
    up_pre = own_ref[1] + got_ref[1].astype(F32)
    sig = jax.nn.sigmoid(gate_pre)
    act = sig * gate_pre
    act_ref[...] = act
    up_deriv[...] = up_pre * (sig * (1.0 + gate_pre * (1.0 - sig)))
    hidden[...] = (act * up_pre).astype(BF)
    rows, hid = hidden.shape
    core = core_ref[0]
    for side in range(2):

        def column(j, _, side=side):
            shown = core if side == 0 else 1 - core
            lo = (shown * half + 2 * j) * LANES
            cols = pl.ds(pl.multiple_of(lo, 2 * LANES), 2 * LANES)
            value = dot_nn(hidden[...], down_w[start : start + hid, cols])
            for k in range(2):
                part = value[:, k * LANES : (k + 1) * LANES]
                mine = pl.ds(pl.multiple_of((2 * j + k) * rows, rows), rows)
                both = pl.ds(pl.multiple_of((side * half + 2 * j + k) * rows, rows), rows)
                if total_ref is not None:
                    part = part + total_ref[both, :]
                if last:
                    out_refs[side][mine, :] = part.astype(out_refs[side].dtype)
                else:
                    out_refs[0][both, :] = part
            return 0

        lax.fori_loop(0, half // 2, column, 0, unroll=True)


def cotangent_kernel(parts, got_ref, gates_ref, target_ref, out_ref):
    rows = target_ref.shape[0]
    total = got_ref[0:rows, :].astype(F32)
    for h in range(1, parts):
        total = total + got_ref[h * rows : (h + 1) * rows, :].astype(F32)
    gate = gates_ref[...]
    value = (gate * (gate * total - target_ref[...])).astype(BF)
    for h in range(parts):
        out_ref[h * rows : (h + 1) * rows, :] = value


def partial_grad_hidden(cot, down_w, start, own_out, send_out):
    def column(j, _):
        cols = pl.ds(pl.multiple_of(j * LANES, LANES), LANES)
        at = pl.ds(pl.multiple_of(start + j * LANES, LANES), LANES)
        value = dot_nt(cot[...], down_w[at, :])
        own_out[:, cols] = value
        send_out[:, cols] = value.astype(BF)
        return 0

    lax.fori_loop(0, own_out.shape[1] // LANES, column, 0, unroll=True)


def first_grad_hidden_kernel(start, core_ref, own_ref, other_ref, down_w, cot, own_out, send_out):
    rows = cot.shape[0]
    parts = own_ref.shape[0] // rows
    core = core_ref[0]
    for ref, side in ((own_ref, core), (other_ref, 1 - core)):
        for h in range(parts):
            lo = (side * parts + h) * LANES
            cot[:, pl.ds(pl.multiple_of(lo, LANES), LANES)] = ref[h * rows : (h + 1) * rows, :]
    partial_grad_hidden(cot, down_w, start, own_out, send_out)


def more_grad_hidden_kernel(start, cot, down_w, own_out, send_out):
    partial_grad_hidden(cot, down_w, start, own_out, send_out)


def row_grad_kernel(dims, start, last, core_ref, own_ref, got_ref, up_deriv, act_ref, gate_w, up_w, *refs):
    n_dp, half, cap, blocks, unit = dims
    sources = 2 * n_dp * half
    refs = list(refs)
    total_ref = refs.pop(0) if start > 0 else None
    gate_out, up_out, *out_refs = refs
    grad_hidden = own_ref[...] + got_ref[...].astype(F32)
    gate_out[...] = (grad_hidden * up_deriv[...]).astype(BF)
    up_out[...] = (grad_hidden * act_ref[...]).astype(BF)
    hid = gate_out.shape[1]
    wide = out_refs[-1]

    def column(j, _):
        at = pl.ds(pl.multiple_of(j * 2 * LANES, 2 * LANES), 2 * LANES)
        value = dot_nt(gate_out[...], gate_w[at, start : start + hid])
        value = value + dot_nt(up_out[...], up_w[at, start : start + hid])
        if total_ref is not None:
            value = value + total_ref[:, at]
        if not last:
            wide[:, at] = value
            return 0
        for k in range(2):
            for c in range(cap):
                piece = value[c * sources : (c + 1) * sources, k * LANES : (k + 1) * LANES]
                wide[pl.ds((2 * j + k) * cap + c, sources, stride=blocks * cap), :] = piece
        return 0

    lax.fori_loop(0, blocks // 2, column, 0, unroll=True)
    if last:
        keep_ref, send_ref, _ = out_refs
        size = keep_ref.shape[0]
        core = core_ref[0]
        keep_ref[...] = wide[pl.ds(pl.multiple_of(core * size, size), size), :]
        send_ref[...] = wide[pl.ds(pl.multiple_of((1 - core) * size, size), size), :].astype(BF)


def weight_grad_kernel(parts, rows_ref, *refs):
    gate_out, up_out = refs[-2:]
    rows = rows_ref[...]
    lo = 0
    for k in range(parts):
        size = refs[k].shape[1]
        gate_out[:, lo : lo + size] = dot_tn(rows, refs[k][...]).astype(BF)
        up_out[:, lo : lo + size] = dot_tn(rows, refs[parts + k][...]).astype(BF)
        lo += size


def token_grad_kernel(dims, ids_ref, got_ref, out_hbm, rows, out, sems):
    n_dp, half, cap, blocks, unit = dims
    size = blocks * cap
    width = blocks * LANES
    pick = select_rows(ids_ref).astype(BF)
    rows[...] = jnp.zeros_like(rows)
    copies = []
    for d in range(n_dp):
        total = got_ref[d * half * size : (d * half + 1) * size, :].astype(F32)
        for h in range(1, half):
            base = (d * half + h) * size
            total = total + got_ref[base : base + size, :].astype(F32)
        for q in range(blocks):
            rows[0:cap, q * LANES : (q + 1) * LANES] = total[q * cap : (q + 1) * cap, :]
        cols = slice(d * width, (d + 1) * width)
        out[:, cols] = dot_tn(pick, rows[...].astype(BF)).astype(out.dtype)
        copies.append(pltpu.make_async_copy(out.at[:, cols], out_hbm.at[:, cols], sems.at[d]))
        copies[-1].start()
    for copy in copies:
        copy.wait()


def fast_shards(n_dp, n_expert, cap, tokens, expert_ids, gate_values, w_gate, w_up, w_down, target):
    tok_rows, features = tokens.shape
    width, hid = w_gate.shape
    half = n_expert // 2
    blocks = width // LANES
    peers = n_dp * half
    sources = 2 * peers
    rows = cap * sources
    unit = -(-(blocks + 2 + GATE_PIECES) * cap // 16) * 16
    dims = (n_dp, half, cap, blocks, unit)
    core = (lax.axis_index("expert") % 2).astype(jnp.int32).reshape(1)
    ids = expert_ids.T
    plane = [[2 * h + c for h in range(half)] for c in range(2)]
    slice_groups = [
        [d * n_expert + 2 * h + c for d in range(n_dp) for h in range(half)] for c in range(2)
    ]

    def other_core(x):
        return lax.ppermute(x, "expert", [(i, i ^ 1) for i in range(n_expert)])

    def other_dp(x):
        return lax.ppermute(x, "dp", [(0, 1), (1, 0)])

    def over_plane(x):
        return lax.all_to_all(x, "expert", 0, 0, axis_index_groups=plane, tiled=True)

    def over_slice(x):
        return lax.all_to_all(x, ("dp", "expert"), 0, 0, axis_index_groups=slice_groups, tiled=True)

    outgoing = call(
        functools.partial(route_kernel, dims),
        sds((peers * unit, LANES), BF),
        (ids, gate_values.T, tokens, target),
        [HBM] * 4,
        [
            pltpu.VMEM(ids.shape, ids.dtype),
            pltpu.VMEM(ids.shape, F32),
            pltpu.VMEM(tokens.shape, tokens.dtype),
            pltpu.VMEM(target.shape, target.dtype),
            pltpu.VMEM((16, features), F32),
            pltpu.VMEM((16, features), F32),
            pltpu.VMEM((blocks * cap, LANES), F32),
            pltpu.VMEM((unit - blocks * cap, LANES), F32),
            pltpu.SemaphoreType.DMA((4,)),
        ],
        limit=60,
        name="route",
    )
    first = -(-hid // (2 * LANES)) * LANES
    head = 2 * LANES

    def load(start, size, after=()):
        return call(
            functools.partial(load_kernel, start),
            (sds((8, LANES), F32), sds((width, size), w_gate.dtype), sds((width, size), w_up.dtype)),
            (w_gate, w_up, *after),
            [HBM] * 2 + [VMEM] * len(after),
            [pltpu.SemaphoreType.DMA((-(-size // (2 * LANES)), 2))],
            limit=50,
            flops=1_000_000_000,
            moved=8 * width * size,
            name="load_weights",
        )

    loaded, *weights = load(0, head)
    own, loaded = lax.optimization_barrier((over_slice(outgoing), loaded))
    loaded, *more = load(head, first - head, (loaded,))
    weights += more
    other = other_core(own)
    chunks = [(0, first), (first, hid - first)]
    last = len(chunks) - 1
    pres = []
    for start, size in chunks:
        outs = (sds((2, rows, size), F32), sds((2, rows, size), BF))
        cost = dict(flops=8 * rows * width * size, moved=4 * width * size)
        fetched = [
            pltpu.VMEM((width, size), w_gate.dtype),
            pltpu.VMEM((width, size), w_up.dtype),
            pltpu.SemaphoreType.DMA((-(-size // (2 * LANES)), 2)),
        ]
        if start == 0:
            all_rows, all_target, all_gates, *pre = call(
                functools.partial(first_pre_kernel, dims),
                (sds((rows, width), BF), sds((rows, LANES), F32), sds((rows, LANES), F32), *outs),
                (core, loaded, own, other, *weights),
                [SMEM] + [VMEM] * 7,
                [pltpu.VMEM((sources * unit, LANES), F32)],
                name="pre_activations",
                **cost,
            )
        else:
            pre = call(
                functools.partial(more_pre_kernel, start),
                outs,
                (all_rows, w_gate, w_up),
                [VMEM] + [HBM] * 2,
                fetched,
                limit=50,
                name="pre_activations",
                **cost,
            )
        pres.append((pre[0], other_dp(pre[1])))
    saved = []
    total = ()
    for k, (start, size) in enumerate(chunks):
        outs = (sds((2 * half * rows, LANES), F32),)
        if k == last:
            outs = (sds((half * rows, LANES), F32), sds((half * rows, LANES), BF))
        up_deriv, act, *total = call(
            functools.partial(down_kernel, dims, start, k == last),
            (sds((rows, size), F32), sds((rows, size), F32), *outs),
            (core, *pres[k], w_down, *total),
            [SMEM] + [VMEM] * (3 + len(total)),
            [pltpu.VMEM((rows, size), BF)],
            flops=4 * rows * width * size,
            moved=2 * width * size,
            name="down",
        )
        saved.append((up_deriv, act))
    keep, send = total
    chip_out = add_cores(keep, other_core(send))
    cot = call(
        functools.partial(cotangent_kernel, half),
        sds((half * rows, LANES), BF),
        (over_plane(chip_out), all_gates, all_target),
        [VMEM] * 3,
        name="cotangent",
    )
    own = over_plane(cot)
    other = other_core(own)
    grads = []
    for start, size in chunks:
        outs = (sds((rows, size), F32), sds((rows, size), BF))
        cost = dict(flops=4 * rows * width * size, moved=2 * width * size)
        if start == 0:
            cot, *grad = call(
                functools.partial(first_grad_hidden_kernel, start),
                (sds((rows, width), BF), *outs),
                (core, own, other, w_down),
                [SMEM] + [VMEM] * 3,
                name="grad_hidden",
                **cost,
            )
        else:
            grad = call(
                functools.partial(more_grad_hidden_kernel, start),
                outs,
                (cot, w_down),
                [VMEM] * 2,
                name="grad_hidden",
                **cost,
            )
        grads.append((grad[0], other_dp(grad[1])))
    pre_grads = []
    total = ()
    peer_rows = peers * blocks * cap
    for k, (start, size) in enumerate(chunks):
        outs, scratch = (sds((rows, width), F32),), []
        if k == last:
            outs = (sds((peer_rows, LANES), F32), sds((peer_rows, LANES), BF))
            scratch = [pltpu.VMEM((2 * peer_rows, LANES), F32)]
        gate_pre_grad, up_pre_grad, *total = call(
            functools.partial(row_grad_kernel, dims, start, k == last),
            (sds((rows, size), BF), sds((rows, size), BF), *outs),
            (core, *grads[k], *saved[k], w_gate, w_up, *total),
            [SMEM] + [VMEM] * (6 + len(total)),
            scratch,
            flops=8 * rows * width * size,
            moved=4 * width * size,
            name="row_grad",
        )
        pre_grads.append((gate_pre_grad, up_pre_grad))
    keep, send = total
    chip_rows = add_cores(keep, other_core(send))
    got_rows = over_slice(chip_rows)
    pre_grads = [pair[0] for pair in pre_grads] + [pair[1] for pair in pre_grads]
    tile = 256
    gate_grad, up_grad = pl.pallas_call(
        functools.partial(weight_grad_kernel, len(chunks)),
        out_shape=(sds((width, hid), BF), sds((width, hid), BF)),
        grid=(width // tile,),
        in_specs=[pl.BlockSpec((rows, tile), lambda i: (0, i))]
        + [pl.BlockSpec(grad.shape, lambda i: (0, 0)) for grad in pre_grads],
        out_specs=(pl.BlockSpec((tile, hid), lambda i: (i, 0)), pl.BlockSpec((tile, hid), lambda i: (i, 0))),
        compiler_params=pltpu.CompilerParams(vmem_limit_bytes=16 << 20),
        cost_estimate=pl.CostEstimate(
            flops=4 * rows * width * hid, bytes_accessed=4 * width * hid, transcendentals=0
        ),
        name="weight_grads",
    )(all_rows, *pre_grads)
    token_grad = call(
        functools.partial(token_grad_kernel, dims),
        sds((tok_rows, features), tokens.dtype),
        (ids, got_rows),
        [VMEM] * 2,
        [
            pltpu.VMEM((16, width), F32),
            pltpu.VMEM((tok_rows, features), tokens.dtype),
            pltpu.SemaphoreType.DMA((n_dp,)),
        ],
        out_spec=HBM,
        name="token_grad",
    )
    return token_grad, gate_grad, up_grad


def contract_last(matrix_a, matrix_b):
    return lax.dot_general(
        matrix_a, matrix_b, (((1,), (1,)), ((), ())), preferred_element_type=jnp.float32
    )


def rounded_terms(column_blocks, grad_blocks):
    terms = jnp.einsum(
        "krd,krh->kdh", column_blocks, grad_blocks, preferred_element_type=jnp.float32
    )
    terms = lax.optimization_barrier(terms.astype(jnp.bfloat16))
    return jnp.sum(terms.astype(jnp.float32), axis=0)


def spread_rows(rows, group_size, capacity, features):
    flat = rows.reshape(EXPERTS, 1, capacity * features)
    wide = jnp.broadcast_to(flat, (EXPERTS, group_size, capacity * features))
    return wide.reshape(EXPERTS * group_size * capacity, features)


def fold_group(rows, group_size, capacity, features):
    shaped = rows.reshape(EXPERTS, group_size, capacity * features).astype(jnp.float32)
    return jnp.sum(shaped, axis=1).reshape(EXPERTS * capacity, features)


def general_shards(tokens, expert_ids, gate_values, w_gate, w_up, w_down, target):
    devices_along = lax.axis_size("expert")
    group_size = devices_along // EXPERTS
    tok_rows = tokens.shape[0]
    features = tokens.shape[1]
    hid_local = w_gate.shape[1]
    capacity = max(2, 3 * tok_rows // 128)
    slot_total = EXPERTS * capacity
    flat_ids = expert_ids.reshape(-1)
    pair_count = flat_ids.shape[0]
    window = flat_ids < EXPERTS
    onehot = (flat_ids[:, None] == jnp.arange(EXPERTS, dtype=jnp.int32)[None, :]).astype(jnp.int32)
    slot_index = jnp.sum((jnp.cumsum(onehot, axis=0) - onehot) * onehot, axis=1)
    position = jnp.where(window, flat_ids * capacity + slot_index, slot_total)
    owning = jnp.arange(pair_count, dtype=jnp.int32) // 2
    slot_token = jnp.zeros((slot_total + 1,), jnp.int32).at[position].set(owning)[:slot_total]
    slot_live = jnp.zeros((slot_total + 1,), jnp.bool_).at[position].set(True)[:slot_total]
    slot_gate = (
        jnp.zeros((slot_total + 1,), jnp.float32)
        .at[position]
        .set(gate_values.reshape(-1))[:slot_total]
    )
    safe_pairs = jnp.minimum(position, slot_total - 1).reshape(tok_rows, 2)
    live_pairs = window.reshape(tok_rows, 2)

    def pick(table, column):
        return jnp.where(live_pairs[:, column : column + 1], table[safe_pairs[:, column]], 0.0)

    outgoing = jnp.where(slot_live[:, None], tokens[slot_token], jnp.zeros((), tokens.dtype))
    outgoing = spread_rows(outgoing, group_size, capacity, features)
    received = lax.all_to_all(outgoing, "expert", split_axis=0, concat_axis=0, tiled=True)
    rows_count = received.shape[0]
    full_gate, full_up, full_down = (
        lax.all_gather(w_gate, "dp", axis=0, tiled=True),
        lax.all_gather(w_up, "dp", axis=0, tiled=True),
        lax.all_gather(w_down, "dp", axis=1, tiled=True),
    )
    gate_pre = jnp.dot(received, full_gate, preferred_element_type=jnp.float32)
    up_pre = jnp.dot(received, full_up, preferred_element_type=jnp.float32)
    sigmoid_gate = jax.nn.sigmoid(gate_pre)
    activated = sigmoid_gate * gate_pre
    hidden = (activated * up_pre).astype(jnp.bfloat16)
    partial_out = jnp.dot(hidden, full_down, preferred_element_type=jnp.float32).astype(
        jnp.bfloat16
    )
    returned_out = lax.all_to_all(partial_out, "expert", split_axis=0, concat_axis=0, tiled=True)
    expert_out = fold_group(returned_out, group_size, capacity, features)
    combined = gate_values[:, 0:1] * pick(expert_out, 0) + gate_values[:, 1:2] * pick(expert_out, 1)
    residual = combined - target.astype(jnp.float32)
    outgoing_grad = jnp.where(
        slot_live[:, None], slot_gate[:, None] * residual[slot_token], 0.0
    ).astype(jnp.bfloat16)
    outgoing_grad = spread_rows(outgoing_grad, group_size, capacity, features)
    cotangent = lax.all_to_all(outgoing_grad, "expert", split_axis=0, concat_axis=0, tiled=True)
    grad_hidden = contract_last(cotangent, full_down)
    derivative = sigmoid_gate * (1.0 + gate_pre * (1.0 - sigmoid_gate))
    grad_gate_pre = (grad_hidden * up_pre * derivative).astype(jnp.bfloat16)
    grad_up_pre = (grad_hidden * activated).astype(jnp.bfloat16)
    row_part = (
        contract_last(grad_gate_pre, full_gate) + contract_last(grad_up_pre, full_up)
    ).astype(jnp.bfloat16)
    back_rows = lax.all_to_all(row_part, "expert", split_axis=0, concat_axis=0, tiled=True)
    row_grad = fold_group(back_rows, group_size, capacity, features)
    token_grad = (pick(row_grad, 0) + pick(row_grad, 1)).astype(jnp.bfloat16)
    shard_columns = lax.all_to_all(received, "dp", split_axis=1, concat_axis=0, tiled=True)
    shard_width = shard_columns.shape[1]
    dp_count = lax.axis_size("dp")
    every_gate, every_up = (
        lax.all_gather(grad_gate_pre, "dp", axis=0, tiled=True),
        lax.all_gather(grad_up_pre, "dp", axis=0, tiled=True),
    )
    column_blocks = shard_columns.reshape(dp_count, rows_count, shard_width)
    gate_sum = rounded_terms(column_blocks, every_gate.reshape(dp_count, rows_count, hid_local))
    up_sum = rounded_terms(column_blocks, every_up.reshape(dp_count, rows_count, hid_local))
    return (token_grad, gate_sum.astype(jnp.bfloat16), up_sum.astype(jnp.bfloat16))


def solution(mesh):
    n_dp, n_expert = mesh.shape["dp"], mesh.shape["expert"]

    def shards(*args):
        tok_rows, features = args[0].shape
        width, hid = args[3].shape
        cap = max(2, 3 * tok_rows // 128)
        whole_blocks = (
            n_dp == 2
            and n_expert % 4 == 0
            and width == n_expert * LANES
            and hid % LANES == 0
            and hid > 4 * LANES
            and n_dp * n_expert % 16 == 0
            and cap <= 8
            and tok_rows % LANES == 0
        )
        if whole_blocks:
            return fast_shards(n_dp, n_expert, cap, *args)
        return general_shards(*args)

    placed = (
        P(("dp", "expert"), None),
        P(("dp", "expert"), None),
        P(("dp", "expert"), None),
        P("dp", "expert"),
        P("dp", "expert"),
        P("expert", "dp"),
        P(("dp", "expert"), None),
    )
    return jax.shard_map(
        shards,
        mesh=mesh,
        in_specs=placed,
        out_specs=(P(("dp", "expert"), None), P("dp", "expert"), P("dp", "expert")),
        check_vma=False,
    )
```

```python
import functools

import jax
import jax.numpy as jnp
from jax import lax
from jax.experimental import pallas as pl
from jax.experimental.pallas import tpu as pltpu
from jax.sharding import PartitionSpec as P

EXPERTS = 1
LANES = 128
GATE_PIECES = 3
BF = jnp.bfloat16
F32 = jnp.float32
VMEM = pl.BlockSpec(memory_space=pltpu.VMEM)
HBM = pl.BlockSpec(memory_space=pltpu.HBM)
SMEM = pl.BlockSpec(memory_space=pltpu.SMEM)


def sds(shape, dtype):
    return jax.ShapeDtypeStruct(shape, dtype)


def dot_nn(a, b):
    return lax.dot_general(a, b, (((1,), (0,)), ((), ())), preferred_element_type=F32)


def dot_nt(a, b):
    return lax.dot_general(a, b, (((1,), (1,)), ((), ())), preferred_element_type=F32)


def dot_tn(a, b):
    return lax.dot_general(a, b, (((0,), (0,)), ((), ())), preferred_element_type=F32)


def in_hbm(*arrays):
    return tuple(pltpu.with_memory_space_constraint(x, pltpu.HBM) for x in arrays)


def call(body, outs, args, specs, scratch=(), limit=16, flops=0, moved=0, name=None, out_spec=VMEM):
    return pl.pallas_call(
        body,
        out_shape=outs,
        in_specs=specs,
        out_specs=jax.tree.map(lambda _: out_spec, outs),
        scratch_shapes=list(scratch),
        compiler_params=pltpu.CompilerParams(vmem_limit_bytes=limit << 20),
        cost_estimate=pl.CostEstimate(flops=flops, bytes_accessed=moved, transcendentals=0),
        name=name,
    )(*args)


def select_rows(ids_ref):
    tok_rows = ids_ref.shape[1]
    live = jnp.sum((ids_ref[...] < EXPERTS).astype(F32), axis=0, keepdims=True)
    before = lax.broadcasted_iota(jnp.int32, (tok_rows, tok_rows), 0)
    after = lax.broadcasted_iota(jnp.int32, (tok_rows, tok_rows), 1)
    earlier = (before < after).astype(BF)
    wide = jnp.broadcast_to(live, (16, tok_rows))
    slot = dot_nn(wide.astype(BF), earlier)
    wanted = lax.broadcasted_iota(jnp.int32, (16, tok_rows), 0).astype(F32)
    return jnp.where(slot == wanted, wide, 0.0)


def add_kernel(own_ref, got_ref, out_ref):
    out_ref[...] = (own_ref[...] + got_ref[...].astype(F32)).astype(out_ref.dtype)


def add_cores(own, got):
    return call(add_kernel, sds(got.shape, got.dtype), (own, got), [VMEM] * 2, name="add_cores")


def route_kernel(dims, ids_hbm, gates_hbm, tokens_hbm, target_hbm, out_ref,
                 ids_ref, gates_ref, tokens_ref, target_ref, tok, tgt, head, tail, sems):
    n_dp, half, cap, blocks, unit = dims
    width = blocks * LANES
    pairs = [(ids_hbm, ids_ref), (gates_hbm, gates_ref)]
    for hbm, ref in ((tokens_hbm, tokens_ref), (target_hbm, target_ref)):
        for d in range(n_dp):
            cols = slice(d * width, (d + 1) * width)
            pairs.append((hbm.at[:, cols], ref.at[:, cols]))
    copies = [pltpu.make_async_copy(src, dst, sems.at[i]) for i, (src, dst) in enumerate(pairs)]
    for copy in copies:
        copy.start()
    tail[...] = jnp.zeros_like(tail)
    copies[0].wait()
    copies[1].wait()
    chosen = select_rows(ids_ref)
    live_gates = jnp.sum(jnp.where(ids_ref[...] < EXPERTS, gates_ref[...], 0.0), axis=0, keepdims=True)
    gate = jnp.sum(chosen * live_gates, axis=1, keepdims=True)
    pick = chosen.astype(BF)
    rest = gate
    for piece in range(GATE_PIECES):
        part = rest.astype(BF).astype(F32)
        rest = rest - part
        at = (2 + piece) * cap
        tail[at : at + cap, :] = jnp.broadcast_to(part[0:cap], (cap, LANES))
    lead = blocks * cap
    for d in range(n_dp):
        cols = slice(d * width, (d + 1) * width)
        copies[2 + d].wait()
        tok[...] = dot_nn(pick, tokens_ref[:, cols])
        for q in range(blocks):
            head[q * cap : (q + 1) * cap, :] = tok[0:cap, q * LANES : (q + 1) * LANES]
        packed = head[...].astype(BF)
        for h in range(half):
            base = (d * half + h) * unit
            out_ref[base : base + lead, :] = packed
    for d in range(n_dp):
        cols = slice(d * width, (d + 1) * width)
        copies[2 + n_dp + d].wait()
        tgt[...] = dot_nn(pick, target_ref[:, cols])
        for h in range(half):
            for core in range(2):
                lo = (core * half + h) * LANES
                tail[core * cap : (core + 1) * cap, :] = tgt[0:cap, lo : lo + LANES]
            base = (d * half + h) * unit
            out_ref[base + lead : base + unit, :] = tail[...].astype(BF)


def both_cores(core_ref, own_ref, other_ref, wide):
    size = own_ref.shape[0]
    core = core_ref[0]
    wide[pl.ds(pl.multiple_of(core * size, size), size), :] = own_ref[...].astype(wide.dtype)
    wide[pl.ds(pl.multiple_of((1 - core) * size, size), size), :] = other_ref[...].astype(wide.dtype)


def fetch_columns(starts, gate_hbm, up_hbm, gate_w, up_w, sems):
    lo, hi = starts
    copies = []
    for k, at in enumerate(range(lo, hi, 2 * LANES)):
        count = min(2 * LANES, hi - at)
        pair = []
        for side, (src, dst) in enumerate(((gate_hbm, gate_w), (up_hbm, up_w))):
            part = src.at[:, pl.ds(at, count)]
            pair.append(pltpu.make_async_copy(part, dst.at[:, pl.ds(at - lo, count)], sems.at[k, side]))
            pair[-1].start()
        copies.append(pair)
    return copies


def load_kernel(start, gate_hbm, up_hbm, *refs):
    done_ref, gate_w, up_w, sems = refs[-4:]
    stop = start + gate_w.shape[1]
    copies = fetch_columns((start, stop), gate_hbm, up_hbm, gate_w, up_w, sems)
    done_ref[...] = jnp.zeros_like(done_ref)
    for pair in copies:
        for copy in pair:
            copy.wait()


def partial_pre(rows_ref, gate_w, up_w, copies, first, own_pre, send_pre):
    for j in range(gate_w.shape[1] // LANES):
        if copies and j % 2 == 0:
            for copy in copies[j // 2]:
                copy.wait()
        here = slice(j * LANES, (j + 1) * LANES)
        cols = slice(first + j * LANES, first + (j + 1) * LANES)
        pair = jnp.concatenate([gate_w[:, here], up_w[:, here]], axis=1)
        both = dot_nn(rows_ref[...], pair)
        for side in range(2):
            value = both[:, side * LANES : (side + 1) * LANES]
            own_pre[side, :, cols] = value
            send_pre[side, :, cols] = value.astype(BF)


def first_pre_kernel(dims, core_ref, loaded_ref, own_ref, other_ref, gate_head, up_head, gate_rest, up_rest,
                     rows_ref, target_ref, gates_ref, own_pre, send_pre, wide):
    n_dp, half, cap, blocks, unit = dims
    sources = 2 * n_dp * half
    both_cores(core_ref, own_ref, other_ref, wide)
    core = core_ref[0]

    def one(k):
        return wide[pl.ds(k, sources, stride=unit), :]

    for c in range(cap):
        rows = slice(c * sources, (c + 1) * sources)
        for q in range(blocks):
            rows_ref[rows, q * LANES : (q + 1) * LANES] = one(q * cap + c).astype(BF)
        base = blocks * cap
        target_ref[rows, :] = jnp.where(core == 0, one(base + c), one(base + cap + c))
        gates_ref[rows, :] = sum(one(base + (2 + piece) * cap + c) for piece in range(GATE_PIECES))
    partial_pre(rows_ref, gate_head, up_head, (), 0, own_pre, send_pre)
    partial_pre(rows_ref, gate_rest, up_rest, (), gate_head.shape[1], own_pre, send_pre)


def more_pre_kernel(start, rows_ref, gate_hbm, up_hbm, turned_ref, own_pre, send_pre, gate_w, up_w, sems):
    copies = fetch_columns((start, start + own_pre.shape[2]), gate_hbm, up_hbm, gate_w, up_w, sems)
    turned_ref[...] = rows_ref[...].T
    partial_pre(rows_ref, gate_w, up_w, copies, 0, own_pre, send_pre)


def down_side(dims, start, lo, hidden, down_w, total_ref, side, out_ref):
    n_dp, half, cap, blocks, unit = dims
    rows, hid = hidden.shape
    for j in range(half // 2):
        cols = pl.ds(pl.multiple_of((lo + 2 * j) * LANES, 2 * LANES), 2 * LANES)
        value = dot_nn(hidden[...], down_w[start : start + hid, cols])
        for k in range(2):
            part = value[:, k * LANES : (k + 1) * LANES]
            block = 2 * j + k
            if total_ref is not None:
                both = side * half + block
                part = part + total_ref[both * rows : (both + 1) * rows, :]
            out_ref[block * rows : (block + 1) * rows, :] = part.astype(out_ref.dtype)


def activate(own_ref, got_ref, up_deriv, act_ref, hidden):
    gate_pre = own_ref[0] + got_ref[0].astype(F32)
    up_pre = own_ref[1] + got_ref[1].astype(F32)
    sig = jax.nn.sigmoid(gate_pre)
    act = sig * gate_pre
    act_ref[...] = act
    up_deriv[...] = up_pre * (sig * (1.0 + gate_pre * (1.0 - sig)))
    hidden[...] = (act * up_pre).astype(BF)


def first_down_kernel(dims, start, core_ref, own_ref, got_ref, down_w, up_deriv, act_ref, total_ref, hidden):
    half = dims[1]
    activate(own_ref, got_ref, up_deriv, act_ref, hidden)
    size = half * hidden.shape[0]
    for side, core in enumerate((core_ref[0], 1 - core_ref[0])):
        part = total_ref.at[side * size : (side + 1) * size]
        down_side(dims, start, core * half, hidden, down_w, None, side, part)


def send_down_kernel(dims, start, core_ref, own_ref, got_ref, down_w, total_ref, up_deriv, act_ref, hidden, send_ref):
    activate(own_ref, got_ref, up_deriv, act_ref, hidden)
    down_side(dims, start, (1 - core_ref[0]) * dims[1], hidden, down_w, total_ref, 1, send_ref)


def keep_down_kernel(dims, start, core_ref, hidden, down_w, total_ref, keep_ref):
    down_side(dims, start, core_ref[0] * dims[1], hidden, down_w, total_ref, 0, keep_ref)


def cotangent_kernel(parts, got_ref, gates_ref, target_ref, out_ref):
    rows = target_ref.shape[0]
    total = got_ref[0:rows, :].astype(F32)
    for h in range(1, parts):
        total = total + got_ref[h * rows : (h + 1) * rows, :].astype(F32)
    gate = gates_ref[...]
    value = (gate * (gate * total - target_ref[...])).astype(BF)
    for h in range(parts):
        out_ref[h * rows : (h + 1) * rows, :] = value


def gather_blocks(ref, out):
    rows = out.shape[0]
    for h in range(out.shape[1] // LANES):
        out[:, h * LANES : (h + 1) * LANES] = ref[h * rows : (h + 1) * rows, :]


def half_grad_hidden(cot, core, down_w, start, total_ref, outs):
    width = cot.shape[1]
    cols = pl.ds(pl.multiple_of(core * width, width), width)
    size = outs[0].shape[1]
    for lo in range(0, size, 2 * LANES):
        here = slice(lo, min(lo + 2 * LANES, size))
        there = slice(start + here.start, start + here.stop)
        value = dot_nt(cot[...], down_w[there, cols])
        if total_ref is not None:
            value = value + total_ref[:, there]
        for out in outs:
            out[:, here] = value.astype(out.dtype)


def own_grad_hidden_kernel(core_ref, own_ref, down_w, total_ref, cot):
    gather_blocks(own_ref, cot)
    half_grad_hidden(cot, core_ref[0], down_w, 0, None, (total_ref,))


def first_grad_hidden_kernel(start, core_ref, other_ref, down_w, total_ref, cot, own_out, send_out):
    gather_blocks(other_ref, cot)
    half_grad_hidden(cot, 1 - core_ref[0], down_w, start, total_ref, (own_out, send_out))


def more_grad_hidden_kernel(start, core_ref, cot, down_w, total_ref, own_out, send_out):
    half_grad_hidden(cot, 1 - core_ref[0], down_w, start, total_ref, (own_out, send_out))


def row_grad_kernel(dims, start, last, core_ref, own_ref, got_ref, up_deriv, act_ref, gate_w, up_w, *refs):
    n_dp, half, cap, blocks, unit = dims
    sources = 2 * n_dp * half
    refs = list(refs)
    total_ref = refs.pop(0) if start > 0 else None
    gate_out, up_out, *out_refs = refs
    grad_hidden = own_ref[...] + got_ref[...].astype(F32)
    gate_out[...] = (grad_hidden * up_deriv[...]).astype(BF)
    up_out[...] = (grad_hidden * act_ref[...]).astype(BF)
    hid = gate_out.shape[1]
    wide = out_refs[-1]

    def column(j, _):
        at = pl.ds(pl.multiple_of(j * 2 * LANES, 2 * LANES), 2 * LANES)
        value = dot_nt(gate_out[...], gate_w[at, start : start + hid])
        value = value + dot_nt(up_out[...], up_w[at, start : start + hid])
        if total_ref is not None:
            value = value + total_ref[:, at]
        if not last:
            wide[:, at] = value
            return 0
        for k in range(2):
            for c in range(cap):
                piece = value[c * sources : (c + 1) * sources, k * LANES : (k + 1) * LANES]
                wide[pl.ds((2 * j + k) * cap + c, sources, stride=blocks * cap), :] = piece
        return 0

    lax.fori_loop(0, blocks // 2, column, 0, unroll=True)
    if last:
        keep_ref, send_ref, _ = out_refs
        size = keep_ref.shape[0]
        core = core_ref[0]
        keep_ref[...] = wide[pl.ds(pl.multiple_of(core * size, size), size), :]
        send_ref[...] = wide[pl.ds(pl.multiple_of((1 - core) * size, size), size), :].astype(BF)


def weight_grad_kernel(parts, tile, turned_ref, *refs):
    grads = (refs[:parts], refs[parts : 2 * parts])
    outs, values, sems = refs[2 * parts : 2 * parts + 2], refs[2 * parts + 2 : 2 * parts + 4], refs[-1]
    copies = []
    for t in range(turned_ref.shape[0] // tile):
        at = slice(t * tile, (t + 1) * tile)
        for side in range(2):
            lo = 0
            for ref in grads[side]:
                size = ref.shape[1]
                values[side][at, lo : lo + size] = dot_nn(turned_ref[at, :], ref[...]).astype(BF)
                lo += size
            copies.append(pltpu.make_async_copy(values[side].at[at, :], outs[side].at[at, :], sems.at[t, side]))
            copies[-1].start()
    for copy in copies:
        copy.wait()


def token_grad_kernel(dims, ids_ref, got_ref, out_hbm, rows, out, sems):
    n_dp, half, cap, blocks, unit = dims
    size = blocks * cap
    width = blocks * LANES
    pick = select_rows(ids_ref).astype(BF)
    rows[...] = jnp.zeros_like(rows)
    copies = []
    for d in range(n_dp):
        total = got_ref[d * half * size : (d * half + 1) * size, :].astype(F32)
        for h in range(1, half):
            base = (d * half + h) * size
            total = total + got_ref[base : base + size, :].astype(F32)
        for q in range(blocks):
            rows[0:cap, q * LANES : (q + 1) * LANES] = total[q * cap : (q + 1) * cap, :]
        cols = slice(d * width, (d + 1) * width)
        out[:, cols] = dot_tn(pick, rows[...].astype(BF)).astype(out.dtype)
        copies.append(pltpu.make_async_copy(out.at[:, cols], out_hbm.at[:, cols], sems.at[d]))
        copies[-1].start()
    for copy in copies:
        copy.wait()


def fast_shards(n_dp, n_expert, cap, tokens, expert_ids, gate_values, w_gate, w_up, w_down, target):
    tok_rows, features = tokens.shape
    width, hid = w_gate.shape
    half = n_expert // 2
    blocks = width // LANES
    peers = n_dp * half
    sources = 2 * peers
    rows = cap * sources
    unit = -(-(blocks + 2 + GATE_PIECES) * cap // 16) * 16
    dims = (n_dp, half, cap, blocks, unit)
    core = (lax.axis_index("expert") % 2).astype(jnp.int32).reshape(1)
    ids = expert_ids.T
    plane = [[2 * h + c for h in range(half)] for c in range(2)]
    slice_groups = [
        [d * n_expert + 2 * h + c for d in range(n_dp) for h in range(half)] for c in range(2)
    ]

    def other_core(x):
        return lax.ppermute(x, "expert", [(i, i ^ 1) for i in range(n_expert)])

    def other_dp(x):
        return lax.ppermute(x, "dp", [(0, 1), (1, 0)])

    def over_plane(x):
        return lax.all_to_all(x, "expert", 0, 0, axis_index_groups=plane, tiled=True)

    def over_slice(x):
        return lax.all_to_all(x, ("dp", "expert"), 0, 0, axis_index_groups=slice_groups, tiled=True)

    outgoing = call(
        functools.partial(route_kernel, dims),
        sds((peers * unit, LANES), BF),
        in_hbm(ids, gate_values.T, tokens, target),
        [HBM] * 4,
        [
            pltpu.VMEM(ids.shape, ids.dtype),
            pltpu.VMEM(ids.shape, F32),
            pltpu.VMEM(tokens.shape, tokens.dtype),
            pltpu.VMEM(target.shape, target.dtype),
            pltpu.VMEM((16, width), F32),
            pltpu.VMEM((16, width), F32),
            pltpu.VMEM((blocks * cap, LANES), F32),
            pltpu.VMEM((unit - blocks * cap, LANES), F32),
            pltpu.SemaphoreType.DMA((2 + 2 * n_dp,)),
        ],
        name="route",
    )
    first = -(-hid // (2 * LANES)) * LANES
    head = 2 * LANES

    def load(start, size, after=()):
        return call(
            functools.partial(load_kernel, start),
            (sds((8, LANES), F32), sds((width, size), w_gate.dtype), sds((width, size), w_up.dtype)),
            (*in_hbm(w_gate, w_up), *after),
            [HBM] * 2 + [VMEM] * len(after),
            [pltpu.SemaphoreType.DMA((-(-size // (2 * LANES)), 2))],
            flops=1_000_000_000,
            moved=8 * width * size,
            name="load_weights",
        )

    loaded, *weights = load(0, head)
    own, loaded = lax.optimization_barrier((over_slice(outgoing), loaded))
    loaded, *more = load(head, first - head, (loaded,))
    weights += more
    other = other_core(own)
    chunks = [(0, first), (first, hid - first)]
    last = len(chunks) - 1
    pres = []
    for start, size in chunks:
        outs = (sds((2, rows, size), F32), sds((2, rows, size), BF))
        cost = dict(flops=8 * rows * width * size, moved=4 * width * size)
        fetched = [
            pltpu.VMEM((width, size), w_gate.dtype),
            pltpu.VMEM((width, size), w_up.dtype),
            pltpu.SemaphoreType.DMA((-(-size // (2 * LANES)), 2)),
        ]
        if start == 0:
            all_rows, all_target, all_gates, *pre = call(
                functools.partial(first_pre_kernel, dims),
                (sds((rows, width), BF), sds((rows, LANES), F32), sds((rows, LANES), F32), *outs),
                (core, loaded, own, other, *weights),
                [SMEM] + [VMEM] * 7,
                [pltpu.VMEM((sources * unit, LANES), F32)],
                name="pre_activations",
                **cost,
            )
        else:
            turned, *pre = call(
                functools.partial(more_pre_kernel, start),
                (sds((width, rows), BF), *outs),
                (all_rows, *in_hbm(w_gate, w_up)),
                [VMEM] + [HBM] * 2,
                fetched,
                name="pre_activations",
                **cost,
            )
        pres.append((pre[0], other_dp(pre[1])))
    (start, size), (start_b, size_b) = chunks
    half_rows = half * rows
    cost = dict(flops=4 * rows * width * size, moved=2 * width * size)
    up_deriv, act, total = call(
        functools.partial(first_down_kernel, dims, start),
        (sds((rows, size), F32), sds((rows, size), F32), sds((2 * half_rows, LANES), F32)),
        (core, *pres[0], w_down),
        [SMEM] + [VMEM] * 3,
        [pltpu.VMEM((rows, size), BF)],
        name="down",
        **cost,
    )
    up_deriv_b, act_b, hidden_b, send = call(
        functools.partial(send_down_kernel, dims, start_b),
        (
            sds((rows, size_b), F32),
            sds((rows, size_b), F32),
            sds((rows, size_b), BF),
            sds((half_rows, LANES), BF),
        ),
        (core, *pres[1], w_down, total),
        [SMEM] + [VMEM] * 4,
        name="down_send",
        **cost,
    )
    sent = other_core(send)
    keep = call(
        functools.partial(keep_down_kernel, dims, start_b),
        sds((half_rows, LANES), F32),
        (core, hidden_b, w_down, total),
        [SMEM] + [VMEM] * 3,
        name="down_keep",
        **cost,
    )
    saved = [(up_deriv, act), (up_deriv_b, act_b)]
    chip_out = add_cores(keep, sent)
    cot = call(
        functools.partial(cotangent_kernel, half),
        sds((half * rows, LANES), BF),
        (over_plane(chip_out), all_gates, all_target),
        [VMEM] * 3,
        name="cotangent",
    )
    own = over_plane(cot)
    other = other_core(own)
    own_total = call(
        own_grad_hidden_kernel,
        sds((rows, hid), F32),
        (core, own, w_down),
        [SMEM] + [VMEM] * 2,
        [pltpu.VMEM((rows, width // 2), BF)],
        flops=2 * rows * width * hid,
        moved=2 * width * hid,
        name="grad_hidden_own",
    )
    grads = []
    for start, size in chunks:
        outs = (sds((rows, size), F32), sds((rows, size), BF))
        cost = dict(flops=2 * rows * width * size, moved=2 * width * size)
        if start == 0:
            cot, *grad = call(
                functools.partial(first_grad_hidden_kernel, start),
                (sds((rows, width // 2), BF), *outs),
                (core, other, w_down, own_total),
                [SMEM] + [VMEM] * 3,
                name="grad_hidden",
                **cost,
            )
        else:
            grad = call(
                functools.partial(more_grad_hidden_kernel, start),
                outs,
                (core, cot, w_down, own_total),
                [SMEM] + [VMEM] * 3,
                name="grad_hidden",
                **cost,
            )
        grads.append((grad[0], other_dp(grad[1])))
    pre_grads = []
    total = ()
    peer_rows = peers * blocks * cap
    for k, (start, size) in enumerate(chunks):
        outs, scratch = (sds((rows, width), F32),), []
        if k == last:
            outs = (sds((peer_rows, LANES), F32), sds((peer_rows, LANES), BF))
            scratch = [pltpu.VMEM((2 * peer_rows, LANES), F32)]
        gate_pre_grad, up_pre_grad, *total = call(
            functools.partial(row_grad_kernel, dims, start, k == last),
            (sds((rows, size), BF), sds((rows, size), BF), *outs),
            (core, *grads[k], *saved[k], w_gate, w_up, *total),
            [SMEM] + [VMEM] * (6 + len(total)),
            scratch,
            flops=8 * rows * width * size,
            moved=4 * width * size,
            name="row_grad",
        )
        pre_grads.append((gate_pre_grad, up_pre_grad))
    keep, send = total
    chip_rows = add_cores(keep, other_core(send))
    got_rows = over_slice(chip_rows)
    pre_grads = [pair[0] for pair in pre_grads] + [pair[1] for pair in pre_grads]
    tile = 256
    gate_grad, up_grad = call(
        functools.partial(weight_grad_kernel, len(chunks), tile),
        (sds((width, hid), BF), sds((width, hid), BF)),
        (turned, *pre_grads),
        [VMEM] * (1 + len(pre_grads)),
        [
            pltpu.VMEM((width, hid), BF),
            pltpu.VMEM((width, hid), BF),
            pltpu.SemaphoreType.DMA((width // tile, 2)),
        ],
        flops=4 * rows * width * hid,
        moved=4 * width * hid,
        out_spec=HBM,
        name="weight_grads",
    )
    token_grad = call(
        functools.partial(token_grad_kernel, dims),
        sds((tok_rows, features), tokens.dtype),
        (ids, got_rows),
        [VMEM] * 2,
        [
            pltpu.VMEM((16, width), F32),
            pltpu.VMEM((tok_rows, features), tokens.dtype),
            pltpu.SemaphoreType.DMA((n_dp,)),
        ],
        out_spec=HBM,
        name="token_grad",
    )
    return token_grad, gate_grad, up_grad


def contract_last(matrix_a, matrix_b):
    return lax.dot_general(
        matrix_a, matrix_b, (((1,), (1,)), ((), ())), preferred_element_type=jnp.float32
    )


def rounded_terms(column_blocks, grad_blocks):
    terms = jnp.einsum(
        "krd,krh->kdh", column_blocks, grad_blocks, preferred_element_type=jnp.float32
    )
    terms = lax.optimization_barrier(terms.astype(jnp.bfloat16))
    return jnp.sum(terms.astype(jnp.float32), axis=0)


def spread_rows(rows, group_size, capacity, features):
    flat = rows.reshape(EXPERTS, 1, capacity * features)
    wide = jnp.broadcast_to(flat, (EXPERTS, group_size, capacity * features))
    return wide.reshape(EXPERTS * group_size * capacity, features)


def fold_group(rows, group_size, capacity, features):
    shaped = rows.reshape(EXPERTS, group_size, capacity * features).astype(jnp.float32)
    return jnp.sum(shaped, axis=1).reshape(EXPERTS * capacity, features)


def general_shards(tokens, expert_ids, gate_values, w_gate, w_up, w_down, target):
    devices_along = lax.axis_size("expert")
    group_size = devices_along // EXPERTS
    tok_rows = tokens.shape[0]
    features = tokens.shape[1]
    hid_local = w_gate.shape[1]
    capacity = max(2, 3 * tok_rows // 128)
    slot_total = EXPERTS * capacity
    flat_ids = expert_ids.reshape(-1)
    pair_count = flat_ids.shape[0]
    window = flat_ids < EXPERTS
    onehot = (flat_ids[:, None] == jnp.arange(EXPERTS, dtype=jnp.int32)[None, :]).astype(jnp.int32)
    slot_index = jnp.sum((jnp.cumsum(onehot, axis=0) - onehot) * onehot, axis=1)
    position = jnp.where(window, flat_ids * capacity + slot_index, slot_total)
    owning = jnp.arange(pair_count, dtype=jnp.int32) // 2
    slot_token = jnp.zeros((slot_total + 1,), jnp.int32).at[position].set(owning)[:slot_total]
    slot_live = jnp.zeros((slot_total + 1,), jnp.bool_).at[position].set(True)[:slot_total]
    slot_gate = (
        jnp.zeros((slot_total + 1,), jnp.float32)
        .at[position]
        .set(gate_values.reshape(-1))[:slot_total]
    )
    safe_pairs = jnp.minimum(position, slot_total - 1).reshape(tok_rows, 2)
    live_pairs = window.reshape(tok_rows, 2)

    def pick(table, column):
        return jnp.where(live_pairs[:, column : column + 1], table[safe_pairs[:, column]], 0.0)

    outgoing = jnp.where(slot_live[:, None], tokens[slot_token], jnp.zeros((), tokens.dtype))
    outgoing = spread_rows(outgoing, group_size, capacity, features)
    received = lax.all_to_all(outgoing, "expert", split_axis=0, concat_axis=0, tiled=True)
    rows_count = received.shape[0]
    full_gate, full_up, full_down = (
        lax.all_gather(w_gate, "dp", axis=0, tiled=True),
        lax.all_gather(w_up, "dp", axis=0, tiled=True),
        lax.all_gather(w_down, "dp", axis=1, tiled=True),
    )
    gate_pre = jnp.dot(received, full_gate, preferred_element_type=jnp.float32)
    up_pre = jnp.dot(received, full_up, preferred_element_type=jnp.float32)
    sigmoid_gate = jax.nn.sigmoid(gate_pre)
    activated = sigmoid_gate * gate_pre
    hidden = (activated * up_pre).astype(jnp.bfloat16)
    partial_out = jnp.dot(hidden, full_down, preferred_element_type=jnp.float32).astype(
        jnp.bfloat16
    )
    returned_out = lax.all_to_all(partial_out, "expert", split_axis=0, concat_axis=0, tiled=True)
    expert_out = fold_group(returned_out, group_size, capacity, features)
    combined = gate_values[:, 0:1] * pick(expert_out, 0) + gate_values[:, 1:2] * pick(expert_out, 1)
    residual = combined - target.astype(jnp.float32)
    outgoing_grad = jnp.where(
        slot_live[:, None], slot_gate[:, None] * residual[slot_token], 0.0
    ).astype(jnp.bfloat16)
    outgoing_grad = spread_rows(outgoing_grad, group_size, capacity, features)
    cotangent = lax.all_to_all(outgoing_grad, "expert", split_axis=0, concat_axis=0, tiled=True)
    grad_hidden = contract_last(cotangent, full_down)
    derivative = sigmoid_gate * (1.0 + gate_pre * (1.0 - sigmoid_gate))
    grad_gate_pre = (grad_hidden * up_pre * derivative).astype(jnp.bfloat16)
    grad_up_pre = (grad_hidden * activated).astype(jnp.bfloat16)
    row_part = (
        contract_last(grad_gate_pre, full_gate) + contract_last(grad_up_pre, full_up)
    ).astype(jnp.bfloat16)
    back_rows = lax.all_to_all(row_part, "expert", split_axis=0, concat_axis=0, tiled=True)
    row_grad = fold_group(back_rows, group_size, capacity, features)
    token_grad = (pick(row_grad, 0) + pick(row_grad, 1)).astype(jnp.bfloat16)
    shard_columns = lax.all_to_all(received, "dp", split_axis=1, concat_axis=0, tiled=True)
    shard_width = shard_columns.shape[1]
    dp_count = lax.axis_size("dp")
    every_gate, every_up = (
        lax.all_gather(grad_gate_pre, "dp", axis=0, tiled=True),
        lax.all_gather(grad_up_pre, "dp", axis=0, tiled=True),
    )
    column_blocks = shard_columns.reshape(dp_count, rows_count, shard_width)
    gate_sum = rounded_terms(column_blocks, every_gate.reshape(dp_count, rows_count, hid_local))
    up_sum = rounded_terms(column_blocks, every_up.reshape(dp_count, rows_count, hid_local))
    return (token_grad, gate_sum.astype(jnp.bfloat16), up_sum.astype(jnp.bfloat16))


def solution(mesh):
    n_dp, n_expert = mesh.shape["dp"], mesh.shape["expert"]

    def shards(*args):
        tok_rows, features = args[0].shape
        width, hid = args[3].shape
        cap = max(2, 3 * tok_rows // 128)
        whole_blocks = (
            n_dp == 2
            and n_expert % 4 == 0
            and width == n_expert * LANES
            and hid % LANES == 0
            and hid > 4 * LANES
            and n_dp * n_expert % 16 == 0
            and cap <= 8
            and tok_rows % LANES == 0
        )
        if whole_blocks:
            return fast_shards(n_dp, n_expert, cap, *args)
        return general_shards(*args)

    placed = (
        P(("dp", "expert"), None),
        P(("dp", "expert"), None),
        P(("dp", "expert"), None),
        P("dp", "expert"),
        P("dp", "expert"),
        P("expert", "dp"),
        P(("dp", "expert"), None),
    )
    return jax.shard_map(
        shards,
        mesh=mesh,
        in_specs=placed,
        out_specs=(P(("dp", "expert"), None), P("dp", "expert"), P("dp", "expert")),
        check_vma=False,
    )
```

```python
import functools

import jax
import jax.numpy as jnp
from jax import lax
from jax.experimental import pallas as pl
from jax.experimental.pallas import tpu as pltpu
from jax.sharding import PartitionSpec as P

EXPERTS = 1
LANES = 128
GATE_PIECES = 3
BF = jnp.bfloat16
F32 = jnp.float32
VMEM = pl.BlockSpec(memory_space=pltpu.VMEM)
HBM = pl.BlockSpec(memory_space=pltpu.HBM)
SMEM = pl.BlockSpec(memory_space=pltpu.SMEM)


def sds(shape, dtype):
    return jax.ShapeDtypeStruct(shape, dtype)


def dot_nn(a, b):
    return lax.dot_general(a, b, (((1,), (0,)), ((), ())), preferred_element_type=F32)


def dot_nt(a, b):
    return lax.dot_general(a, b, (((1,), (1,)), ((), ())), preferred_element_type=F32)


def dot_tn(a, b):
    return lax.dot_general(a, b, (((0,), (0,)), ((), ())), preferred_element_type=F32)


def in_hbm(*arrays):
    return tuple(pltpu.with_memory_space_constraint(x, pltpu.HBM) for x in arrays)


def core_of(place_ref):
    return place_ref[0] & 1


def x_of(place_ref):
    return (place_ref[0] >> 1) & 1


def z_of(place_ref):
    return place_ref[0] >> 2


def call(body, outs, args, specs, scratch=(), limit=16, flops=0, moved=0, name=None, out_spec=VMEM):
    return pl.pallas_call(
        body,
        out_shape=outs,
        in_specs=specs,
        out_specs=jax.tree.map(lambda _: out_spec, outs),
        scratch_shapes=list(scratch),
        compiler_params=pltpu.CompilerParams(vmem_limit_bytes=limit << 20),
        cost_estimate=pl.CostEstimate(flops=flops, bytes_accessed=moved, transcendentals=0),
        name=name,
    )(*args)


def select_rows(ids_ref):
    tok_rows = ids_ref.shape[1]
    live = jnp.sum((ids_ref[...] < EXPERTS).astype(F32), axis=0, keepdims=True)
    before = lax.broadcasted_iota(jnp.int32, (tok_rows, tok_rows), 0)
    after = lax.broadcasted_iota(jnp.int32, (tok_rows, tok_rows), 1)
    earlier = (before < after).astype(BF)
    wide = jnp.broadcast_to(live, (16, tok_rows))
    slot = dot_nn(wide.astype(BF), earlier)
    wanted = lax.broadcasted_iota(jnp.int32, (16, tok_rows), 0).astype(F32)
    return jnp.where(slot == wanted, wide, 0.0)


def add_kernel(own_ref, got_ref, out_ref):
    out_ref[...] = (own_ref[...] + got_ref[...].astype(F32)).astype(out_ref.dtype)


def add_cores(own, got):
    return call(add_kernel, sds(got.shape, got.dtype), (own, got), [VMEM] * 2, name="add_cores")


def route_kernel(dims, ids_hbm, gates_hbm, tokens_hbm, target_hbm, out_ref, pick_ref,
                 ids_ref, gates_ref, tokens_ref, target_ref, tok, tgt, head, tail, sems):
    n_dp, half, cap, blocks, unit = dims
    width = blocks * LANES
    pairs = [(ids_hbm, ids_ref), (gates_hbm, gates_ref)]
    for hbm, ref in ((tokens_hbm, tokens_ref), (target_hbm, target_ref)):
        for d in range(n_dp):
            cols = slice(d * width, (d + 1) * width)
            pairs.append((hbm.at[:, cols], ref.at[:, cols]))
    copies = [pltpu.make_async_copy(src, dst, sems.at[i]) for i, (src, dst) in enumerate(pairs)]
    for copy in copies:
        copy.start()
    tail[...] = jnp.zeros_like(tail)
    copies[0].wait()
    copies[1].wait()
    chosen = select_rows(ids_ref)
    live_gates = jnp.sum(jnp.where(ids_ref[...] < EXPERTS, gates_ref[...], 0.0), axis=0, keepdims=True)
    gate = jnp.sum(chosen * live_gates, axis=1, keepdims=True)
    pick = chosen.astype(BF)
    pick_ref[...] = pick
    rest = gate
    for piece in range(GATE_PIECES):
        part = rest.astype(BF).astype(F32)
        rest = rest - part
        at = (2 + piece) * cap
        tail[at : at + cap, :] = jnp.broadcast_to(part[0:cap], (cap, LANES))
    lead = blocks * cap
    for d in range(n_dp):
        cols = slice(d * width, (d + 1) * width)
        copies[2 + d].wait()
        tok[...] = dot_nn(pick, tokens_ref[:, cols])
        for q in range(blocks):
            head[q * cap : (q + 1) * cap, :] = tok[0:cap, q * LANES : (q + 1) * LANES]
        packed = head[...].astype(BF)
        for h in range(half):
            base = (d * half + h) * unit
            out_ref[base : base + lead, :] = packed
    for d in range(n_dp):
        cols = slice(d * width, (d + 1) * width)
        copies[2 + n_dp + d].wait()
        tgt[...] = dot_nn(pick, target_ref[:, cols])
        for h in range(half):
            for core in range(2):
                lo = (core * half + h % 2 * (half // 2) + h // 2) * LANES
                tail[core * cap : (core + 1) * cap, :] = tgt[0:cap, lo : lo + LANES]
            base = (d * half + h) * unit
            out_ref[base + lead : base + unit, :] = tail[...].astype(BF)


def both_cores(place_ref, own_ref, other_ref, wide):
    size = own_ref.shape[0]
    core = core_of(place_ref)
    wide[pl.ds(pl.multiple_of(core * size, size), size), :] = own_ref[...].astype(wide.dtype)
    wide[pl.ds(pl.multiple_of((1 - core) * size, size), size), :] = other_ref[...].astype(wide.dtype)


def fetch_columns(starts, gate_hbm, up_hbm, gate_w, up_w, sems):
    lo, hi = starts
    copies = []
    for k, at in enumerate(range(lo, hi, 2 * LANES)):
        count = min(2 * LANES, hi - at)
        pair = []
        for side, (src, dst) in enumerate(((gate_hbm, gate_w), (up_hbm, up_w))):
            part = src.at[:, pl.ds(at, count)]
            pair.append(pltpu.make_async_copy(part, dst.at[:, pl.ds(at - lo, count)], sems.at[k, side]))
            pair[-1].start()
        copies.append(pair)
    return copies


def load_kernel(start, gate_hbm, up_hbm, *refs):
    done_ref, gate_w, up_w, sems = refs[-4:]
    stop = start + gate_w.shape[1]
    copies = fetch_columns((start, stop), gate_hbm, up_hbm, gate_w, up_w, sems)
    done_ref[...] = jnp.zeros_like(done_ref)
    for pair in copies:
        for copy in pair:
            copy.wait()


def partial_pre(rows_ref, gate_w, up_w, copies, first, own_pre, send_pre):
    for j in range(gate_w.shape[1] // LANES):
        if copies and j % 2 == 0:
            for copy in copies[j // 2]:
                copy.wait()
        here = slice(j * LANES, (j + 1) * LANES)
        cols = slice(first + j * LANES, first + (j + 1) * LANES)
        pair = jnp.concatenate([gate_w[:, here], up_w[:, here]], axis=1)
        both = dot_nn(rows_ref[...], pair)
        for side in range(2):
            value = both[:, side * LANES : (side + 1) * LANES]
            own_pre[side, :, cols] = value
            send_pre[side, :, cols] = value.astype(BF)


def first_pre_kernel(dims, place_ref, loaded_ref, own_ref, other_ref, gate_head, up_head, gate_rest, up_rest,
                     rows_ref, target_ref, gates_ref, own_pre, send_pre, wide):
    n_dp, half, cap, blocks, unit = dims
    sources = 2 * n_dp * half
    both_cores(place_ref, own_ref, other_ref, wide)
    core = core_of(place_ref)

    def one(k):
        return wide[pl.ds(k, sources, stride=unit), :]

    for c in range(cap):
        rows = slice(c * sources, (c + 1) * sources)
        for q in range(blocks):
            rows_ref[rows, q * LANES : (q + 1) * LANES] = one(q * cap + c).astype(BF)
        base = blocks * cap
        target_ref[rows, :] = jnp.where(core == 0, one(base + c), one(base + cap + c))
        gates_ref[rows, :] = sum(one(base + (2 + piece) * cap + c) for piece in range(GATE_PIECES))
    partial_pre(rows_ref, gate_head, up_head, (), 0, own_pre, send_pre)
    partial_pre(rows_ref, gate_rest, up_rest, (), gate_head.shape[1], own_pre, send_pre)


def more_pre_kernel(start, rows_ref, gate_hbm, up_hbm, turned_ref, own_pre, send_pre, gate_w, up_w, sems):
    copies = fetch_columns((start, start + own_pre.shape[2]), gate_hbm, up_hbm, gate_w, up_w, sems)
    turned_ref[...] = rows_ref[...].T
    partial_pre(rows_ref, gate_w, up_w, copies, 0, own_pre, send_pre)


def down_side(dims, start, place_ref, hidden, down_w, total_ref, side, out_ref):
    n_dp, half, cap, blocks, unit = dims
    rows, hid = hidden.shape
    quarter = half // 2
    core = jnp.where(side == 0, core_of(place_ref), 1 - core_of(place_ref))
    for k in range(2):
        x = x_of(place_ref) if k == 0 else 1 - x_of(place_ref)
        for j in range(0, quarter, 2):
            lo = (core * half + x * quarter + j) * LANES
            cols = pl.ds(pl.multiple_of(lo, 2 * LANES), 2 * LANES)
            value = dot_nn(hidden[...], down_w[start : start + hid, cols])
            for n in range(2):
                part = value[:, n * LANES : (n + 1) * LANES]
                block = k * quarter + j + n
                if total_ref is not None:
                    both = side * half + block
                    part = part + total_ref[both * rows : (both + 1) * rows, :]
                out_ref[block * rows : (block + 1) * rows, :] = part.astype(out_ref.dtype)


def activate(own_ref, got_ref, up_deriv, act_ref, hidden):
    gate_pre = own_ref[0] + got_ref[0].astype(F32)
    up_pre = own_ref[1] + got_ref[1].astype(F32)
    sig = jax.nn.sigmoid(gate_pre)
    act = sig * gate_pre
    act_ref[...] = act
    up_deriv[...] = up_pre * (sig * (1.0 + gate_pre * (1.0 - sig)))
    hidden[...] = (act * up_pre).astype(BF)


def first_down_kernel(dims, start, place_ref, own_ref, got_ref, down_w, up_deriv, act_ref, total_ref, hidden):
    activate(own_ref, got_ref, up_deriv, act_ref, hidden)
    size = dims[1] * hidden.shape[0]
    for side in range(2):
        part = total_ref.at[side * size : (side + 1) * size]
        down_side(dims, start, place_ref, hidden, down_w, None, side, part)


def send_down_kernel(dims, start, place_ref, own_ref, got_ref, down_w, total_ref, up_deriv, act_ref, hidden, send_ref):
    activate(own_ref, got_ref, up_deriv, act_ref, hidden)
    down_side(dims, start, place_ref, hidden, down_w, total_ref, 1, send_ref)


def keep_down_kernel(dims, start, place_ref, hidden, down_w, total_ref, keep_ref):
    down_side(dims, start, place_ref, hidden, down_w, total_ref, 0, keep_ref)


def chip_sum_kernel(own_ref, got_ref, keep_ref, send_ref):
    size = keep_ref.shape[0]
    keep_ref[...] = own_ref[0:size, :] + got_ref[0:size, :].astype(F32)
    send_ref[...] = (own_ref[size : 2 * size, :] + got_ref[size : 2 * size, :].astype(F32)).astype(BF)


def residual_kernel(place_ref, own_ref, got_ref, gates_ref, target_ref, keep_ref, send_ref):
    rows = target_ref.shape[0]
    for z in range(own_ref.shape[0] // rows):
        at = slice(z * rows, (z + 1) * rows)
        value = gates_ref[...] * (own_ref[at, :] + got_ref[at, :].astype(F32))
        value = jnp.where(z_of(place_ref) == z, value - target_ref[...], value)
        keep_ref[at, :] = value
        send_ref[at, :] = value.astype(BF)


def line_sum_kernel(own_ref, got_ref, keep_ref, send_ref):
    value = own_ref[...] + got_ref[...].astype(F32)
    keep_ref[...] = value
    send_ref[...] = value.astype(BF)


def cotangent_kernel(own_ref, got_ref, gates_ref, out_ref):
    rows = gates_ref.shape[0]
    for z in range(own_ref.shape[0] // rows):
        at = slice(z * rows, (z + 1) * rows)
        out_ref[at, :] = (gates_ref[...] * (own_ref[at, :] + got_ref[at, :].astype(F32))).astype(BF)


def gather_blocks(ref, out):
    rows = out.shape[0]
    for h in range(out.shape[1] // LANES):
        out[:, h * LANES : (h + 1) * LANES] = ref[h * rows : (h + 1) * rows, :]


def quarter_grad_hidden(cot, core, x, down_w, start, total_ref, outs):
    width = cot.shape[1]
    cols = pl.ds(pl.multiple_of((2 * core + x) * width, width), width)
    size = outs[0].shape[1]
    for lo in range(0, size, 2 * LANES):
        here = slice(lo, min(lo + 2 * LANES, size))
        there = slice(start + here.start, start + here.stop)
        value = dot_nt(cot[...], down_w[there, cols])
        if total_ref is not None:
            value = value + total_ref[:, there]
        for out in outs:
            out[:, here] = value.astype(out.dtype)


def near_grad_hidden_kernel(flips, place_ref, got_ref, down_w, *refs):
    *total_ref, out_ref, cot = refs
    core = 1 - core_of(place_ref) if flips[0] else core_of(place_ref)
    x = 1 - x_of(place_ref) if flips[1] else x_of(place_ref)
    gather_blocks(got_ref, cot)
    quarter_grad_hidden(cot, core, x, down_w, 0, total_ref[0] if total_ref else None, (out_ref,))


def first_grad_hidden_kernel(start, place_ref, got_ref, down_w, total_ref, cot, own_out, send_out):
    gather_blocks(got_ref, cot)
    quarter_grad_hidden(cot, 1 - core_of(place_ref), 1 - x_of(place_ref), down_w, start, total_ref, (own_out, send_out))


def more_grad_hidden_kernel(start, place_ref, cot, down_w, total_ref, own_out, send_out):
    quarter_grad_hidden(cot, 1 - core_of(place_ref), 1 - x_of(place_ref), down_w, start, total_ref, (own_out, send_out))


def row_grad_kernel(dims, start, last, place_ref, own_ref, got_ref, up_deriv, act_ref, gate_w, up_w, *refs):
    n_dp, half, cap, blocks, unit = dims
    sources = 2 * n_dp * half
    refs = list(refs)
    total_ref = refs.pop(0) if start > 0 else None
    gate_out, up_out, *out_refs = refs
    grad_hidden = own_ref[...] + got_ref[...].astype(F32)
    gate_out[...] = (grad_hidden * up_deriv[...]).astype(BF)
    up_out[...] = (grad_hidden * act_ref[...]).astype(BF)
    hid = gate_out.shape[1]
    wide = out_refs[-1]

    def column(j, _):
        at = pl.ds(pl.multiple_of(j * 2 * LANES, 2 * LANES), 2 * LANES)
        value = dot_nt(gate_out[...], gate_w[at, start : start + hid])
        value = value + dot_nt(up_out[...], up_w[at, start : start + hid])
        if total_ref is not None:
            value = value + total_ref[:, at]
        if not last:
            wide[:, at] = value
            return 0
        for k in range(2):
            for c in range(cap):
                piece = value[c * sources : (c + 1) * sources, k * LANES : (k + 1) * LANES]
                wide[pl.ds((2 * j + k) * cap + c, sources, stride=blocks * cap), :] = piece
        return 0

    lax.fori_loop(0, blocks // 2, column, 0, unroll=True)
    if last:
        keep_ref, send_ref, _ = out_refs
        size = keep_ref.shape[0]
        core = core_of(place_ref)
        keep_ref[...] = wide[pl.ds(pl.multiple_of(core * size, size), size), :]
        send_ref[...] = wide[pl.ds(pl.multiple_of((1 - core) * size, size), size), :].astype(BF)


def weight_grad_kernel(parts, tile, turned_ref, *refs):
    grads = (refs[:parts], refs[parts : 2 * parts])
    outs, values, sems = refs[2 * parts : 2 * parts + 2], refs[2 * parts + 2 : 2 * parts + 4], refs[-1]
    copies = []
    for t in range(turned_ref.shape[0] // tile):
        at = slice(t * tile, (t + 1) * tile)
        for side in range(2):
            lo = 0
            for ref in grads[side]:
                size = ref.shape[1]
                values[side][at, lo : lo + size] = dot_nn(turned_ref[at, :], ref[...]).astype(BF)
                lo += size
            copies.append(pltpu.make_async_copy(values[side].at[at, :], outs[side].at[at, :], sems.at[t, side]))
            copies[-1].start()
    for copy in copies:
        copy.wait()


def token_grad_kernel(dims, pick_ref, got_ref, out_hbm, rows, out, sems):
    n_dp, half, cap, blocks, unit = dims
    size = blocks * cap
    width = blocks * LANES
    pick = pick_ref[...]
    rows[...] = jnp.zeros_like(rows)
    copies = []
    for d in range(n_dp):
        total = got_ref[d * half * size : (d * half + 1) * size, :].astype(F32)
        for h in range(1, half):
            base = (d * half + h) * size
            total = total + got_ref[base : base + size, :].astype(F32)
        for q in range(blocks):
            rows[0:cap, q * LANES : (q + 1) * LANES] = total[q * cap : (q + 1) * cap, :]
        cols = slice(d * width, (d + 1) * width)
        out[:, cols] = dot_tn(pick, rows[...].astype(BF)).astype(out.dtype)
        copies.append(pltpu.make_async_copy(out.at[:, cols], out_hbm.at[:, cols], sems.at[d]))
        copies[-1].start()
    for copy in copies:
        copy.wait()


def fast_shards(n_dp, n_expert, cap, tokens, expert_ids, gate_values, w_gate, w_up, w_down, target):
    tok_rows, features = tokens.shape
    width, hid = w_gate.shape
    half = n_expert // 2
    blocks = width // LANES
    peers = n_dp * half
    sources = 2 * peers
    rows = cap * sources
    unit = -(-(blocks + 2 + GATE_PIECES) * cap // 16) * 16
    dims = (n_dp, half, cap, blocks, unit)
    place = lax.axis_index("expert").astype(jnp.int32).reshape(1)
    ids = expert_ids.T
    slice_groups = [
        [d * n_expert + 2 * h + c for d in range(n_dp) for h in range(half)] for c in range(2)
    ]

    def other(x, mask):
        return lax.ppermute(x, "expert", [(i, i ^ mask) for i in range(n_expert)])

    def other_core(x):
        return other(x, 1)

    def other_dp(x):
        return lax.ppermute(x, "dp", [(0, 1), (1, 0)])

    def over_slice(x):
        return lax.all_to_all(x, ("dp", "expert"), 0, 0, axis_index_groups=slice_groups, tiled=True)

    outgoing, pick = call(
        functools.partial(route_kernel, dims),
        (sds((peers * unit, LANES), BF), sds((16, tok_rows), BF)),
        in_hbm(ids, gate_values.T, tokens, target),
        [HBM] * 4,
        [
            pltpu.VMEM(ids.shape, ids.dtype),
            pltpu.VMEM(ids.shape, F32),
            pltpu.VMEM(tokens.shape, tokens.dtype),
            pltpu.VMEM(target.shape, target.dtype),
            pltpu.VMEM((16, width), F32),
            pltpu.VMEM((16, width), F32),
            pltpu.VMEM((blocks * cap, LANES), F32),
            pltpu.VMEM((unit - blocks * cap, LANES), F32),
            pltpu.SemaphoreType.DMA((2 + 2 * n_dp,)),
        ],
        name="route",
    )
    first = -(-hid // (2 * LANES)) * LANES
    head = 2 * LANES

    def load(start, size, after=()):
        return call(
            functools.partial(load_kernel, start),
            (sds((8, LANES), F32), sds((width, size), w_gate.dtype), sds((width, size), w_up.dtype)),
            (*in_hbm(w_gate, w_up), *after),
            [HBM] * 2 + [VMEM] * len(after),
            [pltpu.SemaphoreType.DMA((-(-size // (2 * LANES)), 2))],
            flops=1_000_000_000,
            moved=8 * width * size,
            name="load_weights",
        )

    loaded, *weights = load(0, head)
    own, loaded = lax.optimization_barrier((over_slice(outgoing), loaded))
    loaded, *more = load(head, first - head, (loaded,))
    weights += more
    near = other_core(own)
    chunks = [(0, first), (first, hid - first)]
    last = len(chunks) - 1
    pres = []
    for start, size in chunks:
        outs = (sds((2, rows, size), F32), sds((2, rows, size), BF))
        cost = dict(flops=8 * rows * width * size, moved=4 * width * size)
        fetched = [
            pltpu.VMEM((width, size), w_gate.dtype),
            pltpu.VMEM((width, size), w_up.dtype),
            pltpu.SemaphoreType.DMA((-(-size // (2 * LANES)), 2)),
        ]
        if start == 0:
            all_rows, all_target, all_gates, *pre = call(
                functools.partial(first_pre_kernel, dims),
                (sds((rows, width), BF), sds((rows, LANES), F32), sds((rows, LANES), F32), *outs),
                (place, loaded, own, near, *weights),
                [SMEM] + [VMEM] * 7,
                [pltpu.VMEM((sources * unit, LANES), F32)],
                name="pre_activations",
                **cost,
            )
        else:
            turned, *pre = call(
                functools.partial(more_pre_kernel, start),
                (sds((width, rows), BF), *outs),
                (all_rows, *in_hbm(w_gate, w_up)),
                [VMEM] + [HBM] * 2,
                fetched,
                name="pre_activations",
                **cost,
            )
        pres.append((pre[0], other_dp(pre[1])))
    (start, size), (start_b, size_b) = chunks
    half_rows = half * rows
    cost = dict(flops=4 * rows * width * size, moved=2 * width * size)
    up_deriv, act, total = call(
        functools.partial(first_down_kernel, dims, start),
        (sds((rows, size), F32), sds((rows, size), F32), sds((2 * half_rows, LANES), F32)),
        (place, *pres[0], w_down),
        [SMEM] + [VMEM] * 3,
        [pltpu.VMEM((rows, size), BF)],
        name="down",
        **cost,
    )
    up_deriv_b, act_b, hidden_b, send = call(
        functools.partial(send_down_kernel, dims, start_b),
        (
            sds((rows, size_b), F32),
            sds((rows, size_b), F32),
            sds((rows, size_b), BF),
            sds((half_rows, LANES), BF),
        ),
        (place, *pres[1], w_down, total),
        [SMEM] + [VMEM] * 4,
        name="down_send",
        **cost,
    )
    sent = other_core(send)
    keep = call(
        functools.partial(keep_down_kernel, dims, start_b),
        sds((half_rows, LANES), F32),
        (place, hidden_b, w_down, total),
        [SMEM] + [VMEM] * 3,
        name="down_keep",
        **cost,
    )
    saved = [(up_deriv, act), (up_deriv_b, act_b)]
    quarter_rows = half_rows // 2
    pair = (sds((quarter_rows, LANES), F32), sds((quarter_rows, LANES), BF))
    keep, send = call(chip_sum_kernel, pair, (keep, sent), [VMEM] * 2, name="chip_sum")
    keep, send = call(
        residual_kernel,
        pair,
        (place, keep, other(send, 2), all_gates, all_target),
        [SMEM] + [VMEM] * 4,
        name="residual",
    )
    step = 4
    while 2 * step < n_expert:
        keep, send = call(line_sum_kernel, pair, (keep, other(send, step)), [VMEM] * 2, name="line_sum")
        step *= 2
    cot = call(
        cotangent_kernel,
        pair[1],
        (keep, other(send, step), all_gates),
        [VMEM] * 3,
        name="cotangent",
    )
    from_x = other(cot, 2)
    from_core = other_core(cot)
    own_total = ()
    for flips in ((0, 0), (1, 0), (0, 1)):
        got = from_x if flips[1] else from_core if flips[0] else cot
        own_total = (
            call(
                functools.partial(near_grad_hidden_kernel, flips),
                sds((rows, hid), F32),
                (place, got, w_down, *own_total),
                [SMEM] + [VMEM] * (2 + len(own_total)),
                [pltpu.VMEM((rows, width // 4), BF)],
                flops=rows * width * hid,
                moved=width * hid,
                name="grad_hidden_near",
            ),
        )
        if flips[0]:
            from_x, own_total = lax.optimization_barrier((from_x, own_total))
            from_both = other_core(from_x)
    own_total = own_total[0]
    grads = []
    for start, size in chunks:
        outs = (sds((rows, size), F32), sds((rows, size), BF))
        cost = dict(flops=2 * rows * width * size, moved=2 * width * size)
        if start == 0:
            cot, *grad = call(
                functools.partial(first_grad_hidden_kernel, start),
                (sds((rows, width // 4), BF), *outs),
                (place, from_both, w_down, own_total),
                [SMEM] + [VMEM] * 3,
                name="grad_hidden",
                **cost,
            )
        else:
            grad = call(
                functools.partial(more_grad_hidden_kernel, start),
                outs,
                (place, cot, w_down, own_total),
                [SMEM] + [VMEM] * 3,
                name="grad_hidden",
                **cost,
            )
        grads.append((grad[0], other_dp(grad[1])))
    pre_grads = []
    total = ()
    peer_rows = peers * blocks * cap
    for k, (start, size) in enumerate(chunks):
        outs, scratch = (sds((rows, width), F32),), []
        if k == last:
            outs = (sds((peer_rows, LANES), F32), sds((peer_rows, LANES), BF))
            scratch = [pltpu.VMEM((2 * peer_rows, LANES), F32)]
        gate_pre_grad, up_pre_grad, *total = call(
            functools.partial(row_grad_kernel, dims, start, k == last),
            (sds((rows, size), BF), sds((rows, size), BF), *outs),
            (place, *grads[k], *saved[k], w_gate, w_up, *total),
            [SMEM] + [VMEM] * (6 + len(total)),
            scratch,
            flops=8 * rows * width * size,
            moved=4 * width * size,
            name="row_grad",
        )
        pre_grads.append((gate_pre_grad, up_pre_grad))
    keep, send = total
    chip_rows = add_cores(keep, other_core(send))
    got_rows = over_slice(chip_rows)
    pre_grads = [pair[0] for pair in pre_grads] + [pair[1] for pair in pre_grads]
    tile = 256
    gate_grad, up_grad = call(
        functools.partial(weight_grad_kernel, len(chunks), tile),
        (sds((width, hid), BF), sds((width, hid), BF)),
        (turned, *pre_grads),
        [VMEM] * (1 + len(pre_grads)),
        [
            pltpu.VMEM((width, hid), BF),
            pltpu.VMEM((width, hid), BF),
            pltpu.SemaphoreType.DMA((width // tile, 2)),
        ],
        flops=4 * rows * width * hid,
        moved=4 * width * hid,
        out_spec=HBM,
        name="weight_grads",
    )
    token_grad = call(
        functools.partial(token_grad_kernel, dims),
        sds((tok_rows, features), tokens.dtype),
        (pick, got_rows),
        [VMEM] * 2,
        [
            pltpu.VMEM((16, width), F32),
            pltpu.VMEM((tok_rows, features), tokens.dtype),
            pltpu.SemaphoreType.DMA((n_dp,)),
        ],
        out_spec=HBM,
        name="token_grad",
    )
    return token_grad, gate_grad, up_grad


def contract_last(matrix_a, matrix_b):
    return lax.dot_general(
        matrix_a, matrix_b, (((1,), (1,)), ((), ())), preferred_element_type=jnp.float32
    )


def rounded_terms(column_blocks, grad_blocks):
    terms = jnp.einsum(
        "krd,krh->kdh", column_blocks, grad_blocks, preferred_element_type=jnp.float32
    )
    terms = lax.optimization_barrier(terms.astype(jnp.bfloat16))
    return jnp.sum(terms.astype(jnp.float32), axis=0)


def spread_rows(rows, group_size, capacity, features):
    flat = rows.reshape(EXPERTS, 1, capacity * features)
    wide = jnp.broadcast_to(flat, (EXPERTS, group_size, capacity * features))
    return wide.reshape(EXPERTS * group_size * capacity, features)


def fold_group(rows, group_size, capacity, features):
    shaped = rows.reshape(EXPERTS, group_size, capacity * features).astype(jnp.float32)
    return jnp.sum(shaped, axis=1).reshape(EXPERTS * capacity, features)


def general_shards(tokens, expert_ids, gate_values, w_gate, w_up, w_down, target):
    devices_along = lax.axis_size("expert")
    group_size = devices_along // EXPERTS
    tok_rows = tokens.shape[0]
    features = tokens.shape[1]
    hid_local = w_gate.shape[1]
    capacity = max(2, 3 * tok_rows // 128)
    slot_total = EXPERTS * capacity
    flat_ids = expert_ids.reshape(-1)
    pair_count = flat_ids.shape[0]
    window = flat_ids < EXPERTS
    onehot = (flat_ids[:, None] == jnp.arange(EXPERTS, dtype=jnp.int32)[None, :]).astype(jnp.int32)
    slot_index = jnp.sum((jnp.cumsum(onehot, axis=0) - onehot) * onehot, axis=1)
    position = jnp.where(window, flat_ids * capacity + slot_index, slot_total)
    owning = jnp.arange(pair_count, dtype=jnp.int32) // 2
    slot_token = jnp.zeros((slot_total + 1,), jnp.int32).at[position].set(owning)[:slot_total]
    slot_live = jnp.zeros((slot_total + 1,), jnp.bool_).at[position].set(True)[:slot_total]
    slot_gate = (
        jnp.zeros((slot_total + 1,), jnp.float32)
        .at[position]
        .set(gate_values.reshape(-1))[:slot_total]
    )
    safe_pairs = jnp.minimum(position, slot_total - 1).reshape(tok_rows, 2)
    live_pairs = window.reshape(tok_rows, 2)

    def pick(table, column):
        return jnp.where(live_pairs[:, column : column + 1], table[safe_pairs[:, column]], 0.0)

    outgoing = jnp.where(slot_live[:, None], tokens[slot_token], jnp.zeros((), tokens.dtype))
    outgoing = spread_rows(outgoing, group_size, capacity, features)
    received = lax.all_to_all(outgoing, "expert", split_axis=0, concat_axis=0, tiled=True)
    rows_count = received.shape[0]
    full_gate, full_up, full_down = (
        lax.all_gather(w_gate, "dp", axis=0, tiled=True),
        lax.all_gather(w_up, "dp", axis=0, tiled=True),
        lax.all_gather(w_down, "dp", axis=1, tiled=True),
    )
    gate_pre = jnp.dot(received, full_gate, preferred_element_type=jnp.float32)
    up_pre = jnp.dot(received, full_up, preferred_element_type=jnp.float32)
    sigmoid_gate = jax.nn.sigmoid(gate_pre)
    activated = sigmoid_gate * gate_pre
    hidden = (activated * up_pre).astype(jnp.bfloat16)
    partial_out = jnp.dot(hidden, full_down, preferred_element_type=jnp.float32).astype(
        jnp.bfloat16
    )
    returned_out = lax.all_to_all(partial_out, "expert", split_axis=0, concat_axis=0, tiled=True)
    expert_out = fold_group(returned_out, group_size, capacity, features)
    combined = gate_values[:, 0:1] * pick(expert_out, 0) + gate_values[:, 1:2] * pick(expert_out, 1)
    residual = combined - target.astype(jnp.float32)
    outgoing_grad = jnp.where(
        slot_live[:, None], slot_gate[:, None] * residual[slot_token], 0.0
    ).astype(jnp.bfloat16)
    outgoing_grad = spread_rows(outgoing_grad, group_size, capacity, features)
    cotangent = lax.all_to_all(outgoing_grad, "expert", split_axis=0, concat_axis=0, tiled=True)
    grad_hidden = contract_last(cotangent, full_down)
    derivative = sigmoid_gate * (1.0 + gate_pre * (1.0 - sigmoid_gate))
    grad_gate_pre = (grad_hidden * up_pre * derivative).astype(jnp.bfloat16)
    grad_up_pre = (grad_hidden * activated).astype(jnp.bfloat16)
    row_part = (
        contract_last(grad_gate_pre, full_gate) + contract_last(grad_up_pre, full_up)
    ).astype(jnp.bfloat16)
    back_rows = lax.all_to_all(row_part, "expert", split_axis=0, concat_axis=0, tiled=True)
    row_grad = fold_group(back_rows, group_size, capacity, features)
    token_grad = (pick(row_grad, 0) + pick(row_grad, 1)).astype(jnp.bfloat16)
    shard_columns = lax.all_to_all(received, "dp", split_axis=1, concat_axis=0, tiled=True)
    shard_width = shard_columns.shape[1]
    dp_count = lax.axis_size("dp")
    every_gate, every_up = (
        lax.all_gather(grad_gate_pre, "dp", axis=0, tiled=True),
        lax.all_gather(grad_up_pre, "dp", axis=0, tiled=True),
    )
    column_blocks = shard_columns.reshape(dp_count, rows_count, shard_width)
    gate_sum = rounded_terms(column_blocks, every_gate.reshape(dp_count, rows_count, hid_local))
    up_sum = rounded_terms(column_blocks, every_up.reshape(dp_count, rows_count, hid_local))
    return (token_grad, gate_sum.astype(jnp.bfloat16), up_sum.astype(jnp.bfloat16))


def solution(mesh):
    n_dp, n_expert = mesh.shape["dp"], mesh.shape["expert"]

    def shards(*args):
        tok_rows, features = args[0].shape
        width, hid = args[3].shape
        cap = max(2, 3 * tok_rows // 128)
        whole_blocks = (
            n_dp == 2
            and n_expert % 16 == 0
            and n_expert & (n_expert - 1) == 0
            and width == n_expert * LANES
            and hid % LANES == 0
            and hid > 4 * LANES
            and cap <= 8
            and tok_rows % LANES == 0
        )
        if whole_blocks:
            return fast_shards(n_dp, n_expert, cap, *args)
        return general_shards(*args)

    placed = (
        P(("dp", "expert"), None),
        P(("dp", "expert"), None),
        P(("dp", "expert"), None),
        P("dp", "expert"),
        P("dp", "expert"),
        P("expert", "dp"),
        P(("dp", "expert"), None),
    )
    return jax.shard_map(
        shards,
        mesh=mesh,
        in_specs=placed,
        out_specs=(P(("dp", "expert"), None), P("dp", "expert"), P("dp", "expert")),
        check_vma=False,
    )
```

```python
import functools

import jax
import jax.numpy as jnp
from jax import lax
from jax.experimental import pallas as pl
from jax.experimental.pallas import tpu as pltpu
from jax.sharding import PartitionSpec as P

EXPERTS = 1
LANES = 128
GATE_PIECES = 3
BF = jnp.bfloat16
F32 = jnp.float32
VMEM = pl.BlockSpec(memory_space=pltpu.VMEM)
HBM = pl.BlockSpec(memory_space=pltpu.HBM)
SMEM = pl.BlockSpec(memory_space=pltpu.SMEM)


def sds(shape, dtype):
    return jax.ShapeDtypeStruct(shape, dtype)


def dot_nn(a, b):
    return lax.dot_general(a, b, (((1,), (0,)), ((), ())), preferred_element_type=F32)


def dot_nt(a, b):
    return lax.dot_general(a, b, (((1,), (1,)), ((), ())), preferred_element_type=F32)


def dot_tn(a, b):
    return lax.dot_general(a, b, (((0,), (0,)), ((), ())), preferred_element_type=F32)


def in_hbm(*arrays):
    return tuple(pltpu.with_memory_space_constraint(x, pltpu.HBM) for x in arrays)


def core_of(place_ref):
    return place_ref[0] & 1


def quad_of(place_ref, k=0):
    x, low = (place_ref[0] >> 1) & 1, (place_ref[0] >> 2) & 1
    return (1 - x if k & 1 else x) + 2 * (1 - low if k & 2 else low)


def rest_of(place_ref):
    return place_ref[0] >> 3


def call(body, outs, args, specs, scratch=(), limit=16, flops=0, moved=0, name=None, out_spec=VMEM):
    return pl.pallas_call(
        body,
        out_shape=outs,
        in_specs=specs,
        out_specs=jax.tree.map(lambda _: out_spec, outs),
        scratch_shapes=list(scratch),
        compiler_params=pltpu.CompilerParams(vmem_limit_bytes=limit << 20),
        cost_estimate=pl.CostEstimate(flops=flops, bytes_accessed=moved, transcendentals=0),
        name=name,
    )(*args)


def select_rows(ids_ref):
    tok_rows = ids_ref.shape[1]
    live = jnp.sum((ids_ref[...] < EXPERTS).astype(F32), axis=0, keepdims=True)
    before = lax.broadcasted_iota(jnp.int32, (tok_rows, tok_rows), 0)
    after = lax.broadcasted_iota(jnp.int32, (tok_rows, tok_rows), 1)
    earlier = (before < after).astype(BF)
    wide = jnp.broadcast_to(live, (16, tok_rows))
    slot = dot_nn(wide.astype(BF), earlier)
    wanted = lax.broadcasted_iota(jnp.int32, (16, tok_rows), 0).astype(F32)
    return jnp.where(slot == wanted, wide, 0.0)


def add_kernel(own_ref, got_ref, out_ref):
    out_ref[...] = (own_ref[...] + got_ref[...].astype(F32)).astype(out_ref.dtype)


def add_cores(own, got):
    return call(add_kernel, sds(got.shape, got.dtype), (own, got), [VMEM] * 2, name="add_cores")


def route_kernel(dims, ids_hbm, gates_hbm, tokens_hbm, target_hbm, out_ref, pick_ref,
                 ids_ref, gates_ref, tokens_ref, target_ref, tok, tgt, head, tail, sems):
    n_dp, half, cap, blocks, unit = dims
    width = blocks * LANES
    pairs = [(ids_hbm, ids_ref), (gates_hbm, gates_ref)]
    for hbm, ref in ((tokens_hbm, tokens_ref), (target_hbm, target_ref)):
        for d in range(n_dp):
            cols = slice(d * width, (d + 1) * width)
            pairs.append((hbm.at[:, cols], ref.at[:, cols]))
    copies = [pltpu.make_async_copy(src, dst, sems.at[i]) for i, (src, dst) in enumerate(pairs)]
    for copy in copies:
        copy.start()
    tail[...] = jnp.zeros_like(tail)
    copies[0].wait()
    copies[1].wait()
    chosen = select_rows(ids_ref)
    live_gates = jnp.sum(jnp.where(ids_ref[...] < EXPERTS, gates_ref[...], 0.0), axis=0, keepdims=True)
    gate = jnp.sum(chosen * live_gates, axis=1, keepdims=True)
    pick = chosen.astype(BF)
    pick_ref[...] = pick
    rest = gate
    for piece in range(GATE_PIECES):
        part = rest.astype(BF).astype(F32)
        rest = rest - part
        at = (2 + piece) * cap
        tail[at : at + cap, :] = jnp.broadcast_to(part[0:cap], (cap, LANES))
    lead = blocks * cap
    for d in range(n_dp):
        cols = slice(d * width, (d + 1) * width)
        copies[2 + d].wait()
        tok[...] = dot_nn(pick, tokens_ref[:, cols])
        for q in range(blocks):
            head[q * cap : (q + 1) * cap, :] = tok[0:cap, q * LANES : (q + 1) * LANES]
        packed = head[...].astype(BF)
        for h in range(half):
            base = (d * half + h) * unit
            out_ref[base : base + lead, :] = packed
    for d in range(n_dp):
        cols = slice(d * width, (d + 1) * width)
        copies[2 + n_dp + d].wait()
        tgt[...] = dot_nn(pick, target_ref[:, cols])
        for h in range(half):
            for core in range(2):
                lo = (core * half + h % 4 * (half // 4) + h // 4) * LANES
                tail[core * cap : (core + 1) * cap, :] = tgt[0:cap, lo : lo + LANES]
            base = (d * half + h) * unit
            out_ref[base + lead : base + unit, :] = tail[...].astype(BF)


def both_cores(place_ref, own_ref, other_ref, wide):
    size = own_ref.shape[0]
    core = core_of(place_ref)
    wide[pl.ds(pl.multiple_of(core * size, size), size), :] = own_ref[...].astype(wide.dtype)
    wide[pl.ds(pl.multiple_of((1 - core) * size, size), size), :] = other_ref[...].astype(wide.dtype)


def fetch_columns(starts, gate_hbm, up_hbm, gate_w, up_w, sems):
    lo, hi = starts
    copies = []
    for k, at in enumerate(range(lo, hi, 2 * LANES)):
        count = min(2 * LANES, hi - at)
        pair = []
        for side, (src, dst) in enumerate(((gate_hbm, gate_w), (up_hbm, up_w))):
            part = src.at[:, pl.ds(at, count)]
            pair.append(pltpu.make_async_copy(part, dst.at[:, pl.ds(at - lo, count)], sems.at[k, side]))
            pair[-1].start()
        copies.append(pair)
    return copies


def load_kernel(start, gate_hbm, up_hbm, *refs):
    done_ref, gate_w, up_w, sems = refs[-4:]
    stop = start + gate_w.shape[1]
    copies = fetch_columns((start, stop), gate_hbm, up_hbm, gate_w, up_w, sems)
    done_ref[...] = jnp.zeros_like(done_ref)
    for pair in copies:
        for copy in pair:
            copy.wait()


def partial_pre(rows_ref, gate_w, up_w, copies, first, own_pre, send_pre):
    for j in range(gate_w.shape[1] // LANES):
        if copies and j % 2 == 0:
            for copy in copies[j // 2]:
                copy.wait()
        here = slice(j * LANES, (j + 1) * LANES)
        cols = slice(first + j * LANES, first + (j + 1) * LANES)
        pair = jnp.concatenate([gate_w[:, here], up_w[:, here]], axis=1)
        both = dot_nn(rows_ref[...], pair)
        for side in range(2):
            value = both[:, side * LANES : (side + 1) * LANES]
            own_pre[side, :, cols] = value
            send_pre[side, :, cols] = value.astype(BF)


def first_pre_kernel(dims, place_ref, loaded_ref, own_ref, other_ref, gate_head, up_head, gate_rest, up_rest,
                     rows_ref, target_ref, gates_ref, own_pre, send_pre, wide):
    n_dp, half, cap, blocks, unit = dims
    sources = 2 * n_dp * half
    both_cores(place_ref, own_ref, other_ref, wide)
    core = core_of(place_ref)

    def one(k):
        return wide[pl.ds(k, sources, stride=unit), :]

    for c in range(cap):
        rows = slice(c * sources, (c + 1) * sources)
        for q in range(blocks):
            rows_ref[rows, q * LANES : (q + 1) * LANES] = one(q * cap + c).astype(BF)
        base = blocks * cap
        target_ref[rows, :] = jnp.where(core == 0, one(base + c), one(base + cap + c))
        gates_ref[rows, :] = sum(one(base + (2 + piece) * cap + c) for piece in range(GATE_PIECES))
    partial_pre(rows_ref, gate_head, up_head, (), 0, own_pre, send_pre)
    partial_pre(rows_ref, gate_rest, up_rest, (), gate_head.shape[1], own_pre, send_pre)


def more_pre_kernel(start, rows_ref, gate_hbm, up_hbm, turned_ref, own_pre, send_pre, gate_w, up_w, sems):
    copies = fetch_columns((start, start + own_pre.shape[2]), gate_hbm, up_hbm, gate_w, up_w, sems)
    turned_ref[...] = rows_ref[...].T
    partial_pre(rows_ref, gate_w, up_w, copies, 0, own_pre, send_pre)


def down_side(dims, start, place_ref, hidden, down_w, total_ref, side, out_ref):
    n_dp, half, cap, blocks, unit = dims
    rows, hid = hidden.shape
    quarter = half // 4
    core = core_of(place_ref) if side == 0 else 1 - core_of(place_ref)
    for k in range(4):
        quad = quad_of(place_ref, k)
        for j in range(0, quarter, 2):
            lo = (core * half + quad * quarter + j) * LANES
            cols = pl.ds(pl.multiple_of(lo, 2 * LANES), 2 * LANES)
            value = dot_nn(hidden[...], down_w[start : start + hid, cols])
            for n in range(2):
                part = value[:, n * LANES : (n + 1) * LANES]
                block = k * quarter + j + n
                if total_ref is not None:
                    both = side * half + block
                    part = part + total_ref[both * rows : (both + 1) * rows, :]
                out_ref[block * rows : (block + 1) * rows, :] = part.astype(out_ref.dtype)


def activate(own_ref, got_ref, up_deriv, act_ref, hidden):
    gate_pre = own_ref[0] + got_ref[0].astype(F32)
    up_pre = own_ref[1] + got_ref[1].astype(F32)
    sig = jax.nn.sigmoid(gate_pre)
    act = sig * gate_pre
    act_ref[...] = act
    up_deriv[...] = up_pre * (sig * (1.0 + gate_pre * (1.0 - sig)))
    hidden[...] = (act * up_pre).astype(BF)


def first_down_kernel(dims, start, place_ref, own_ref, got_ref, down_w, up_deriv, act_ref, total_ref, hidden):
    activate(own_ref, got_ref, up_deriv, act_ref, hidden)
    size = dims[1] * hidden.shape[0]
    for side in range(2):
        part = total_ref.at[side * size : (side + 1) * size]
        down_side(dims, start, place_ref, hidden, down_w, None, side, part)


def send_down_kernel(dims, start, place_ref, own_ref, got_ref, down_w, total_ref, up_deriv, act_ref, hidden, send_ref):
    activate(own_ref, got_ref, up_deriv, act_ref, hidden)
    down_side(dims, start, place_ref, hidden, down_w, total_ref, 1, send_ref)


def keep_down_kernel(dims, start, place_ref, hidden, down_w, total_ref, keep_ref):
    down_side(dims, start, place_ref, hidden, down_w, total_ref, 0, keep_ref)


def chip_sum_kernel(own_ref, got_ref, keep_ref, *send_refs):
    size = keep_ref.shape[0]
    for k, ref in enumerate((keep_ref, *send_refs)):
        at = slice(k * size, (k + 1) * size)
        ref[...] = (own_ref[at, :] + got_ref[at, :].astype(F32)).astype(ref.dtype)


def residual_kernel(place_ref, own_ref, first_ref, second_ref, third_ref, gates_ref, target_ref, keep_ref, send_ref):
    rows = target_ref.shape[0]
    for z in range(own_ref.shape[0] // rows):
        at = slice(z * rows, (z + 1) * rows)
        value = own_ref[at, :] + first_ref[at, :].astype(F32)
        value = value + (second_ref[at, :].astype(F32) + third_ref[at, :].astype(F32))
        value = gates_ref[...] * value
        value = jnp.where(rest_of(place_ref) == z, value - target_ref[...], value)
        keep_ref[at, :] = value
        send_ref[at, :] = value.astype(BF)


def line_sum_kernel(own_ref, got_ref, keep_ref, send_ref):
    value = own_ref[...] + got_ref[...].astype(F32)
    keep_ref[...] = value
    send_ref[...] = value.astype(BF)


def cotangent_kernel(own_ref, got_ref, gates_ref, out_ref):
    rows = gates_ref.shape[0]
    for z in range(own_ref.shape[0] // rows):
        at = slice(z * rows, (z + 1) * rows)
        out_ref[at, :] = (gates_ref[...] * (own_ref[at, :] + got_ref[at, :].astype(F32))).astype(BF)


def gather_blocks(refs, out):
    rows = out.shape[0]
    parts = refs[0].shape[0] // rows
    for k, ref in enumerate(refs):
        for h in range(parts):
            lo = (k * parts + h) * LANES
            out[:, lo : lo + LANES] = ref[h * rows : (h + 1) * rows, :]


def quad_grad_hidden(cot, core, quads, down_w, start, total_ref, outs):
    width = cot.shape[1] // len(quads)
    size = outs[0].shape[1]
    for lo in range(0, size, 2 * LANES):
        here = slice(lo, min(lo + 2 * LANES, size))
        there = slice(start + here.start, start + here.stop)
        value = total_ref[:, there] if total_ref is not None else None
        for k, quad in enumerate(quads):
            cols = pl.ds(pl.multiple_of((4 * core + quad) * width, width), width)
            part = dot_nt(cot[:, k * width : (k + 1) * width], down_w[there, cols])
            value = part if value is None else value + part
        for out in outs:
            out[:, here] = value.astype(out.dtype)


def near_grad_hidden_kernel(flip, flips, place_ref, down_w, *refs):
    got_refs, rest = refs[: len(flips)], refs[len(flips) :]
    *total_ref, out_ref, cot = rest
    core = 1 - core_of(place_ref) if flip else core_of(place_ref)
    quads = [quad_of(place_ref, k) for k in flips]
    gather_blocks(got_refs, cot)
    quad_grad_hidden(cot, core, quads, down_w, 0, total_ref[0] if total_ref else None, (out_ref,))


def first_grad_hidden_kernel(start, place_ref, first_ref, second_ref, third_ref, down_w, total_ref, cot, own_out, send_out):
    gather_blocks((first_ref, second_ref, third_ref), cot)
    quads = [quad_of(place_ref, k) for k in (1, 2, 3)]
    quad_grad_hidden(cot, 1 - core_of(place_ref), quads, down_w, start, total_ref, (own_out, send_out))


def more_grad_hidden_kernel(start, place_ref, cot, down_w, total_ref, own_out, send_out):
    quads = [quad_of(place_ref, k) for k in (1, 2, 3)]
    quad_grad_hidden(cot, 1 - core_of(place_ref), quads, down_w, start, total_ref, (own_out, send_out))


def row_grad_kernel(dims, start, last, place_ref, own_ref, got_ref, up_deriv, act_ref, gate_w, up_w, *refs):
    n_dp, half, cap, blocks, unit = dims
    sources = 2 * n_dp * half
    refs = list(refs)
    total_ref = refs.pop(0) if start > 0 else None
    gate_out, up_out, *out_refs = refs
    grad_hidden = own_ref[...] + got_ref[...].astype(F32)
    gate_out[...] = (grad_hidden * up_deriv[...]).astype(BF)
    up_out[...] = (grad_hidden * act_ref[...]).astype(BF)
    hid = gate_out.shape[1]
    wide = out_refs[-1]

    def column(j, _):
        at = pl.ds(pl.multiple_of(j * 2 * LANES, 2 * LANES), 2 * LANES)
        value = dot_nt(gate_out[...], gate_w[at, start : start + hid])
        value = value + dot_nt(up_out[...], up_w[at, start : start + hid])
        if total_ref is not None:
            value = value + total_ref[:, at]
        if not last:
            wide[:, at] = value
            return 0
        for k in range(2):
            for c in range(cap):
                piece = value[c * sources : (c + 1) * sources, k * LANES : (k + 1) * LANES]
                wide[pl.ds((2 * j + k) * cap + c, sources, stride=blocks * cap), :] = piece
        return 0

    lax.fori_loop(0, blocks // 2, column, 0, unroll=True)
    if last:
        keep_ref, send_ref, _ = out_refs
        size = keep_ref.shape[0]
        core = core_of(place_ref)
        keep_ref[...] = wide[pl.ds(pl.multiple_of(core * size, size), size), :]
        send_ref[...] = wide[pl.ds(pl.multiple_of((1 - core) * size, size), size), :].astype(BF)


def weight_grad_kernel(parts, tile, turned_ref, *refs):
    grads = (refs[:parts], refs[parts : 2 * parts])
    outs, values, sems = refs[2 * parts : 2 * parts + 2], refs[2 * parts + 2 : 2 * parts + 4], refs[-1]
    copies = []
    for t in range(turned_ref.shape[0] // tile):
        at = slice(t * tile, (t + 1) * tile)
        for side in range(2):
            lo = 0
            for ref in grads[side]:
                size = ref.shape[1]
                values[side][at, lo : lo + size] = dot_nn(turned_ref[at, :], ref[...]).astype(BF)
                lo += size
            copies.append(pltpu.make_async_copy(values[side].at[at, :], outs[side].at[at, :], sems.at[t, side]))
            copies[-1].start()
    for copy in copies:
        copy.wait()


def token_grad_kernel(dims, pick_ref, got_ref, out_hbm, rows, out, sems):
    n_dp, half, cap, blocks, unit = dims
    size = blocks * cap
    width = blocks * LANES
    pick = pick_ref[...]
    rows[...] = jnp.zeros_like(rows)
    copies = []
    for d in range(n_dp):
        total = got_ref[d * half * size : (d * half + 1) * size, :].astype(F32)
        for h in range(1, half):
            base = (d * half + h) * size
            total = total + got_ref[base : base + size, :].astype(F32)
        for q in range(blocks):
            rows[0:cap, q * LANES : (q + 1) * LANES] = total[q * cap : (q + 1) * cap, :]
        cols = slice(d * width, (d + 1) * width)
        out[:, cols] = dot_tn(pick, rows[...].astype(BF)).astype(out.dtype)
        copies.append(pltpu.make_async_copy(out.at[:, cols], out_hbm.at[:, cols], sems.at[d]))
        copies[-1].start()
    for copy in copies:
        copy.wait()


def fast_shards(n_dp, n_expert, cap, tokens, expert_ids, gate_values, w_gate, w_up, w_down, target):
    tok_rows, features = tokens.shape
    width, hid = w_gate.shape
    half = n_expert // 2
    blocks = width // LANES
    peers = n_dp * half
    sources = 2 * peers
    rows = cap * sources
    unit = -(-(blocks + 2 + GATE_PIECES) * cap // 16) * 16
    dims = (n_dp, half, cap, blocks, unit)
    place = lax.axis_index("expert").astype(jnp.int32).reshape(1)
    ids = expert_ids.T
    slice_groups = [
        [d * n_expert + 2 * h + c for d in range(n_dp) for h in range(half)] for c in range(2)
    ]

    def other(x, mask):
        return lax.ppermute(x, "expert", [(i, i ^ mask) for i in range(n_expert)])

    def other_core(x):
        return other(x, 1)

    def other_dp(x):
        return lax.ppermute(x, "dp", [(0, 1), (1, 0)])

    def over_slice(x):
        return lax.all_to_all(x, ("dp", "expert"), 0, 0, axis_index_groups=slice_groups, tiled=True)

    outgoing, pick = call(
        functools.partial(route_kernel, dims),
        (sds((peers * unit, LANES), BF), sds((16, tok_rows), BF)),
        in_hbm(ids, gate_values.T, tokens, target),
        [HBM] * 4,
        [
            pltpu.VMEM(ids.shape, ids.dtype),
            pltpu.VMEM(ids.shape, F32),
            pltpu.VMEM(tokens.shape, tokens.dtype),
            pltpu.VMEM(target.shape, target.dtype),
            pltpu.VMEM((16, width), F32),
            pltpu.VMEM((16, width), F32),
            pltpu.VMEM((blocks * cap, LANES), F32),
            pltpu.VMEM((unit - blocks * cap, LANES), F32),
            pltpu.SemaphoreType.DMA((2 + 2 * n_dp,)),
        ],
        name="route",
    )
    first = -(-hid // (2 * LANES)) * LANES
    head = 2 * LANES

    def load(start, size, after=()):
        return call(
            functools.partial(load_kernel, start),
            (sds((8, LANES), F32), sds((width, size), w_gate.dtype), sds((width, size), w_up.dtype)),
            (*in_hbm(w_gate, w_up), *after),
            [HBM] * 2 + [VMEM] * len(after),
            [pltpu.SemaphoreType.DMA((-(-size // (2 * LANES)), 2))],
            flops=1_000_000_000,
            moved=8 * width * size,
            name="load_weights",
        )

    loaded, *weights = load(0, head)
    own, loaded = lax.optimization_barrier((over_slice(outgoing), loaded))
    loaded, *more = load(head, first - head, (loaded,))
    weights += more
    neighbour = other_core(own)
    chunks = [(0, first), (first, hid - first)]
    last = len(chunks) - 1
    pres = []
    for start, size in chunks:
        outs = (sds((2, rows, size), F32), sds((2, rows, size), BF))
        cost = dict(flops=8 * rows * width * size, moved=4 * width * size)
        fetched = [
            pltpu.VMEM((width, size), w_gate.dtype),
            pltpu.VMEM((width, size), w_up.dtype),
            pltpu.SemaphoreType.DMA((-(-size // (2 * LANES)), 2)),
        ]
        if start == 0:
            all_rows, all_target, all_gates, *pre = call(
                functools.partial(first_pre_kernel, dims),
                (sds((rows, width), BF), sds((rows, LANES), F32), sds((rows, LANES), F32), *outs),
                (place, loaded, own, neighbour, *weights),
                [SMEM] + [VMEM] * 7,
                [pltpu.VMEM((sources * unit, LANES), F32)],
                name="pre_activations",
                **cost,
            )
        else:
            turned, *pre = call(
                functools.partial(more_pre_kernel, start),
                (sds((width, rows), BF), *outs),
                (all_rows, *in_hbm(w_gate, w_up)),
                [VMEM] + [HBM] * 2,
                fetched,
                name="pre_activations",
                **cost,
            )
        pres.append((pre[0], other_dp(pre[1])))
    (start, size), (start_b, size_b) = chunks
    half_rows = half * rows
    cost = dict(flops=4 * rows * width * size, moved=2 * width * size)
    up_deriv, act, total = call(
        functools.partial(first_down_kernel, dims, start),
        (sds((rows, size), F32), sds((rows, size), F32), sds((2 * half_rows, LANES), F32)),
        (place, *pres[0], w_down),
        [SMEM] + [VMEM] * 3,
        [pltpu.VMEM((rows, size), BF)],
        name="down",
        **cost,
    )
    up_deriv_b, act_b, hidden_b, send = call(
        functools.partial(send_down_kernel, dims, start_b),
        (
            sds((rows, size_b), F32),
            sds((rows, size_b), F32),
            sds((rows, size_b), BF),
            sds((half_rows, LANES), BF),
        ),
        (place, *pres[1], w_down, total),
        [SMEM] + [VMEM] * 4,
        name="down_send",
        **cost,
    )
    sent = other_core(send)
    keep = call(
        functools.partial(keep_down_kernel, dims, start_b),
        sds((half_rows, LANES), F32),
        (place, hidden_b, w_down, total),
        [SMEM] + [VMEM] * 3,
        name="down_keep",
        **cost,
    )
    saved = [(up_deriv, act), (up_deriv_b, act_b)]
    quad_rows = half_rows // 4
    kept, sent_on = sds((quad_rows, LANES), F32), sds((quad_rows, LANES), BF)
    keep, *sends = call(chip_sum_kernel, (kept, *[sent_on] * 3), (keep, sent), [VMEM] * 2, name="chip_sum")
    keep, send = call(
        residual_kernel,
        (kept, sent_on),
        (place, keep, *[other(x, 2 * (k + 1)) for k, x in enumerate(sends)], all_gates, all_target),
        [SMEM] + [VMEM] * 6,
        name="residual",
    )
    step = 8
    while 2 * step < n_expert:
        keep, send = call(line_sum_kernel, (kept, sent_on), (keep, other(send, step)), [VMEM] * 2, name="line_sum")
        step *= 2
    cot = call(
        cotangent_kernel,
        sent_on,
        (keep, other(send, step), all_gates),
        [VMEM] * 3,
        name="cotangent",
    )
    from_quad = [other(cot, 2 * k) for k in (1, 2, 3)]
    from_core = other_core(cot)

    def near(flip, flips, got, *total):
        return call(
            functools.partial(near_grad_hidden_kernel, flip, flips),
            sds((rows, hid), F32),
            (place, w_down, *got, *total),
            [SMEM] + [VMEM] * (1 + len(got) + len(total)),
            [pltpu.VMEM((rows, len(got) * quad_rows // rows * LANES), BF)],
            flops=len(got) * rows * width * hid // 4,
            moved=len(got) * width * hid // 4,
            name="grad_hidden_near",
        )

    own_total = near(0, (0,), (cot,))
    own_total = near(1, (0,), (from_core,), own_total)
    from_quad, own_total = lax.optimization_barrier((from_quad, own_total))
    from_both = [other_core(x) for x in from_quad]
    own_total = near(0, (1, 2, 3), from_quad, own_total)
    grads = []
    for start, size in chunks:
        outs = (sds((rows, size), F32), sds((rows, size), BF))
        cost = dict(flops=2 * rows * width * size, moved=2 * width * size)
        if start == 0:
            cot, *grad = call(
                functools.partial(first_grad_hidden_kernel, start),
                (sds((rows, 3 * width // 8), BF), *outs),
                (place, *from_both, w_down, own_total),
                [SMEM] + [VMEM] * 5,
                name="grad_hidden",
                **cost,
            )
        else:
            grad = call(
                functools.partial(more_grad_hidden_kernel, start),
                outs,
                (place, cot, w_down, own_total),
                [SMEM] + [VMEM] * 3,
                name="grad_hidden",
                **cost,
            )
        grads.append((grad[0], other_dp(grad[1])))
    pre_grads = []
    total = ()
    peer_rows = peers * blocks * cap
    for k, (start, size) in enumerate(chunks):
        outs, scratch = (sds((rows, width), F32),), []
        if k == last:
            outs = (sds((peer_rows, LANES), F32), sds((peer_rows, LANES), BF))
            scratch = [pltpu.VMEM((2 * peer_rows, LANES), F32)]
        gate_pre_grad, up_pre_grad, *total = call(
            functools.partial(row_grad_kernel, dims, start, k == last),
            (sds((rows, size), BF), sds((rows, size), BF), *outs),
            (place, *grads[k], *saved[k], w_gate, w_up, *total),
            [SMEM] + [VMEM] * (6 + len(total)),
            scratch,
            flops=8 * rows * width * size,
            moved=4 * width * size,
            name="row_grad",
        )
        pre_grads.append((gate_pre_grad, up_pre_grad))
    keep, send = total
    chip_rows = add_cores(keep, other_core(send))
    got_rows = over_slice(chip_rows)
    pre_grads = [pair[0] for pair in pre_grads] + [pair[1] for pair in pre_grads]
    tile = 256
    gate_grad, up_grad = call(
        functools.partial(weight_grad_kernel, len(chunks), tile),
        (sds((width, hid), BF), sds((width, hid), BF)),
        (turned, *pre_grads),
        [VMEM] * (1 + len(pre_grads)),
        [
            pltpu.VMEM((width, hid), BF),
            pltpu.VMEM((width, hid), BF),
            pltpu.SemaphoreType.DMA((width // tile, 2)),
        ],
        flops=4 * rows * width * hid,
        moved=4 * width * hid,
        out_spec=HBM,
        name="weight_grads",
    )
    token_grad = call(
        functools.partial(token_grad_kernel, dims),
        sds((tok_rows, features), tokens.dtype),
        (pick, got_rows),
        [VMEM] * 2,
        [
            pltpu.VMEM((16, width), F32),
            pltpu.VMEM((tok_rows, features), tokens.dtype),
            pltpu.SemaphoreType.DMA((n_dp,)),
        ],
        out_spec=HBM,
        name="token_grad",
    )
    return token_grad, gate_grad, up_grad


def contract_last(matrix_a, matrix_b):
    return lax.dot_general(
        matrix_a, matrix_b, (((1,), (1,)), ((), ())), preferred_element_type=jnp.float32
    )


def rounded_terms(column_blocks, grad_blocks):
    terms = jnp.einsum(
        "krd,krh->kdh", column_blocks, grad_blocks, preferred_element_type=jnp.float32
    )
    terms = lax.optimization_barrier(terms.astype(jnp.bfloat16))
    return jnp.sum(terms.astype(jnp.float32), axis=0)


def spread_rows(rows, group_size, capacity, features):
    flat = rows.reshape(EXPERTS, 1, capacity * features)
    wide = jnp.broadcast_to(flat, (EXPERTS, group_size, capacity * features))
    return wide.reshape(EXPERTS * group_size * capacity, features)


def fold_group(rows, group_size, capacity, features):
    shaped = rows.reshape(EXPERTS, group_size, capacity * features).astype(jnp.float32)
    return jnp.sum(shaped, axis=1).reshape(EXPERTS * capacity, features)


def general_shards(tokens, expert_ids, gate_values, w_gate, w_up, w_down, target):
    devices_along = lax.axis_size("expert")
    group_size = devices_along // EXPERTS
    tok_rows = tokens.shape[0]
    features = tokens.shape[1]
    hid_local = w_gate.shape[1]
    capacity = max(2, 3 * tok_rows // 128)
    slot_total = EXPERTS * capacity
    flat_ids = expert_ids.reshape(-1)
    pair_count = flat_ids.shape[0]
    window = flat_ids < EXPERTS
    onehot = (flat_ids[:, None] == jnp.arange(EXPERTS, dtype=jnp.int32)[None, :]).astype(jnp.int32)
    slot_index = jnp.sum((jnp.cumsum(onehot, axis=0) - onehot) * onehot, axis=1)
    position = jnp.where(window, flat_ids * capacity + slot_index, slot_total)
    owning = jnp.arange(pair_count, dtype=jnp.int32) // 2
    slot_token = jnp.zeros((slot_total + 1,), jnp.int32).at[position].set(owning)[:slot_total]
    slot_live = jnp.zeros((slot_total + 1,), jnp.bool_).at[position].set(True)[:slot_total]
    slot_gate = (
        jnp.zeros((slot_total + 1,), jnp.float32)
        .at[position]
        .set(gate_values.reshape(-1))[:slot_total]
    )
    safe_pairs = jnp.minimum(position, slot_total - 1).reshape(tok_rows, 2)
    live_pairs = window.reshape(tok_rows, 2)

    def pick(table, column):
        return jnp.where(live_pairs[:, column : column + 1], table[safe_pairs[:, column]], 0.0)

    outgoing = jnp.where(slot_live[:, None], tokens[slot_token], jnp.zeros((), tokens.dtype))
    outgoing = spread_rows(outgoing, group_size, capacity, features)
    received = lax.all_to_all(outgoing, "expert", split_axis=0, concat_axis=0, tiled=True)
    rows_count = received.shape[0]
    full_gate, full_up, full_down = (
        lax.all_gather(w_gate, "dp", axis=0, tiled=True),
        lax.all_gather(w_up, "dp", axis=0, tiled=True),
        lax.all_gather(w_down, "dp", axis=1, tiled=True),
    )
    gate_pre = jnp.dot(received, full_gate, preferred_element_type=jnp.float32)
    up_pre = jnp.dot(received, full_up, preferred_element_type=jnp.float32)
    sigmoid_gate = jax.nn.sigmoid(gate_pre)
    activated = sigmoid_gate * gate_pre
    hidden = (activated * up_pre).astype(jnp.bfloat16)
    partial_out = jnp.dot(hidden, full_down, preferred_element_type=jnp.float32).astype(
        jnp.bfloat16
    )
    returned_out = lax.all_to_all(partial_out, "expert", split_axis=0, concat_axis=0, tiled=True)
    expert_out = fold_group(returned_out, group_size, capacity, features)
    combined = gate_values[:, 0:1] * pick(expert_out, 0) + gate_values[:, 1:2] * pick(expert_out, 1)
    residual = combined - target.astype(jnp.float32)
    outgoing_grad = jnp.where(
        slot_live[:, None], slot_gate[:, None] * residual[slot_token], 0.0
    ).astype(jnp.bfloat16)
    outgoing_grad = spread_rows(outgoing_grad, group_size, capacity, features)
    cotangent = lax.all_to_all(outgoing_grad, "expert", split_axis=0, concat_axis=0, tiled=True)
    grad_hidden = contract_last(cotangent, full_down)
    derivative = sigmoid_gate * (1.0 + gate_pre * (1.0 - sigmoid_gate))
    grad_gate_pre = (grad_hidden * up_pre * derivative).astype(jnp.bfloat16)
    grad_up_pre = (grad_hidden * activated).astype(jnp.bfloat16)
    row_part = (
        contract_last(grad_gate_pre, full_gate) + contract_last(grad_up_pre, full_up)
    ).astype(jnp.bfloat16)
    back_rows = lax.all_to_all(row_part, "expert", split_axis=0, concat_axis=0, tiled=True)
    row_grad = fold_group(back_rows, group_size, capacity, features)
    token_grad = (pick(row_grad, 0) + pick(row_grad, 1)).astype(jnp.bfloat16)
    shard_columns = lax.all_to_all(received, "dp", split_axis=1, concat_axis=0, tiled=True)
    shard_width = shard_columns.shape[1]
    dp_count = lax.axis_size("dp")
    every_gate, every_up = (
        lax.all_gather(grad_gate_pre, "dp", axis=0, tiled=True),
        lax.all_gather(grad_up_pre, "dp", axis=0, tiled=True),
    )
    column_blocks = shard_columns.reshape(dp_count, rows_count, shard_width)
    gate_sum = rounded_terms(column_blocks, every_gate.reshape(dp_count, rows_count, hid_local))
    up_sum = rounded_terms(column_blocks, every_up.reshape(dp_count, rows_count, hid_local))
    return (token_grad, gate_sum.astype(jnp.bfloat16), up_sum.astype(jnp.bfloat16))


def solution(mesh):
    n_dp, n_expert = mesh.shape["dp"], mesh.shape["expert"]

    def shards(*args):
        tok_rows, features = args[0].shape
        width, hid = args[3].shape
        cap = max(2, 3 * tok_rows // 128)
        whole_blocks = (
            n_dp == 2
            and n_expert % 16 == 0
            and n_expert & (n_expert - 1) == 0
            and width == n_expert * LANES
            and hid % LANES == 0
            and hid > 4 * LANES
            and cap <= 8
            and tok_rows % LANES == 0
        )
        if whole_blocks:
            return fast_shards(n_dp, n_expert, cap, *args)
        return general_shards(*args)

    placed = (
        P(("dp", "expert"), None),
        P(("dp", "expert"), None),
        P(("dp", "expert"), None),
        P("dp", "expert"),
        P("dp", "expert"),
        P("expert", "dp"),
        P(("dp", "expert"), None),
    )
    return jax.shard_map(
        shards,
        mesh=mesh,
        in_specs=placed,
        out_specs=(P(("dp", "expert"), None), P("dp", "expert"), P("dp", "expert")),
        check_vma=False,
    )
```

```python
import functools

import jax
import jax.numpy as jnp
from jax import lax
from jax.experimental import pallas as pl
from jax.experimental.pallas import tpu as pltpu
from jax.sharding import PartitionSpec as P

EXPERTS = 1
LANES = 128
GATE_PIECES = 3
BF = jnp.bfloat16
F32 = jnp.float32
VMEM = pl.BlockSpec(memory_space=pltpu.VMEM)
HBM = pl.BlockSpec(memory_space=pltpu.HBM)
SMEM = pl.BlockSpec(memory_space=pltpu.SMEM)


def sds(shape, dtype):
    return jax.ShapeDtypeStruct(shape, dtype)


def dot_nn(a, b):
    return lax.dot_general(a, b, (((1,), (0,)), ((), ())), preferred_element_type=F32)


def dot_nt(a, b):
    return lax.dot_general(a, b, (((1,), (1,)), ((), ())), preferred_element_type=F32)


def dot_tn(a, b):
    return lax.dot_general(a, b, (((0,), (0,)), ((), ())), preferred_element_type=F32)


def in_hbm(*arrays):
    return tuple(pltpu.with_memory_space_constraint(x, pltpu.HBM) for x in arrays)


def core_of(place_ref):
    return place_ref[0] & 1


def quad_of(place_ref, k=0):
    x, low = (place_ref[0] >> 1) & 1, (place_ref[0] >> 2) & 1
    return (1 - x if k & 1 else x) + 2 * (1 - low if k & 2 else low)


def rest_of(place_ref):
    return place_ref[0] >> 3


def call(body, outs, args, specs, scratch=(), limit=16, flops=0, moved=0, name=None, out_spec=VMEM):
    return pl.pallas_call(
        body,
        out_shape=outs,
        in_specs=specs,
        out_specs=jax.tree.map(lambda _: out_spec, outs),
        scratch_shapes=list(scratch),
        compiler_params=pltpu.CompilerParams(vmem_limit_bytes=limit << 20),
        cost_estimate=pl.CostEstimate(flops=flops, bytes_accessed=moved, transcendentals=0),
        name=name,
    )(*args)


def select_rows(ids_ref):
    tok_rows = ids_ref.shape[1]
    live = jnp.sum((ids_ref[...] < EXPERTS).astype(F32), axis=0, keepdims=True)
    before = lax.broadcasted_iota(jnp.int32, (tok_rows, tok_rows), 0)
    after = lax.broadcasted_iota(jnp.int32, (tok_rows, tok_rows), 1)
    earlier = (before < after).astype(BF)
    wide = jnp.broadcast_to(live, (16, tok_rows))
    slot = dot_nn(wide.astype(BF), earlier)
    wanted = lax.broadcasted_iota(jnp.int32, (16, tok_rows), 0).astype(F32)
    return jnp.where(slot == wanted, wide, 0.0)


def add_kernel(own_ref, got_ref, out_ref):
    out_ref[...] = (own_ref[...] + got_ref[...].astype(F32)).astype(out_ref.dtype)


def add_cores(own, got):
    return call(add_kernel, sds(got.shape, got.dtype), (own, got), [VMEM] * 2, name="add_cores")


def route_kernel(dims, ids_hbm, gates_hbm, tokens_hbm, target_hbm, out_ref, pick_ref,
                 ids_ref, gates_ref, tokens_ref, target_ref, tok, tgt, head, tail, sems):
    n_dp, half, cap, blocks, unit = dims
    width = blocks * LANES
    pairs = [(ids_hbm, ids_ref), (gates_hbm, gates_ref)]
    for hbm, ref in ((tokens_hbm, tokens_ref), (target_hbm, target_ref)):
        for d in range(n_dp):
            cols = slice(d * width, (d + 1) * width)
            pairs.append((hbm.at[:, cols], ref.at[:, cols]))
    copies = [pltpu.make_async_copy(src, dst, sems.at[i]) for i, (src, dst) in enumerate(pairs)]
    for copy in copies:
        copy.start()
    tail[...] = jnp.zeros_like(tail)
    copies[0].wait()
    copies[1].wait()
    chosen = select_rows(ids_ref)
    live_gates = jnp.sum(jnp.where(ids_ref[...] < EXPERTS, gates_ref[...], 0.0), axis=0, keepdims=True)
    gate = jnp.sum(chosen * live_gates, axis=1, keepdims=True)
    pick = chosen.astype(BF)
    pick_ref[...] = pick
    rest = gate
    for piece in range(GATE_PIECES):
        part = rest.astype(BF).astype(F32)
        rest = rest - part
        at = (2 + piece) * cap
        tail[at : at + cap, :] = jnp.broadcast_to(part[0:cap], (cap, LANES))
    lead = blocks * cap
    for d in range(n_dp):
        cols = slice(d * width, (d + 1) * width)
        copies[2 + d].wait()
        tok[...] = dot_nn(pick, tokens_ref[:, cols])
        for q in range(blocks):
            head[q * cap : (q + 1) * cap, :] = tok[0:cap, q * LANES : (q + 1) * LANES]
        packed = head[...].astype(BF)
        for h in range(half):
            base = (d * half + h) * unit
            out_ref[base : base + lead, :] = packed
    for d in range(n_dp):
        cols = slice(d * width, (d + 1) * width)
        copies[2 + n_dp + d].wait()
        tgt[...] = dot_nn(pick, target_ref[:, cols])
        for h in range(half):
            for core in range(2):
                lo = (core * half + h % 4 * (half // 4) + h // 4) * LANES
                tail[core * cap : (core + 1) * cap, :] = tgt[0:cap, lo : lo + LANES]
            base = (d * half + h) * unit
            out_ref[base + lead : base + unit, :] = tail[...].astype(BF)


def lay_out(dims, place_ref, src_ref, wide, begin, rows_ref, target_ref, gates_ref):
    n_dp, half, cap, blocks, unit = dims
    peers = n_dp * half
    wide[...] = src_ref[...].astype(F32)

    def one(k):
        return wide[pl.ds(k, peers, stride=unit), :]

    for c in range(cap):
        at = begin(c)
        for q in range(blocks):
            rows_ref[at, q * LANES : (q + 1) * LANES] = one(q * cap + c).astype(BF)
        base = blocks * cap
        target_ref[at, :] = jnp.where(core_of(place_ref) == 0, one(base + c), one(base + cap + c))
        gates_ref[at, :] = sum(one(base + (2 + piece) * cap + c) for piece in range(GATE_PIECES))


def fetch_columns(starts, gate_hbm, up_hbm, gate_w, up_w, sems):
    lo, hi = starts
    copies = []
    for k, at in enumerate(range(lo, hi, 2 * LANES)):
        count = min(2 * LANES, hi - at)
        pair = []
        for side, (src, dst) in enumerate(((gate_hbm, gate_w), (up_hbm, up_w))):
            part = src.at[:, pl.ds(at, count)]
            pair.append(pltpu.make_async_copy(part, dst.at[:, pl.ds(at - lo, count)], sems.at[k, side]))
            pair[-1].start()
        copies.append(pair)
    return copies


def load_kernel(gate_hbm, up_hbm, done_ref, gate_w, up_w, sems):
    copies = fetch_columns((0, gate_w.shape[1]), gate_hbm, up_hbm, gate_w, up_w, sems)
    done_ref[...] = jnp.zeros_like(done_ref)
    for pair in copies:
        for copy in pair:
            copy.wait()


def load_more_kernel(dims, start, place_ref, own_ref, gate_hbm, up_hbm, gate_w, up_w,
                     rows_ref, target_ref, gates_ref, wide, sems):
    peers = dims[0] * dims[1]
    copies = fetch_columns((start, start + gate_w.shape[1]), gate_hbm, up_hbm, gate_w, up_w, sems)
    begin = lambda c: slice(c * peers, (c + 1) * peers)
    lay_out(dims, place_ref, own_ref, wide, begin, rows_ref, target_ref, gates_ref)
    for pair in copies:
        for copy in pair:
            copy.wait()


def partial_pre(rows_ref, gate_w, up_w, copies, first, own_pre, send_pre):
    for j in range(gate_w.shape[1] // LANES):
        if copies and j % 2 == 0:
            for copy in copies[j // 2]:
                copy.wait()
        here = slice(j * LANES, (j + 1) * LANES)
        cols = slice(first + j * LANES, first + (j + 1) * LANES)
        pair = jnp.concatenate([gate_w[:, here], up_w[:, here]], axis=1)
        both = dot_nn(rows_ref[...], pair)
        for side in range(2):
            value = both[:, side * LANES : (side + 1) * LANES]
            own_pre[side, :, cols] = value
            send_pre[side, :, cols] = value.astype(BF)


def first_pre_kernel(dims, place_ref, loaded_ref, own_rows, own_target, own_gates, other_ref,
                     gate_head, up_head, gate_rest, up_rest,
                     rows_ref, target_ref, gates_ref, own_pre, send_pre, wide):
    n_dp, half, cap, blocks, unit = dims
    peers = n_dp * half
    core = core_of(place_ref)

    def begin(c, side):
        return pl.ds(pl.multiple_of((2 * c + side) * peers, peers), peers)

    for c in range(cap):
        here = slice(c * peers, (c + 1) * peers)
        for own, full in ((own_rows, rows_ref), (own_target, target_ref), (own_gates, gates_ref)):
            full[begin(c, core), :] = own[here, :]
    there = lambda c: begin(c, 1 - core)
    lay_out(dims, place_ref, other_ref, wide, there, rows_ref, target_ref, gates_ref)
    partial_pre(rows_ref, gate_head, up_head, (), 0, own_pre, send_pre)
    partial_pre(rows_ref, gate_rest, up_rest, (), gate_head.shape[1], own_pre, send_pre)


def more_pre_kernel(start, rows_ref, gate_hbm, up_hbm, turned_ref, own_pre, send_pre, gate_w, up_w, sems):
    copies = fetch_columns((start, start + own_pre.shape[2]), gate_hbm, up_hbm, gate_w, up_w, sems)
    turned_ref[...] = rows_ref[...].T
    partial_pre(rows_ref, gate_w, up_w, copies, 0, own_pre, send_pre)


def down_side(dims, start, place_ref, hidden, down_w, total_ref, side, out_ref):
    n_dp, half, cap, blocks, unit = dims
    rows, hid = hidden.shape
    quarter = half // 4
    core = core_of(place_ref) if side == 0 else 1 - core_of(place_ref)
    for k in range(4):
        quad = quad_of(place_ref, k)
        for j in range(0, quarter, 2):
            lo = (core * half + quad * quarter + j) * LANES
            cols = pl.ds(pl.multiple_of(lo, 2 * LANES), 2 * LANES)
            value = dot_nn(hidden[...], down_w[start : start + hid, cols])
            for n in range(2):
                part = value[:, n * LANES : (n + 1) * LANES]
                block = k * quarter + j + n
                if total_ref is not None:
                    both = side * half + block
                    part = part + total_ref[both * rows : (both + 1) * rows, :]
                out_ref[block * rows : (block + 1) * rows, :] = part.astype(out_ref.dtype)


def activate(own_ref, got_ref, up_deriv, act_ref, hidden):
    gate_pre = own_ref[0] + got_ref[0].astype(F32)
    up_pre = own_ref[1] + got_ref[1].astype(F32)
    sig = jax.nn.sigmoid(gate_pre)
    act = sig * gate_pre
    act_ref[...] = act
    up_deriv[...] = up_pre * (sig * (1.0 + gate_pre * (1.0 - sig)))
    hidden[...] = (act * up_pre).astype(BF)


def first_down_kernel(dims, start, place_ref, own_ref, got_ref, down_w, up_deriv, act_ref, total_ref, hidden):
    activate(own_ref, got_ref, up_deriv, act_ref, hidden)
    size = dims[1] * hidden.shape[0]
    for side in range(2):
        part = total_ref.at[side * size : (side + 1) * size]
        down_side(dims, start, place_ref, hidden, down_w, None, side, part)


def send_down_kernel(dims, start, place_ref, own_ref, got_ref, down_w, total_ref, up_deriv, act_ref, hidden, send_ref):
    activate(own_ref, got_ref, up_deriv, act_ref, hidden)
    down_side(dims, start, place_ref, hidden, down_w, total_ref, 1, send_ref)


def keep_down_kernel(dims, start, place_ref, hidden, down_w, total_ref, keep_ref):
    down_side(dims, start, place_ref, hidden, down_w, total_ref, 0, keep_ref)


def chip_sum_kernel(own_ref, got_ref, keep_ref, *send_refs):
    size = keep_ref.shape[0]
    for k, ref in enumerate((keep_ref, *send_refs)):
        at = slice(k * size, (k + 1) * size)
        ref[...] = (own_ref[at, :] + got_ref[at, :].astype(F32)).astype(ref.dtype)


def residual_kernel(place_ref, own_ref, first_ref, second_ref, third_ref, gates_ref, target_ref, keep_ref, send_ref):
    rows = target_ref.shape[0]
    for z in range(own_ref.shape[0] // rows):
        at = slice(z * rows, (z + 1) * rows)
        value = own_ref[at, :] + first_ref[at, :].astype(F32)
        value = value + (second_ref[at, :].astype(F32) + third_ref[at, :].astype(F32))
        value = gates_ref[...] * value
        value = jnp.where(rest_of(place_ref) == z, value - target_ref[...], value)
        keep_ref[at, :] = value
        send_ref[at, :] = value.astype(BF)


def line_sum_kernel(own_ref, got_ref, keep_ref, send_ref):
    value = own_ref[...] + got_ref[...].astype(F32)
    keep_ref[...] = value
    send_ref[...] = value.astype(BF)


def cotangent_kernel(own_ref, got_ref, gates_ref, out_ref):
    rows = gates_ref.shape[0]
    for z in range(own_ref.shape[0] // rows):
        at = slice(z * rows, (z + 1) * rows)
        out_ref[at, :] = (gates_ref[...] * (own_ref[at, :] + got_ref[at, :].astype(F32))).astype(BF)


def gather_blocks(refs, out):
    rows = out.shape[0]
    parts = refs[0].shape[0] // rows
    for k, ref in enumerate(refs):
        for h in range(parts):
            lo = (k * parts + h) * LANES
            out[:, lo : lo + LANES] = ref[h * rows : (h + 1) * rows, :]


def quad_grad_hidden(cot, core, quads, down_w, start, total_ref, outs):
    width = cot.shape[1] // len(quads)
    size = outs[0].shape[1]
    for lo in range(0, size, 2 * LANES):
        here = slice(lo, min(lo + 2 * LANES, size))
        there = slice(start + here.start, start + here.stop)
        value = total_ref[:, there] if total_ref is not None else None
        for k, quad in enumerate(quads):
            cols = pl.ds(pl.multiple_of((4 * core + quad) * width, width), width)
            part = dot_nt(cot[:, k * width : (k + 1) * width], down_w[there, cols])
            value = part if value is None else value + part
        for out in outs:
            out[:, here] = value.astype(out.dtype)


def near_grad_hidden_kernel(flip, flips, place_ref, down_w, *refs):
    got_refs, rest = refs[: len(flips)], refs[len(flips) :]
    *total_ref, out_ref, cot = rest
    core = 1 - core_of(place_ref) if flip else core_of(place_ref)
    quads = [quad_of(place_ref, k) for k in flips]
    gather_blocks(got_refs, cot)
    quad_grad_hidden(cot, core, quads, down_w, 0, total_ref[0] if total_ref else None, (out_ref,))


def first_grad_hidden_kernel(start, place_ref, first_ref, second_ref, third_ref, down_w, total_ref, cot, own_out, send_out):
    gather_blocks((first_ref, second_ref, third_ref), cot)
    quads = [quad_of(place_ref, k) for k in (1, 2, 3)]
    quad_grad_hidden(cot, 1 - core_of(place_ref), quads, down_w, start, total_ref, (own_out, send_out))


def more_grad_hidden_kernel(start, place_ref, cot, down_w, total_ref, own_out, send_out):
    quads = [quad_of(place_ref, k) for k in (1, 2, 3)]
    quad_grad_hidden(cot, 1 - core_of(place_ref), quads, down_w, start, total_ref, (own_out, send_out))


def row_grad_kernel(dims, start, last, place_ref, own_ref, got_ref, up_deriv, act_ref, gate_w, up_w, *refs):
    n_dp, half, cap, blocks, unit = dims
    sources = 2 * n_dp * half
    refs = list(refs)
    total_ref = refs.pop(0) if last else None
    gate_out, up_out, *out_refs = refs
    grad_hidden = own_ref[...] + got_ref[...].astype(F32)
    gate_out[...] = (grad_hidden * up_deriv[...]).astype(BF)
    up_out[...] = (grad_hidden * act_ref[...]).astype(BF)
    hid = gate_out.shape[1]
    wide = out_refs[-1]

    def column(j, _):
        at = pl.ds(pl.multiple_of(j * 2 * LANES, 2 * LANES), 2 * LANES)
        value = dot_nt(gate_out[...], gate_w[at, start : start + hid])
        value = value + dot_nt(up_out[...], up_w[at, start : start + hid])
        if total_ref is not None:
            value = value + total_ref[:, at]
        if not last:
            wide[:, at] = value
            return 0
        for k in range(2):
            for c in range(cap):
                piece = value[c * sources : (c + 1) * sources, k * LANES : (k + 1) * LANES]
                wide[pl.ds((2 * j + k) * cap + c, sources, stride=blocks * cap), :] = piece
        return 0

    lax.fori_loop(0, blocks // 2, column, 0, unroll=True)
    if last:
        keep_ref, send_ref, _ = out_refs
        size = keep_ref.shape[0]
        core = core_of(place_ref)
        keep_ref[...] = wide[pl.ds(pl.multiple_of(core * size, size), size), :]
        send_ref[...] = wide[pl.ds(pl.multiple_of((1 - core) * size, size), size), :].astype(BF)


def weight_grad_kernel(parts, tile, turned_ref, *refs):
    grads = (refs[:parts], refs[parts : 2 * parts])
    outs, values, sems = refs[2 * parts : 2 * parts + 2], refs[2 * parts + 2 : 2 * parts + 4], refs[-1]
    copies = []
    for t in range(turned_ref.shape[0] // tile):
        at = slice(t * tile, (t + 1) * tile)
        for side in range(2):
            lo = 0
            for ref in grads[side]:
                size = ref.shape[1]
                values[side][at, lo : lo + size] = dot_nn(turned_ref[at, :], ref[...]).astype(BF)
                lo += size
            copies.append(pltpu.make_async_copy(values[side].at[at, :], outs[side].at[at, :], sems.at[t, side]))
            copies[-1].start()
    for copy in copies:
        copy.wait()


def token_grad_kernel(dims, pick_ref, got_ref, out_hbm, rows, out, sems):
    n_dp, half, cap, blocks, unit = dims
    size = blocks * cap
    width = blocks * LANES
    pick = pick_ref[...]
    rows[...] = jnp.zeros_like(rows)
    copies = []
    for d in range(n_dp):
        total = got_ref[d * half * size : (d * half + 1) * size, :].astype(F32)
        for h in range(1, half):
            base = (d * half + h) * size
            total = total + got_ref[base : base + size, :].astype(F32)
        for q in range(blocks):
            rows[0:cap, q * LANES : (q + 1) * LANES] = total[q * cap : (q + 1) * cap, :]
        cols = slice(d * width, (d + 1) * width)
        out[:, cols] = dot_tn(pick, rows[...].astype(BF)).astype(out.dtype)
        copies.append(pltpu.make_async_copy(out.at[:, cols], out_hbm.at[:, cols], sems.at[d]))
        copies[-1].start()
    for copy in copies:
        copy.wait()


def fast_shards(n_dp, n_expert, cap, tokens, expert_ids, gate_values, w_gate, w_up, w_down, target):
    tok_rows, features = tokens.shape
    width, hid = w_gate.shape
    half = n_expert // 2
    blocks = width // LANES
    peers = n_dp * half
    sources = 2 * peers
    rows = cap * sources
    unit = -(-(blocks + 2 + GATE_PIECES) * cap // 16) * 16
    dims = (n_dp, half, cap, blocks, unit)
    place = lax.axis_index("expert").astype(jnp.int32).reshape(1)
    ids = expert_ids.T
    slice_groups = [
        [d * n_expert + 2 * h + c for d in range(n_dp) for h in range(half)] for c in range(2)
    ]

    def other(x, mask):
        return lax.ppermute(x, "expert", [(i, i ^ mask) for i in range(n_expert)])

    def other_core(x):
        return other(x, 1)

    def other_dp(x):
        return lax.ppermute(x, "dp", [(0, 1), (1, 0)])

    def over_slice(x):
        return lax.all_to_all(x, ("dp", "expert"), 0, 0, axis_index_groups=slice_groups, tiled=True)

    outgoing, pick = call(
        functools.partial(route_kernel, dims),
        (sds((peers * unit, LANES), BF), sds((16, tok_rows), BF)),
        in_hbm(ids, gate_values.T, tokens, target),
        [HBM] * 4,
        [
            pltpu.VMEM(ids.shape, ids.dtype),
            pltpu.VMEM(ids.shape, F32),
            pltpu.VMEM(tokens.shape, tokens.dtype),
            pltpu.VMEM(target.shape, target.dtype),
            pltpu.VMEM((16, width), F32),
            pltpu.VMEM((16, width), F32),
            pltpu.VMEM((blocks * cap, LANES), F32),
            pltpu.VMEM((unit - blocks * cap, LANES), F32),
            pltpu.SemaphoreType.DMA((2 + 2 * n_dp,)),
        ],
        name="route",
    )
    first = -(-hid // (2 * LANES)) * LANES
    head = 2 * LANES

    def columns(size):
        return sds((width, size), w_gate.dtype), sds((width, size), w_up.dtype)

    def column_sems(size):
        return pltpu.SemaphoreType.DMA((-(-size // (2 * LANES)), 2))

    loaded, *weights = call(
        load_kernel,
        (sds((8, LANES), F32), *columns(head)),
        in_hbm(w_gate, w_up),
        [HBM] * 2,
        [column_sems(head)],
        flops=1_000_000_000,
        moved=8 * width * head,
        name="load_weights",
    )
    own, loaded = lax.optimization_barrier((over_slice(outgoing), loaded))
    *more, own_rows, own_target, own_gates = call(
        functools.partial(load_more_kernel, dims, head),
        (
            *columns(first - head),
            sds((cap * peers, width), BF),
            sds((cap * peers, LANES), F32),
            sds((cap * peers, LANES), F32),
        ),
        (place, own, *in_hbm(w_gate, w_up)),
        [SMEM, VMEM] + [HBM] * 2,
        [pltpu.VMEM((peers * unit, LANES), F32), column_sems(first - head)],
        flops=1_000_000_000,
        moved=8 * width * head,
        name="load_weights",
    )
    weights += more
    neighbour = other_core(own)
    chunks = [(0, first), (first, hid - first)]
    pres = []
    for start, size in chunks:
        outs = (sds((2, rows, size), F32), sds((2, rows, size), BF))
        cost = dict(flops=8 * rows * width * size, moved=4 * width * size)
        fetched = [
            pltpu.VMEM((width, size), w_gate.dtype),
            pltpu.VMEM((width, size), w_up.dtype),
            column_sems(size),
        ]
        if start == 0:
            all_rows, all_target, all_gates, *pre = call(
                functools.partial(first_pre_kernel, dims),
                (sds((rows, width), BF), sds((rows, LANES), F32), sds((rows, LANES), F32), *outs),
                (place, loaded, own_rows, own_target, own_gates, neighbour, *weights),
                [SMEM] + [VMEM] * 9,
                [pltpu.VMEM((peers * unit, LANES), F32)],
                name="pre_activations",
                **cost,
            )
        else:
            turned, *pre = call(
                functools.partial(more_pre_kernel, start),
                (sds((width, rows), BF), *outs),
                (all_rows, *in_hbm(w_gate, w_up)),
                [VMEM] + [HBM] * 2,
                fetched,
                name="pre_activations",
                **cost,
            )
        pres.append((pre[0], other_dp(pre[1])))
    (start, size), (start_b, size_b) = chunks
    half_rows = half * rows
    cost = dict(flops=4 * rows * width * size, moved=2 * width * size)
    up_deriv, act, total = call(
        functools.partial(first_down_kernel, dims, start),
        (sds((rows, size), F32), sds((rows, size), F32), sds((2 * half_rows, LANES), F32)),
        (place, *pres[0], w_down),
        [SMEM] + [VMEM] * 3,
        [pltpu.VMEM((rows, size), BF)],
        name="down",
        **cost,
    )
    up_deriv_b, act_b, hidden_b, send = call(
        functools.partial(send_down_kernel, dims, start_b),
        (
            sds((rows, size_b), F32),
            sds((rows, size_b), F32),
            sds((rows, size_b), BF),
            sds((half_rows, LANES), BF),
        ),
        (place, *pres[1], w_down, total),
        [SMEM] + [VMEM] * 4,
        name="down_send",
        **cost,
    )
    sent = other_core(send)
    keep = call(
        functools.partial(keep_down_kernel, dims, start_b),
        sds((half_rows, LANES), F32),
        (place, hidden_b, w_down, total),
        [SMEM] + [VMEM] * 3,
        name="down_keep",
        **cost,
    )
    saved = [(up_deriv, act), (up_deriv_b, act_b)]
    quad_rows = half_rows // 4
    kept, sent_on = sds((quad_rows, LANES), F32), sds((quad_rows, LANES), BF)
    keep, *sends = call(chip_sum_kernel, (kept, *[sent_on] * 3), (keep, sent), [VMEM] * 2, name="chip_sum")
    keep, send = call(
        residual_kernel,
        (kept, sent_on),
        (place, keep, *[other(x, 2 * (k + 1)) for k, x in enumerate(sends)], all_gates, all_target),
        [SMEM] + [VMEM] * 6,
        name="residual",
    )
    step = 8
    while 2 * step < n_expert:
        keep, send = call(line_sum_kernel, (kept, sent_on), (keep, other(send, step)), [VMEM] * 2, name="line_sum")
        step *= 2
    cot = call(
        cotangent_kernel,
        sent_on,
        (keep, other(send, step), all_gates),
        [VMEM] * 3,
        name="cotangent",
    )
    from_quad = [other(cot, 2 * k) for k in (1, 2, 3)]
    from_core = other_core(cot)

    def near(flip, flips, got, *total):
        return call(
            functools.partial(near_grad_hidden_kernel, flip, flips),
            sds((rows, hid), F32),
            (place, w_down, *got, *total),
            [SMEM] + [VMEM] * (1 + len(got) + len(total)),
            [pltpu.VMEM((rows, len(got) * quad_rows // rows * LANES), BF)],
            flops=len(got) * rows * width * hid // 4,
            moved=len(got) * width * hid // 4,
            name="grad_hidden_near",
        )

    own_total = near(0, (0,), (cot,))
    own_total = near(1, (0,), (from_core,), own_total)
    from_quad, own_total = lax.optimization_barrier((from_quad, own_total))
    from_both = [other_core(x) for x in from_quad]
    own_total = near(0, (1, 2, 3), from_quad, own_total)
    grads = []
    order = [1, 0]
    for k in order:
        start, size = chunks[k]
        outs = (sds((rows, size), F32), sds((rows, size), BF))
        cost = dict(flops=2 * rows * width * size, moved=2 * width * size)
        if k == order[0]:
            cot, *grad = call(
                functools.partial(first_grad_hidden_kernel, start),
                (sds((rows, 3 * width // 8), BF), *outs),
                (place, *from_both, w_down, own_total),
                [SMEM] + [VMEM] * 5,
                name="grad_hidden",
                **cost,
            )
        else:
            grad = call(
                functools.partial(more_grad_hidden_kernel, start),
                outs,
                (place, cot, w_down, own_total),
                [SMEM] + [VMEM] * 3,
                name="grad_hidden",
                **cost,
            )
        grads.append((grad[0], other_dp(grad[1])))
    pre_grads = [None] * len(chunks)
    total = ()
    peer_rows = peers * blocks * cap
    for k, grad in zip(order, grads):
        start, size = chunks[k]
        outs, scratch = (sds((rows, width), F32),), []
        if k == order[-1]:
            outs = (sds((peer_rows, LANES), F32), sds((peer_rows, LANES), BF))
            scratch = [pltpu.VMEM((2 * peer_rows, LANES), F32)]
        gate_pre_grad, up_pre_grad, *total = call(
            functools.partial(row_grad_kernel, dims, start, k == order[-1]),
            (sds((rows, size), BF), sds((rows, size), BF), *outs),
            (place, *grad, *saved[k], w_gate, w_up, *total),
            [SMEM] + [VMEM] * (6 + len(total)),
            scratch,
            flops=8 * rows * width * size,
            moved=4 * width * size,
            name="row_grad",
        )
        pre_grads[k] = (gate_pre_grad, up_pre_grad)
    keep, send = total
    chip_rows = add_cores(keep, other_core(send))
    got_rows = over_slice(chip_rows)
    pre_grads = [pair[0] for pair in pre_grads] + [pair[1] for pair in pre_grads]
    tile = 256
    gate_grad, up_grad = call(
        functools.partial(weight_grad_kernel, len(chunks), tile),
        (sds((width, hid), BF), sds((width, hid), BF)),
        (turned, *pre_grads),
        [VMEM] * (1 + len(pre_grads)),
        [
            pltpu.VMEM((width, hid), BF),
            pltpu.VMEM((width, hid), BF),
            pltpu.SemaphoreType.DMA((width // tile, 2)),
        ],
        flops=4 * rows * width * hid,
        moved=4 * width * hid,
        out_spec=HBM,
        name="weight_grads",
    )
    token_grad = call(
        functools.partial(token_grad_kernel, dims),
        sds((tok_rows, features), tokens.dtype),
        (pick, got_rows),
        [VMEM] * 2,
        [
            pltpu.VMEM((16, width), F32),
            pltpu.VMEM((tok_rows, features), tokens.dtype),
            pltpu.SemaphoreType.DMA((n_dp,)),
        ],
        out_spec=HBM,
        name="token_grad",
    )
    return token_grad, gate_grad, up_grad


def contract_last(matrix_a, matrix_b):
    return lax.dot_general(
        matrix_a, matrix_b, (((1,), (1,)), ((), ())), preferred_element_type=jnp.float32
    )


def rounded_terms(column_blocks, grad_blocks):
    terms = jnp.einsum(
        "krd,krh->kdh", column_blocks, grad_blocks, preferred_element_type=jnp.float32
    )
    terms = lax.optimization_barrier(terms.astype(jnp.bfloat16))
    return jnp.sum(terms.astype(jnp.float32), axis=0)


def spread_rows(rows, group_size, capacity, features):
    flat = rows.reshape(EXPERTS, 1, capacity * features)
    wide = jnp.broadcast_to(flat, (EXPERTS, group_size, capacity * features))
    return wide.reshape(EXPERTS * group_size * capacity, features)


def fold_group(rows, group_size, capacity, features):
    shaped = rows.reshape(EXPERTS, group_size, capacity * features).astype(jnp.float32)
    return jnp.sum(shaped, axis=1).reshape(EXPERTS * capacity, features)


def general_shards(tokens, expert_ids, gate_values, w_gate, w_up, w_down, target):
    devices_along = lax.axis_size("expert")
    group_size = devices_along // EXPERTS
    tok_rows = tokens.shape[0]
    features = tokens.shape[1]
    hid_local = w_gate.shape[1]
    capacity = max(2, 3 * tok_rows // 128)
    slot_total = EXPERTS * capacity
    flat_ids = expert_ids.reshape(-1)
    pair_count = flat_ids.shape[0]
    window = flat_ids < EXPERTS
    onehot = (flat_ids[:, None] == jnp.arange(EXPERTS, dtype=jnp.int32)[None, :]).astype(jnp.int32)
    slot_index = jnp.sum((jnp.cumsum(onehot, axis=0) - onehot) * onehot, axis=1)
    position = jnp.where(window, flat_ids * capacity + slot_index, slot_total)
    owning = jnp.arange(pair_count, dtype=jnp.int32) // 2
    slot_token = jnp.zeros((slot_total + 1,), jnp.int32).at[position].set(owning)[:slot_total]
    slot_live = jnp.zeros((slot_total + 1,), jnp.bool_).at[position].set(True)[:slot_total]
    slot_gate = (
        jnp.zeros((slot_total + 1,), jnp.float32)
        .at[position]
        .set(gate_values.reshape(-1))[:slot_total]
    )
    safe_pairs = jnp.minimum(position, slot_total - 1).reshape(tok_rows, 2)
    live_pairs = window.reshape(tok_rows, 2)

    def pick(table, column):
        return jnp.where(live_pairs[:, column : column + 1], table[safe_pairs[:, column]], 0.0)

    outgoing = jnp.where(slot_live[:, None], tokens[slot_token], jnp.zeros((), tokens.dtype))
    outgoing = spread_rows(outgoing, group_size, capacity, features)
    received = lax.all_to_all(outgoing, "expert", split_axis=0, concat_axis=0, tiled=True)
    rows_count = received.shape[0]
    full_gate, full_up, full_down = (
        lax.all_gather(w_gate, "dp", axis=0, tiled=True),
        lax.all_gather(w_up, "dp", axis=0, tiled=True),
        lax.all_gather(w_down, "dp", axis=1, tiled=True),
    )
    gate_pre = jnp.dot(received, full_gate, preferred_element_type=jnp.float32)
    up_pre = jnp.dot(received, full_up, preferred_element_type=jnp.float32)
    sigmoid_gate = jax.nn.sigmoid(gate_pre)
    activated = sigmoid_gate * gate_pre
    hidden = (activated * up_pre).astype(jnp.bfloat16)
    partial_out = jnp.dot(hidden, full_down, preferred_element_type=jnp.float32).astype(
        jnp.bfloat16
    )
    returned_out = lax.all_to_all(partial_out, "expert", split_axis=0, concat_axis=0, tiled=True)
    expert_out = fold_group(returned_out, group_size, capacity, features)
    combined = gate_values[:, 0:1] * pick(expert_out, 0) + gate_values[:, 1:2] * pick(expert_out, 1)
    residual = combined - target.astype(jnp.float32)
    outgoing_grad = jnp.where(
        slot_live[:, None], slot_gate[:, None] * residual[slot_token], 0.0
    ).astype(jnp.bfloat16)
    outgoing_grad = spread_rows(outgoing_grad, group_size, capacity, features)
    cotangent = lax.all_to_all(outgoing_grad, "expert", split_axis=0, concat_axis=0, tiled=True)
    grad_hidden = contract_last(cotangent, full_down)
    derivative = sigmoid_gate * (1.0 + gate_pre * (1.0 - sigmoid_gate))
    grad_gate_pre = (grad_hidden * up_pre * derivative).astype(jnp.bfloat16)
    grad_up_pre = (grad_hidden * activated).astype(jnp.bfloat16)
    row_part = (
        contract_last(grad_gate_pre, full_gate) + contract_last(grad_up_pre, full_up)
    ).astype(jnp.bfloat16)
    back_rows = lax.all_to_all(row_part, "expert", split_axis=0, concat_axis=0, tiled=True)
    row_grad = fold_group(back_rows, group_size, capacity, features)
    token_grad = (pick(row_grad, 0) + pick(row_grad, 1)).astype(jnp.bfloat16)
    shard_columns = lax.all_to_all(received, "dp", split_axis=1, concat_axis=0, tiled=True)
    shard_width = shard_columns.shape[1]
    dp_count = lax.axis_size("dp")
    every_gate, every_up = (
        lax.all_gather(grad_gate_pre, "dp", axis=0, tiled=True),
        lax.all_gather(grad_up_pre, "dp", axis=0, tiled=True),
    )
    column_blocks = shard_columns.reshape(dp_count, rows_count, shard_width)
    gate_sum = rounded_terms(column_blocks, every_gate.reshape(dp_count, rows_count, hid_local))
    up_sum = rounded_terms(column_blocks, every_up.reshape(dp_count, rows_count, hid_local))
    return (token_grad, gate_sum.astype(jnp.bfloat16), up_sum.astype(jnp.bfloat16))


def solution(mesh):
    n_dp, n_expert = mesh.shape["dp"], mesh.shape["expert"]

    def shards(*args):
        tok_rows, features = args[0].shape
        width, hid = args[3].shape
        cap = max(2, 3 * tok_rows // 128)
        whole_blocks = (
            n_dp == 2
            and n_expert % 16 == 0
            and n_expert & (n_expert - 1) == 0
            and width == n_expert * LANES
            and hid % LANES == 0
            and hid > 4 * LANES
            and cap <= 8
            and tok_rows % LANES == 0
        )
        if whole_blocks:
            return fast_shards(n_dp, n_expert, cap, *args)
        return general_shards(*args)

    placed = (
        P(("dp", "expert"), None),
        P(("dp", "expert"), None),
        P(("dp", "expert"), None),
        P("dp", "expert"),
        P("dp", "expert"),
        P("expert", "dp"),
        P(("dp", "expert"), None),
    )
    return jax.shard_map(
        shards,
        mesh=mesh,
        in_specs=placed,
        out_specs=(P(("dp", "expert"), None), P("dp", "expert"), P("dp", "expert")),
        check_vma=False,
    )
```

```python
import functools

import jax
import jax.numpy as jnp
from jax import lax
from jax.experimental import pallas as pl
from jax.experimental.pallas import tpu as pltpu
from jax.sharding import PartitionSpec as P

EXPERTS = 1
LANES = 128
GATE_PIECES = 3
BF = jnp.bfloat16
F32 = jnp.float32
VMEM = pl.BlockSpec(memory_space=pltpu.VMEM)
HBM = pl.BlockSpec(memory_space=pltpu.HBM)
SMEM = pl.BlockSpec(memory_space=pltpu.SMEM)


def sds(shape, dtype):
    return jax.ShapeDtypeStruct(shape, dtype)


def dot_nn(a, b):
    return lax.dot_general(a, b, (((1,), (0,)), ((), ())), preferred_element_type=F32)


def dot_nt(a, b):
    return lax.dot_general(a, b, (((1,), (1,)), ((), ())), preferred_element_type=F32)


def dot_tn(a, b):
    return lax.dot_general(a, b, (((0,), (0,)), ((), ())), preferred_element_type=F32)


def in_hbm(*arrays):
    return tuple(pltpu.with_memory_space_constraint(x, pltpu.HBM) for x in arrays)


def core_of(place_ref):
    return place_ref[0] & 1


def quad_of(place_ref, k=0):
    x, low = (place_ref[0] >> 1) & 1, (place_ref[0] >> 2) & 1
    return (1 - x if k & 1 else x) + 2 * (1 - low if k & 2 else low)


def rest_of(place_ref):
    return place_ref[0] >> 3


def call(body, outs, args, specs, scratch=(), limit=16, flops=0, moved=0, name=None, out_spec=VMEM):
    return pl.pallas_call(
        body,
        out_shape=outs,
        in_specs=specs,
        out_specs=jax.tree.map(lambda _: out_spec, outs),
        scratch_shapes=list(scratch),
        compiler_params=pltpu.CompilerParams(vmem_limit_bytes=limit << 20),
        cost_estimate=pl.CostEstimate(flops=flops, bytes_accessed=moved, transcendentals=0),
        name=name,
    )(*args)


def select_rows(ids_ref):
    tok_rows = ids_ref.shape[1]
    live = jnp.sum((ids_ref[...] < EXPERTS).astype(F32), axis=0, keepdims=True)
    before = lax.broadcasted_iota(jnp.int32, (tok_rows, tok_rows), 0)
    after = lax.broadcasted_iota(jnp.int32, (tok_rows, tok_rows), 1)
    earlier = (before < after).astype(BF)
    wide = jnp.broadcast_to(live, (16, tok_rows))
    slot = dot_nn(wide.astype(BF), earlier)
    wanted = lax.broadcasted_iota(jnp.int32, (16, tok_rows), 0).astype(F32)
    return jnp.where(slot == wanted, wide, 0.0)


def add_kernel(own_ref, got_ref, out_ref):
    out_ref[...] = (own_ref[...] + got_ref[...].astype(F32)).astype(out_ref.dtype)


def add_cores(own, got):
    return call(add_kernel, sds(got.shape, got.dtype), (own, got), [VMEM] * 2, name="add_cores")


def route_kernel(dims, ids_hbm, gates_hbm, tokens_hbm, target_hbm, out_ref, pick_ref,
                 ids_ref, gates_ref, tokens_ref, target_ref, tok, tgt, head, tail, sems):
    n_dp, half, cap, blocks, unit = dims
    width = blocks * LANES
    pairs = [(ids_hbm, ids_ref), (gates_hbm, gates_ref)]
    for hbm, ref in ((tokens_hbm, tokens_ref), (target_hbm, target_ref)):
        for d in range(n_dp):
            cols = slice(d * width, (d + 1) * width)
            pairs.append((hbm.at[:, cols], ref.at[:, cols]))
    copies = [pltpu.make_async_copy(src, dst, sems.at[i]) for i, (src, dst) in enumerate(pairs)]
    for copy in copies:
        copy.start()
    tail[...] = jnp.zeros_like(tail)
    copies[0].wait()
    copies[1].wait()
    chosen = select_rows(ids_ref)
    live_gates = jnp.sum(jnp.where(ids_ref[...] < EXPERTS, gates_ref[...], 0.0), axis=0, keepdims=True)
    gate = jnp.sum(chosen * live_gates, axis=1, keepdims=True)
    pick = chosen.astype(BF)
    pick_ref[...] = pick
    rest = gate
    for piece in range(GATE_PIECES):
        part = rest.astype(BF).astype(F32)
        rest = rest - part
        at = (2 + piece) * cap
        tail[at : at + cap, :] = jnp.broadcast_to(part[0:cap], (cap, LANES))
    lead = blocks * cap
    for d in range(n_dp):
        cols = slice(d * width, (d + 1) * width)
        copies[2 + d].wait()
        tok[...] = dot_nn(pick, tokens_ref[:, cols])
        for q in range(blocks):
            head[q * cap : (q + 1) * cap, :] = tok[0:cap, q * LANES : (q + 1) * LANES]
        packed = head[...].astype(BF)
        for h in range(half):
            base = (d * half + h) * unit
            out_ref[base : base + lead, :] = packed
    for d in range(n_dp):
        cols = slice(d * width, (d + 1) * width)
        copies[2 + n_dp + d].wait()
        tgt[...] = dot_nn(pick, target_ref[:, cols])
        for h in range(half):
            for core in range(2):
                lo = (core * half + h % 4 * (half // 4) + h // 4) * LANES
                tail[core * cap : (core + 1) * cap, :] = tgt[0:cap, lo : lo + LANES]
            base = (d * half + h) * unit
            out_ref[base + lead : base + unit, :] = tail[...].astype(BF)


def lay_out(dims, place_ref, src_ref, wide, begin, rows_ref, target_ref, gates_ref):
    n_dp, half, cap, blocks, unit = dims
    peers = n_dp * half
    wide[...] = src_ref[...].astype(F32)

    def one(k):
        return wide[pl.ds(k, peers, stride=unit), :]

    for c in range(cap):
        at = begin(c)
        for q in range(blocks):
            rows_ref[at, q * LANES : (q + 1) * LANES] = one(q * cap + c).astype(BF)
        base = blocks * cap
        target_ref[at, :] = jnp.where(core_of(place_ref) == 0, one(base + c), one(base + cap + c))
        gates_ref[at, :] = sum(one(base + (2 + piece) * cap + c) for piece in range(GATE_PIECES))


def fetch_columns(starts, gate_hbm, up_hbm, gate_w, up_w, sems):
    lo, hi = starts
    copies = []
    for k, at in enumerate(range(lo, hi, 2 * LANES)):
        count = min(2 * LANES, hi - at)
        pair = []
        for side, (src, dst) in enumerate(((gate_hbm, gate_w), (up_hbm, up_w))):
            part = src.at[:, pl.ds(at, count)]
            pair.append(pltpu.make_async_copy(part, dst.at[:, pl.ds(at - lo, count)], sems.at[k, side]))
            pair[-1].start()
        copies.append(pair)
    return copies


def load_kernel(gate_hbm, up_hbm, done_ref, gate_w, up_w, sems):
    copies = fetch_columns((0, gate_w.shape[1]), gate_hbm, up_hbm, gate_w, up_w, sems)
    done_ref[...] = jnp.zeros_like(done_ref)
    for pair in copies:
        for copy in pair:
            copy.wait()


def load_more_kernel(dims, start, place_ref, own_ref, gate_hbm, up_hbm, gate_w, up_w,
                     rows_ref, target_ref, gates_ref, wide, sems):
    peers = dims[0] * dims[1]
    copies = fetch_columns((start, start + gate_w.shape[1]), gate_hbm, up_hbm, gate_w, up_w, sems)
    begin = lambda c: slice(c * peers, (c + 1) * peers)
    lay_out(dims, place_ref, own_ref, wide, begin, rows_ref, target_ref, gates_ref)
    for pair in copies:
        for copy in pair:
            copy.wait()


def partial_pre(rows_ref, gate_w, up_w, copies, first, own_pre, send_pre):
    for j in range(gate_w.shape[1] // LANES):
        if copies and j % 2 == 0:
            for copy in copies[j // 2]:
                copy.wait()
        here = slice(j * LANES, (j + 1) * LANES)
        cols = slice(first + j * LANES, first + (j + 1) * LANES)
        pair = jnp.concatenate([gate_w[:, here], up_w[:, here]], axis=1)
        both = dot_nn(rows_ref[...], pair)
        for side in range(2):
            value = both[:, side * LANES : (side + 1) * LANES]
            own_pre[side, :, cols] = value
            send_pre[side, :, cols] = value.astype(BF)


def first_pre_kernel(dims, place_ref, loaded_ref, own_rows, own_target, own_gates, other_ref,
                     gate_head, up_head, gate_rest, up_rest,
                     rows_ref, target_ref, gates_ref, own_pre, send_pre, wide):
    n_dp, half, cap, blocks, unit = dims
    peers = n_dp * half
    core = core_of(place_ref)

    def begin(c, side):
        return pl.ds(pl.multiple_of((2 * c + side) * peers, peers), peers)

    for c in range(cap):
        here = slice(c * peers, (c + 1) * peers)
        for own, full in ((own_rows, rows_ref), (own_target, target_ref), (own_gates, gates_ref)):
            full[begin(c, core), :] = own[here, :]
    there = lambda c: begin(c, 1 - core)
    lay_out(dims, place_ref, other_ref, wide, there, rows_ref, target_ref, gates_ref)
    partial_pre(rows_ref, gate_head, up_head, (), 0, own_pre, send_pre)
    partial_pre(rows_ref, gate_rest, up_rest, (), gate_head.shape[1], own_pre, send_pre)


def more_pre_kernel(start, rows_ref, gate_hbm, up_hbm, turned_ref, own_pre, send_pre, gate_w, up_w, sems):
    copies = fetch_columns((start, start + own_pre.shape[2]), gate_hbm, up_hbm, gate_w, up_w, sems)
    turned_ref[...] = rows_ref[...].T
    partial_pre(rows_ref, gate_w, up_w, copies, 0, own_pre, send_pre)


def down_side(dims, start, place_ref, hidden, down_w, total_ref, side, out_ref):
    n_dp, half, cap, blocks, unit = dims
    rows, hid = hidden.shape
    quarter = half // 4
    core = core_of(place_ref) if side == 0 else 1 - core_of(place_ref)
    for k in range(4):
        quad = quad_of(place_ref, k)
        for j in range(0, quarter, 2):
            lo = (core * half + quad * quarter + j) * LANES
            cols = pl.ds(pl.multiple_of(lo, 2 * LANES), 2 * LANES)
            value = dot_nn(hidden[...], down_w[start : start + hid, cols])
            for n in range(2):
                part = value[:, n * LANES : (n + 1) * LANES]
                block = k * quarter + j + n
                if total_ref is not None:
                    both = side * half + block
                    part = part + total_ref[both * rows : (both + 1) * rows, :]
                out_ref[block * rows : (block + 1) * rows, :] = part.astype(out_ref.dtype)


def activate(own_ref, got_ref, up_deriv, act_ref, hidden):
    gate_pre = own_ref[0] + got_ref[0].astype(F32)
    up_pre = own_ref[1] + got_ref[1].astype(F32)
    sig = jax.nn.sigmoid(gate_pre)
    act = sig * gate_pre
    act_ref[...] = act
    up_deriv[...] = up_pre * (sig * (1.0 + gate_pre * (1.0 - sig)))
    hidden[...] = (act * up_pre).astype(BF)


def first_down_kernel(dims, start, place_ref, own_ref, got_ref, down_w, up_deriv, act_ref, total_ref, hidden):
    activate(own_ref, got_ref, up_deriv, act_ref, hidden)
    size = dims[1] * hidden.shape[0]
    for side in range(2):
        part = total_ref.at[side * size : (side + 1) * size]
        down_side(dims, start, place_ref, hidden, down_w, None, side, part)


def send_down_kernel(dims, start, place_ref, own_ref, got_ref, down_w, total_ref, up_deriv, act_ref, hidden, send_ref):
    activate(own_ref, got_ref, up_deriv, act_ref, hidden)
    down_side(dims, start, place_ref, hidden, down_w, total_ref, 1, send_ref)


def keep_down_kernel(dims, start, place_ref, hidden, down_w, total_ref, keep_ref):
    down_side(dims, start, place_ref, hidden, down_w, total_ref, 0, keep_ref)


def chip_sum_kernel(own_ref, got_ref, keep_ref, *send_refs):
    size = keep_ref.shape[0]
    for k, ref in enumerate((keep_ref, *send_refs)):
        at = slice(k * size, (k + 1) * size)
        ref[...] = (own_ref[at, :] + got_ref[at, :].astype(F32)).astype(ref.dtype)


def residual_kernel(place_ref, own_ref, first_ref, second_ref, third_ref, gates_ref, target_ref, keep_ref, send_ref):
    rows = target_ref.shape[0]
    for z in range(own_ref.shape[0] // rows):
        at = slice(z * rows, (z + 1) * rows)
        value = own_ref[at, :] + first_ref[at, :].astype(F32)
        value = value + (second_ref[at, :].astype(F32) + third_ref[at, :].astype(F32))
        value = gates_ref[...] * value
        value = jnp.where(rest_of(place_ref) == z, value - target_ref[...], value)
        keep_ref[at, :] = value
        send_ref[at, :] = value.astype(BF)


def line_sum_kernel(own_ref, got_ref, keep_ref, send_ref):
    value = own_ref[...] + got_ref[...].astype(F32)
    keep_ref[...] = value
    send_ref[...] = value.astype(BF)


def cotangent_kernel(own_ref, got_ref, gates_ref, out_ref):
    rows = gates_ref.shape[0]
    for z in range(own_ref.shape[0] // rows):
        at = slice(z * rows, (z + 1) * rows)
        out_ref[at, :] = (gates_ref[...] * (own_ref[at, :] + got_ref[at, :].astype(F32))).astype(BF)


def gather_blocks(refs, out):
    rows = out.shape[0]
    parts = refs[0].shape[0] // rows
    for k, ref in enumerate(refs):
        for h in range(parts):
            lo = (k * parts + h) * LANES
            out[:, lo : lo + LANES] = ref[h * rows : (h + 1) * rows, :]


def quad_grad_hidden(cot, core, quads, down_w, start, total_ref, outs):
    width = cot.shape[1] // len(quads)
    size = outs[0].shape[1]
    for lo in range(0, size, 2 * LANES):
        here = slice(lo, min(lo + 2 * LANES, size))
        there = slice(start + here.start, start + here.stop)
        value = total_ref[:, there] if total_ref is not None else None
        for k, quad in enumerate(quads):
            cols = pl.ds(pl.multiple_of((4 * core + quad) * width, width), width)
            part = dot_nt(cot[:, k * width : (k + 1) * width], down_w[there, cols])
            value = part if value is None else value + part
        for out in outs:
            out[:, here] = value.astype(out.dtype)


def near_grad_hidden_kernel(flip, flips, place_ref, down_w, *refs):
    got_refs, rest = refs[: len(flips)], refs[len(flips) :]
    *total_ref, out_ref, cot = rest
    core = 1 - core_of(place_ref) if flip else core_of(place_ref)
    quads = [quad_of(place_ref, k) for k in flips]
    gather_blocks(got_refs, cot)
    quad_grad_hidden(cot, core, quads, down_w, 0, total_ref[0] if total_ref else None, (out_ref,))


def first_grad_hidden_kernel(start, place_ref, first_ref, second_ref, third_ref, down_w, total_ref, cot, own_out, send_out):
    gather_blocks((first_ref, second_ref, third_ref), cot)
    quads = [quad_of(place_ref, k) for k in (1, 2, 3)]
    quad_grad_hidden(cot, 1 - core_of(place_ref), quads, down_w, start, total_ref, (own_out, send_out))


def more_grad_hidden_kernel(start, place_ref, cot, down_w, total_ref, own_out, send_out):
    quads = [quad_of(place_ref, k) for k in (1, 2, 3)]
    quad_grad_hidden(cot, 1 - core_of(place_ref), quads, down_w, start, total_ref, (own_out, send_out))


def row_grad_kernel(dims, start, last, place_ref, own_ref, got_ref, up_deriv, act_ref, gate_w, up_w, *refs):
    n_dp, half, cap, blocks, unit = dims
    sources = 2 * n_dp * half
    refs = list(refs)
    total_ref = refs.pop(0) if last else None
    gate_out, up_out, *out_refs = refs
    grad_hidden = own_ref[...] + got_ref[...].astype(F32)
    gate_out[...] = (grad_hidden * up_deriv[...]).astype(BF)
    up_out[...] = (grad_hidden * act_ref[...]).astype(BF)
    hid = gate_out.shape[1]
    wide = out_refs[-1]

    def column(j, _):
        at = pl.ds(pl.multiple_of(j * 2 * LANES, 2 * LANES), 2 * LANES)
        value = dot_nt(gate_out[...], gate_w[at, start : start + hid])
        value = value + dot_nt(up_out[...], up_w[at, start : start + hid])
        if total_ref is not None:
            value = value + total_ref[:, at]
        if not last:
            wide[:, at] = value
            return 0
        for k in range(2):
            for c in range(cap):
                piece = value[c * sources : (c + 1) * sources, k * LANES : (k + 1) * LANES]
                wide[pl.ds((2 * j + k) * cap + c, sources, stride=blocks * cap), :] = piece
        return 0

    lax.fori_loop(0, blocks // 2, column, 0, unroll=True)
    if last:
        keep_ref, send_ref, _ = out_refs
        size = keep_ref.shape[0]
        core = core_of(place_ref)
        keep_ref[...] = wide[pl.ds(pl.multiple_of(core * size, size), size), :]
        send_ref[...] = wide[pl.ds(pl.multiple_of((1 - core) * size, size), size), :].astype(BF)


def weight_grad_kernel(parts, tile, turned_ref, *refs):
    grads = (refs[:parts], refs[parts : 2 * parts])
    outs, values, sems = refs[2 * parts : 2 * parts + 2], refs[2 * parts + 2 : 2 * parts + 4], refs[-1]
    copies = []
    for t in range(turned_ref.shape[0] // tile):
        at = slice(t * tile, (t + 1) * tile)
        for side in range(2):
            lo = 0
            for ref in grads[side]:
                size = ref.shape[1]
                values[side][at, lo : lo + size] = dot_nn(turned_ref[at, :], ref[...]).astype(BF)
                lo += size
            copies.append(pltpu.make_async_copy(values[side].at[at, :], outs[side].at[at, :], sems.at[t, side]))
            copies[-1].start()
    for copy in copies:
        copy.wait()


def token_grad_kernel(dims, pick_ref, got_ref, out_hbm, rows, out, sems):
    n_dp, half, cap, blocks, unit = dims
    size = blocks * cap
    width = blocks * LANES
    pick = pick_ref[...]
    rows[...] = jnp.zeros_like(rows)
    copies = []
    for d in range(n_dp):
        total = got_ref[d * half * size : (d * half + 1) * size, :].astype(F32)
        for h in range(1, half):
            base = (d * half + h) * size
            total = total + got_ref[base : base + size, :].astype(F32)
        for q in range(blocks):
            rows[0:cap, q * LANES : (q + 1) * LANES] = total[q * cap : (q + 1) * cap, :]
        cols = slice(d * width, (d + 1) * width)
        out[:, cols] = dot_tn(pick, rows[...].astype(BF)).astype(out.dtype)
        copies.append(pltpu.make_async_copy(out.at[:, cols], out_hbm.at[:, cols], sems.at[d]))
        copies[-1].start()
    for copy in copies:
        copy.wait()


def fast_shards(n_dp, n_expert, cap, tokens, expert_ids, gate_values, w_gate, w_up, w_down, target):
    tok_rows, features = tokens.shape
    width, hid = w_gate.shape
    half = n_expert // 2
    blocks = width // LANES
    peers = n_dp * half
    sources = 2 * peers
    rows = cap * sources
    unit = -(-(blocks + 2 + GATE_PIECES) * cap // 16) * 16
    dims = (n_dp, half, cap, blocks, unit)
    place = lax.axis_index("expert").astype(jnp.int32).reshape(1)
    ids = expert_ids.T
    slice_groups = [
        [d * n_expert + 2 * h + c for d in range(n_dp) for h in range(half)] for c in range(2)
    ]

    def other(x, mask):
        return lax.ppermute(x, "expert", [(i, i ^ mask) for i in range(n_expert)])

    def other_core(x):
        return other(x, 1)

    def other_dp(x):
        return lax.ppermute(x, "dp", [(0, 1), (1, 0)])

    def over_slice(x):
        return lax.all_to_all(x, ("dp", "expert"), 0, 0, axis_index_groups=slice_groups, tiled=True)

    outgoing, pick = call(
        functools.partial(route_kernel, dims),
        (sds((peers * unit, LANES), BF), sds((16, tok_rows), BF)),
        in_hbm(ids, gate_values.T, tokens, target),
        [HBM] * 4,
        [
            pltpu.VMEM(ids.shape, ids.dtype),
            pltpu.VMEM(ids.shape, F32),
            pltpu.VMEM(tokens.shape, tokens.dtype),
            pltpu.VMEM(target.shape, target.dtype),
            pltpu.VMEM((16, width), F32),
            pltpu.VMEM((16, width), F32),
            pltpu.VMEM((blocks * cap, LANES), F32),
            pltpu.VMEM((unit - blocks * cap, LANES), F32),
            pltpu.SemaphoreType.DMA((2 + 2 * n_dp,)),
        ],
        name="route",
    )
    first = -(-hid // (2 * LANES)) * LANES
    head = 2 * LANES

    def columns(size):
        return sds((width, size), w_gate.dtype), sds((width, size), w_up.dtype)

    def column_sems(size):
        return pltpu.SemaphoreType.DMA((-(-size // (2 * LANES)), 2))

    loaded, *weights = call(
        load_kernel,
        (sds((8, LANES), F32), *columns(head)),
        in_hbm(w_gate, w_up),
        [HBM] * 2,
        [column_sems(head)],
        flops=1_000_000_000,
        moved=8 * width * head,
        name="load_weights",
    )
    own, loaded = lax.optimization_barrier((over_slice(outgoing), loaded))
    *more, own_rows, own_target, own_gates = call(
        functools.partial(load_more_kernel, dims, head),
        (
            *columns(first - head),
            sds((cap * peers, width), BF),
            sds((cap * peers, LANES), F32),
            sds((cap * peers, LANES), F32),
        ),
        (place, own, *in_hbm(w_gate, w_up)),
        [SMEM, VMEM] + [HBM] * 2,
        [pltpu.VMEM((peers * unit, LANES), F32), column_sems(first - head)],
        flops=1_000_000_000,
        moved=8 * width * head,
        name="load_weights",
    )
    weights += more
    neighbour = other_core(own)
    chunks = [(0, first), (first, hid - first)]
    pres = []
    for start, size in chunks:
        outs = (sds((2, rows, size), F32), sds((2, rows, size), BF))
        cost = dict(flops=8 * rows * width * size, moved=4 * width * size)
        fetched = [
            pltpu.VMEM((width, size), w_gate.dtype),
            pltpu.VMEM((width, size), w_up.dtype),
            column_sems(size),
        ]
        if start == 0:
            all_rows, all_target, all_gates, *pre = call(
                functools.partial(first_pre_kernel, dims),
                (sds((rows, width), BF), sds((rows, LANES), F32), sds((rows, LANES), F32), *outs),
                (place, loaded, own_rows, own_target, own_gates, neighbour, *weights),
                [SMEM] + [VMEM] * 9,
                [pltpu.VMEM((peers * unit, LANES), F32)],
                name="pre_activations",
                **cost,
            )
        else:
            turned, *pre = call(
                functools.partial(more_pre_kernel, start),
                (sds((width, rows), BF), *outs),
                (all_rows, *in_hbm(w_gate, w_up)),
                [VMEM] + [HBM] * 2,
                fetched,
                name="pre_activations",
                **cost,
            )
        pres.append((pre[0], other_dp(pre[1])))
    (start, size), (start_b, size_b) = chunks
    half_rows = half * rows
    cost = dict(flops=4 * rows * width * size, moved=2 * width * size)
    up_deriv, act, total = call(
        functools.partial(first_down_kernel, dims, start),
        (sds((rows, size), F32), sds((rows, size), F32), sds((2 * half_rows, LANES), F32)),
        (place, *pres[0], w_down),
        [SMEM] + [VMEM] * 3,
        [pltpu.VMEM((rows, size), BF)],
        name="down",
        **cost,
    )
    up_deriv_b, act_b, hidden_b, send = call(
        functools.partial(send_down_kernel, dims, start_b),
        (
            sds((rows, size_b), F32),
            sds((rows, size_b), F32),
            sds((rows, size_b), BF),
            sds((half_rows, LANES), BF),
        ),
        (place, *pres[1], w_down, total),
        [SMEM] + [VMEM] * 4,
        name="down_send",
        **cost,
    )
    sent = other_core(send)
    keep = call(
        functools.partial(keep_down_kernel, dims, start_b),
        sds((half_rows, LANES), F32),
        (place, hidden_b, w_down, total),
        [SMEM] + [VMEM] * 3,
        name="down_keep",
        **cost,
    )
    saved = [(up_deriv, act), (up_deriv_b, act_b)]
    quad_rows = half_rows // 4
    kept, sent_on = sds((quad_rows, LANES), F32), sds((quad_rows, LANES), BF)
    keep, *sends = call(chip_sum_kernel, (kept, *[sent_on] * 3), (keep, sent), [VMEM] * 2, name="chip_sum")
    keep, send = call(
        residual_kernel,
        (kept, sent_on),
        (place, keep, *[other(x, 2 * (k + 1)) for k, x in enumerate(sends)], all_gates, all_target),
        [SMEM] + [VMEM] * 6,
        name="residual",
    )
    step = 8
    while 2 * step < n_expert:
        keep, send = call(line_sum_kernel, (kept, sent_on), (keep, other(send, step)), [VMEM] * 2, name="line_sum")
        step *= 2
    cot = call(
        cotangent_kernel,
        sent_on,
        (keep, other(send, step), all_gates),
        [VMEM] * 3,
        name="cotangent",
    )
    from_quad = [other(cot, 2 * k) for k in (1, 2, 3)]
    from_core = other_core(cot)

    def near(flip, flips, got, *total):
        return call(
            functools.partial(near_grad_hidden_kernel, flip, flips),
            sds((rows, hid), F32),
            (place, w_down, *got, *total),
            [SMEM] + [VMEM] * (1 + len(got) + len(total)),
            [pltpu.VMEM((rows, len(got) * quad_rows // rows * LANES), BF)],
            flops=len(got) * rows * width * hid // 4,
            moved=len(got) * width * hid // 4,
            name="grad_hidden_near",
        )

    own_total = near(0, (0,), (cot,))
    own_total = near(1, (0,), (from_core,), own_total)
    from_quad[2], own_total = lax.optimization_barrier((from_quad[2], own_total))
    from_both = [other_core(x) for x in from_quad]
    own_total = near(0, (1, 2, 3), from_quad, own_total)
    grads = []
    order = [1, 0]
    for k in order:
        start, size = chunks[k]
        outs = (sds((rows, size), F32), sds((rows, size), BF))
        cost = dict(flops=2 * rows * width * size, moved=2 * width * size)
        if k == order[0]:
            cot, *grad = call(
                functools.partial(first_grad_hidden_kernel, start),
                (sds((rows, 3 * width // 8), BF), *outs),
                (place, *from_both, w_down, own_total),
                [SMEM] + [VMEM] * 5,
                name="grad_hidden",
                **cost,
            )
        else:
            grad = call(
                functools.partial(more_grad_hidden_kernel, start),
                outs,
                (place, cot, w_down, own_total),
                [SMEM] + [VMEM] * 3,
                name="grad_hidden",
                **cost,
            )
        grads.append((grad[0], other_dp(grad[1])))
    pre_grads = [None] * len(chunks)
    total = ()
    peer_rows = peers * blocks * cap
    for k, grad in zip(order, grads):
        start, size = chunks[k]
        outs, scratch = (sds((rows, width), F32),), []
        if k == order[-1]:
            outs = (sds((peer_rows, LANES), F32), sds((peer_rows, LANES), BF))
            scratch = [pltpu.VMEM((2 * peer_rows, LANES), F32)]
        gate_pre_grad, up_pre_grad, *total = call(
            functools.partial(row_grad_kernel, dims, start, k == order[-1]),
            (sds((rows, size), BF), sds((rows, size), BF), *outs),
            (place, *grad, *saved[k], w_gate, w_up, *total),
            [SMEM] + [VMEM] * (6 + len(total)),
            scratch,
            flops=8 * rows * width * size,
            moved=4 * width * size,
            name="row_grad",
        )
        pre_grads[k] = (gate_pre_grad, up_pre_grad)
    keep, send = total
    chip_rows = add_cores(keep, other_core(send))
    got_rows = over_slice(chip_rows)
    pre_grads = [pair[0] for pair in pre_grads] + [pair[1] for pair in pre_grads]
    tile = 256
    gate_grad, up_grad = call(
        functools.partial(weight_grad_kernel, len(chunks), tile),
        (sds((width, hid), BF), sds((width, hid), BF)),
        (turned, *pre_grads),
        [VMEM] * (1 + len(pre_grads)),
        [
            pltpu.VMEM((width, hid), BF),
            pltpu.VMEM((width, hid), BF),
            pltpu.SemaphoreType.DMA((width // tile, 2)),
        ],
        flops=4 * rows * width * hid,
        moved=4 * width * hid,
        out_spec=HBM,
        name="weight_grads",
    )
    token_grad = call(
        functools.partial(token_grad_kernel, dims),
        sds((tok_rows, features), tokens.dtype),
        (pick, got_rows),
        [VMEM] * 2,
        [
            pltpu.VMEM((16, width), F32),
            pltpu.VMEM((tok_rows, features), tokens.dtype),
            pltpu.SemaphoreType.DMA((n_dp,)),
        ],
        out_spec=HBM,
        name="token_grad",
    )
    return token_grad, gate_grad, up_grad


def contract_last(matrix_a, matrix_b):
    return lax.dot_general(
        matrix_a, matrix_b, (((1,), (1,)), ((), ())), preferred_element_type=jnp.float32
    )


def rounded_terms(column_blocks, grad_blocks):
    terms = jnp.einsum(
        "krd,krh->kdh", column_blocks, grad_blocks, preferred_element_type=jnp.float32
    )
    terms = lax.optimization_barrier(terms.astype(jnp.bfloat16))
    return jnp.sum(terms.astype(jnp.float32), axis=0)


def spread_rows(rows, group_size, capacity, features):
    flat = rows.reshape(EXPERTS, 1, capacity * features)
    wide = jnp.broadcast_to(flat, (EXPERTS, group_size, capacity * features))
    return wide.reshape(EXPERTS * group_size * capacity, features)


def fold_group(rows, group_size, capacity, features):
    shaped = rows.reshape(EXPERTS, group_size, capacity * features).astype(jnp.float32)
    return jnp.sum(shaped, axis=1).reshape(EXPERTS * capacity, features)


def general_shards(tokens, expert_ids, gate_values, w_gate, w_up, w_down, target):
    devices_along = lax.axis_size("expert")
    group_size = devices_along // EXPERTS
    tok_rows = tokens.shape[0]
    features = tokens.shape[1]
    hid_local = w_gate.shape[1]
    capacity = max(2, 3 * tok_rows // 128)
    slot_total = EXPERTS * capacity
    flat_ids = expert_ids.reshape(-1)
    pair_count = flat_ids.shape[0]
    window = flat_ids < EXPERTS
    onehot = (flat_ids[:, None] == jnp.arange(EXPERTS, dtype=jnp.int32)[None, :]).astype(jnp.int32)
    slot_index = jnp.sum((jnp.cumsum(onehot, axis=0) - onehot) * onehot, axis=1)
    position = jnp.where(window, flat_ids * capacity + slot_index, slot_total)
    owning = jnp.arange(pair_count, dtype=jnp.int32) // 2
    slot_token = jnp.zeros((slot_total + 1,), jnp.int32).at[position].set(owning)[:slot_total]
    slot_live = jnp.zeros((slot_total + 1,), jnp.bool_).at[position].set(True)[:slot_total]
    slot_gate = (
        jnp.zeros((slot_total + 1,), jnp.float32)
        .at[position]
        .set(gate_values.reshape(-1))[:slot_total]
    )
    safe_pairs = jnp.minimum(position, slot_total - 1).reshape(tok_rows, 2)
    live_pairs = window.reshape(tok_rows, 2)

    def pick(table, column):
        return jnp.where(live_pairs[:, column : column + 1], table[safe_pairs[:, column]], 0.0)

    outgoing = jnp.where(slot_live[:, None], tokens[slot_token], jnp.zeros((), tokens.dtype))
    outgoing = spread_rows(outgoing, group_size, capacity, features)
    received = lax.all_to_all(outgoing, "expert", split_axis=0, concat_axis=0, tiled=True)
    rows_count = received.shape[0]
    full_gate, full_up, full_down = (
        lax.all_gather(w_gate, "dp", axis=0, tiled=True),
        lax.all_gather(w_up, "dp", axis=0, tiled=True),
        lax.all_gather(w_down, "dp", axis=1, tiled=True),
    )
    gate_pre = jnp.dot(received, full_gate, preferred_element_type=jnp.float32)
    up_pre = jnp.dot(received, full_up, preferred_element_type=jnp.float32)
    sigmoid_gate = jax.nn.sigmoid(gate_pre)
    activated = sigmoid_gate * gate_pre
    hidden = (activated * up_pre).astype(jnp.bfloat16)
    partial_out = jnp.dot(hidden, full_down, preferred_element_type=jnp.float32).astype(
        jnp.bfloat16
    )
    returned_out = lax.all_to_all(partial_out, "expert", split_axis=0, concat_axis=0, tiled=True)
    expert_out = fold_group(returned_out, group_size, capacity, features)
    combined = gate_values[:, 0:1] * pick(expert_out, 0) + gate_values[:, 1:2] * pick(expert_out, 1)
    residual = combined - target.astype(jnp.float32)
    outgoing_grad = jnp.where(
        slot_live[:, None], slot_gate[:, None] * residual[slot_token], 0.0
    ).astype(jnp.bfloat16)
    outgoing_grad = spread_rows(outgoing_grad, group_size, capacity, features)
    cotangent = lax.all_to_all(outgoing_grad, "expert", split_axis=0, concat_axis=0, tiled=True)
    grad_hidden = contract_last(cotangent, full_down)
    derivative = sigmoid_gate * (1.0 + gate_pre * (1.0 - sigmoid_gate))
    grad_gate_pre = (grad_hidden * up_pre * derivative).astype(jnp.bfloat16)
    grad_up_pre = (grad_hidden * activated).astype(jnp.bfloat16)
    row_part = (
        contract_last(grad_gate_pre, full_gate) + contract_last(grad_up_pre, full_up)
    ).astype(jnp.bfloat16)
    back_rows = lax.all_to_all(row_part, "expert", split_axis=0, concat_axis=0, tiled=True)
    row_grad = fold_group(back_rows, group_size, capacity, features)
    token_grad = (pick(row_grad, 0) + pick(row_grad, 1)).astype(jnp.bfloat16)
    shard_columns = lax.all_to_all(received, "dp", split_axis=1, concat_axis=0, tiled=True)
    shard_width = shard_columns.shape[1]
    dp_count = lax.axis_size("dp")
    every_gate, every_up = (
        lax.all_gather(grad_gate_pre, "dp", axis=0, tiled=True),
        lax.all_gather(grad_up_pre, "dp", axis=0, tiled=True),
    )
    column_blocks = shard_columns.reshape(dp_count, rows_count, shard_width)
    gate_sum = rounded_terms(column_blocks, every_gate.reshape(dp_count, rows_count, hid_local))
    up_sum = rounded_terms(column_blocks, every_up.reshape(dp_count, rows_count, hid_local))
    return (token_grad, gate_sum.astype(jnp.bfloat16), up_sum.astype(jnp.bfloat16))


def solution(mesh):
    n_dp, n_expert = mesh.shape["dp"], mesh.shape["expert"]

    def shards(*args):
        tok_rows, features = args[0].shape
        width, hid = args[3].shape
        cap = max(2, 3 * tok_rows // 128)
        whole_blocks = (
            n_dp == 2
            and n_expert % 16 == 0
            and n_expert & (n_expert - 1) == 0
            and width == n_expert * LANES
            and hid % LANES == 0
            and hid > 4 * LANES
            and cap <= 8
            and tok_rows % LANES == 0
        )
        if whole_blocks:
            return fast_shards(n_dp, n_expert, cap, *args)
        return general_shards(*args)

    placed = (
        P(("dp", "expert"), None),
        P(("dp", "expert"), None),
        P(("dp", "expert"), None),
        P("dp", "expert"),
        P("dp", "expert"),
        P("expert", "dp"),
        P(("dp", "expert"), None),
    )
    return jax.shard_map(
        shards,
        mesh=mesh,
        in_specs=placed,
        out_specs=(P(("dp", "expert"), None), P("dp", "expert"), P("dp", "expert")),
        check_vma=False,
    )
```

```python
import functools

import jax
import jax.numpy as jnp
from jax import lax
from jax.experimental import pallas as pl
from jax.experimental.pallas import tpu as pltpu
from jax.sharding import PartitionSpec as P

EXPERTS = 1
LANES = 128
GATE_PIECES = 3
BF = jnp.bfloat16
F32 = jnp.float32
VMEM = pl.BlockSpec(memory_space=pltpu.VMEM)
HBM = pl.BlockSpec(memory_space=pltpu.HBM)
SMEM = pl.BlockSpec(memory_space=pltpu.SMEM)


def sds(shape, dtype):
    return jax.ShapeDtypeStruct(shape, dtype)


def dot_nn(a, b):
    return lax.dot_general(a, b, (((1,), (0,)), ((), ())), preferred_element_type=F32)


def dot_nt(a, b):
    return lax.dot_general(a, b, (((1,), (1,)), ((), ())), preferred_element_type=F32)


def dot_tn(a, b):
    return lax.dot_general(a, b, (((0,), (0,)), ((), ())), preferred_element_type=F32)


def in_hbm(*arrays):
    return tuple(pltpu.with_memory_space_constraint(x, pltpu.HBM) for x in arrays)


def core_of(place_ref):
    return place_ref[0] & 1


def quad_of(place_ref, k=0):
    x, low = (place_ref[0] >> 1) & 1, (place_ref[0] >> 2) & 1
    return (1 - x if k & 1 else x) + 2 * (1 - low if k & 2 else low)


def rest_of(place_ref):
    return place_ref[0] >> 3


def call(body, outs, args, specs, scratch=(), limit=16, flops=0, moved=0, name=None, out_spec=VMEM):
    return pl.pallas_call(
        body,
        out_shape=outs,
        in_specs=specs,
        out_specs=jax.tree.map(lambda _: out_spec, outs),
        scratch_shapes=list(scratch),
        compiler_params=pltpu.CompilerParams(vmem_limit_bytes=limit << 20),
        cost_estimate=pl.CostEstimate(flops=flops, bytes_accessed=moved, transcendentals=0),
        name=name,
    )(*args)


def select_rows(ids_ref):
    tok_rows = ids_ref.shape[1]
    live = jnp.sum((ids_ref[...] < EXPERTS).astype(F32), axis=0, keepdims=True)
    before = lax.broadcasted_iota(jnp.int32, (tok_rows, tok_rows), 0)
    after = lax.broadcasted_iota(jnp.int32, (tok_rows, tok_rows), 1)
    earlier = (before < after).astype(BF)
    wide = jnp.broadcast_to(live, (16, tok_rows))
    slot = dot_nn(wide.astype(BF), earlier)
    wanted = lax.broadcasted_iota(jnp.int32, (16, tok_rows), 0).astype(F32)
    return jnp.where(slot == wanted, wide, 0.0)


def add_kernel(own_ref, got_ref, out_ref):
    out_ref[...] = (own_ref[...] + got_ref[...].astype(F32)).astype(out_ref.dtype)


def add_cores(own, got):
    return call(add_kernel, sds(got.shape, got.dtype), (own, got), [VMEM] * 2, name="add_cores")


def route_kernel(dims, ids_hbm, gates_hbm, tokens_hbm, target_hbm, out_ref, pick_ref,
                 ids_ref, gates_ref, tokens_ref, target_ref, tok, tgt, head, tail, sems):
    n_dp, half, cap, blocks, unit = dims
    width = blocks * LANES
    pairs = [(ids_hbm, ids_ref), (gates_hbm, gates_ref)]
    for hbm, ref in ((tokens_hbm, tokens_ref), (target_hbm, target_ref)):
        for d in range(n_dp):
            cols = slice(d * width, (d + 1) * width)
            pairs.append((hbm.at[:, cols], ref.at[:, cols]))
    copies = [pltpu.make_async_copy(src, dst, sems.at[i]) for i, (src, dst) in enumerate(pairs)]
    for copy in copies:
        copy.start()
    tail[...] = jnp.zeros_like(tail)
    copies[0].wait()
    copies[1].wait()
    chosen = select_rows(ids_ref)
    live_gates = jnp.sum(jnp.where(ids_ref[...] < EXPERTS, gates_ref[...], 0.0), axis=0, keepdims=True)
    gate = jnp.sum(chosen * live_gates, axis=1, keepdims=True)
    pick = chosen.astype(BF)
    pick_ref[...] = pick
    rest = gate
    for piece in range(GATE_PIECES):
        part = rest.astype(BF).astype(F32)
        rest = rest - part
        at = (2 + piece) * cap
        tail[at : at + cap, :] = jnp.broadcast_to(part[0:cap], (cap, LANES))
    lead = blocks * cap
    for d in range(n_dp):
        cols = slice(d * width, (d + 1) * width)
        copies[2 + d].wait()
        tok[...] = dot_nn(pick, tokens_ref[:, cols])
        for q in range(blocks):
            head[q * cap : (q + 1) * cap, :] = tok[0:cap, q * LANES : (q + 1) * LANES]
        packed = head[...].astype(BF)
        for h in range(half):
            base = (d * half + h) * unit
            out_ref[base : base + lead, :] = packed
    for d in range(n_dp):
        cols = slice(d * width, (d + 1) * width)
        copies[2 + n_dp + d].wait()
        tgt[...] = dot_nn(pick, target_ref[:, cols])
        for h in range(half):
            for core in range(2):
                lo = (core * half + h % 4 * (half // 4) + h // 4) * LANES
                tail[core * cap : (core + 1) * cap, :] = tgt[0:cap, lo : lo + LANES]
            base = (d * half + h) * unit
            out_ref[base + lead : base + unit, :] = tail[...].astype(BF)


def lay_out(dims, place_ref, src_ref, wide, begin, rows_ref, target_ref, gates_ref):
    n_dp, half, cap, blocks, unit = dims
    peers = n_dp * half
    wide[...] = src_ref[...].astype(F32)

    def one(k):
        return wide[pl.ds(k, peers, stride=unit), :]

    for c in range(cap):
        at = begin(c)
        for q in range(blocks):
            rows_ref[at, q * LANES : (q + 1) * LANES] = one(q * cap + c).astype(BF)
        base = blocks * cap
        target_ref[at, :] = jnp.where(core_of(place_ref) == 0, one(base + c), one(base + cap + c))
        gates_ref[at, :] = sum(one(base + (2 + piece) * cap + c) for piece in range(GATE_PIECES))


def fetch_columns(starts, gate_hbm, up_hbm, gate_w, up_w, sems):
    lo, hi = starts
    copies = []
    for k, at in enumerate(range(lo, hi, 2 * LANES)):
        count = min(2 * LANES, hi - at)
        pair = []
        for side, (src, dst) in enumerate(((gate_hbm, gate_w), (up_hbm, up_w))):
            part = src.at[:, pl.ds(at, count)]
            pair.append(pltpu.make_async_copy(part, dst.at[:, pl.ds(at - lo, count)], sems.at[k, side]))
            pair[-1].start()
        copies.append(pair)
    return copies


def load_kernel(gate_hbm, up_hbm, done_ref, gate_w, up_w, sems):
    copies = fetch_columns((0, gate_w.shape[1]), gate_hbm, up_hbm, gate_w, up_w, sems)
    done_ref[...] = jnp.zeros_like(done_ref)
    for pair in copies:
        for copy in pair:
            copy.wait()


def load_more_kernel(dims, start, place_ref, own_ref, gate_hbm, up_hbm, gate_w, up_w,
                     rows_ref, target_ref, gates_ref, wide, sems):
    peers = dims[0] * dims[1]
    copies = fetch_columns((start, start + gate_w.shape[1]), gate_hbm, up_hbm, gate_w, up_w, sems)
    begin = lambda c: slice(c * peers, (c + 1) * peers)
    lay_out(dims, place_ref, own_ref, wide, begin, rows_ref, target_ref, gates_ref)
    for pair in copies:
        for copy in pair:
            copy.wait()


def partial_pre(rows_ref, gate_w, up_w, copies, first, own_pre, send_pre):
    for j in range(gate_w.shape[1] // LANES):
        if copies and j % 2 == 0:
            for copy in copies[j // 2]:
                copy.wait()
        here = slice(j * LANES, (j + 1) * LANES)
        cols = slice(first + j * LANES, first + (j + 1) * LANES)
        pair = jnp.concatenate([gate_w[:, here], up_w[:, here]], axis=1)
        both = dot_nn(rows_ref[...], pair)
        for side in range(2):
            value = both[:, side * LANES : (side + 1) * LANES]
            own_pre[side, :, cols] = value
            send_pre[side, :, cols] = value.astype(BF)


def first_pre_kernel(dims, place_ref, loaded_ref, own_rows, own_target, own_gates, other_ref,
                     gate_head, up_head, gate_rest, up_rest,
                     rows_ref, target_ref, gates_ref, own_pre, send_pre, wide):
    n_dp, half, cap, blocks, unit = dims
    peers = n_dp * half
    core = core_of(place_ref)

    def begin(c, side):
        return pl.ds(pl.multiple_of((2 * c + side) * peers, peers), peers)

    for c in range(cap):
        here = slice(c * peers, (c + 1) * peers)
        for own, full in ((own_rows, rows_ref), (own_target, target_ref), (own_gates, gates_ref)):
            full[begin(c, core), :] = own[here, :]
    there = lambda c: begin(c, 1 - core)
    lay_out(dims, place_ref, other_ref, wide, there, rows_ref, target_ref, gates_ref)
    partial_pre(rows_ref, gate_head, up_head, (), 0, own_pre, send_pre)
    partial_pre(rows_ref, gate_rest, up_rest, (), gate_head.shape[1], own_pre, send_pre)


def more_pre_kernel(start, rows_ref, gate_hbm, up_hbm, turned_ref, own_pre, send_pre, gate_w, up_w, sems):
    copies = fetch_columns((start, start + own_pre.shape[2]), gate_hbm, up_hbm, gate_w, up_w, sems)
    turned_ref[...] = rows_ref[...].T
    partial_pre(rows_ref, gate_w, up_w, copies, 0, own_pre, send_pre)


def down_side(dims, start, place_ref, hidden, down_w, total_ref, side, out_ref):
    n_dp, half, cap, blocks, unit = dims
    rows, hid = hidden.shape
    quarter = half // 4
    core = core_of(place_ref) if side == 0 else 1 - core_of(place_ref)
    for k in range(4):
        quad = quad_of(place_ref, k)
        for j in range(0, quarter, 2):
            lo = (core * half + quad * quarter + j) * LANES
            cols = pl.ds(pl.multiple_of(lo, 2 * LANES), 2 * LANES)
            value = dot_nn(hidden[...], down_w[start : start + hid, cols])
            for n in range(2):
                part = value[:, n * LANES : (n + 1) * LANES]
                block = k * quarter + j + n
                if total_ref is not None:
                    both = side * half + block
                    part = part + total_ref[both * rows : (both + 1) * rows, :]
                out_ref[block * rows : (block + 1) * rows, :] = part.astype(out_ref.dtype)


def activate(own_ref, got_ref, up_deriv, act_ref, hidden):
    gate_pre = own_ref[0] + got_ref[0].astype(F32)
    up_pre = own_ref[1] + got_ref[1].astype(F32)
    sig = jax.nn.sigmoid(gate_pre)
    act = sig * gate_pre
    act_ref[...] = act
    up_deriv[...] = up_pre * (sig * (1.0 + gate_pre * (1.0 - sig)))
    hidden[...] = (act * up_pre).astype(BF)


def first_down_kernel(dims, start, place_ref, own_ref, got_ref, down_w, up_deriv, act_ref, total_ref, hidden):
    activate(own_ref, got_ref, up_deriv, act_ref, hidden)
    size = dims[1] * hidden.shape[0]
    for side in range(2):
        part = total_ref.at[side * size : (side + 1) * size]
        down_side(dims, start, place_ref, hidden, down_w, None, side, part)


def send_down_kernel(dims, start, place_ref, own_ref, got_ref, down_w, total_ref, up_deriv, act_ref, hidden, send_ref):
    activate(own_ref, got_ref, up_deriv, act_ref, hidden)
    down_side(dims, start, place_ref, hidden, down_w, total_ref, 1, send_ref)


def keep_down_kernel(dims, start, place_ref, hidden, down_w, total_ref, keep_ref):
    down_side(dims, start, place_ref, hidden, down_w, total_ref, 0, keep_ref)


def chip_sum_kernel(own_ref, got_ref, keep_ref, *send_refs):
    size = keep_ref.shape[0]
    for k, ref in enumerate((keep_ref, *send_refs)):
        at = slice(k * size, (k + 1) * size)
        ref[...] = (own_ref[at, :] + got_ref[at, :].astype(F32)).astype(ref.dtype)


def residual_kernel(place_ref, own_ref, first_ref, second_ref, third_ref, gates_ref, target_ref, keep_ref, send_ref):
    rows = target_ref.shape[0]
    for z in range(own_ref.shape[0] // rows):
        at = slice(z * rows, (z + 1) * rows)
        value = own_ref[at, :] + first_ref[at, :].astype(F32)
        value = value + (second_ref[at, :].astype(F32) + third_ref[at, :].astype(F32))
        value = gates_ref[...] * value
        value = jnp.where(rest_of(place_ref) == z, value - target_ref[...], value)
        keep_ref[at, :] = value
        send_ref[at, :] = value.astype(BF)


def line_sum_kernel(own_ref, got_ref, keep_ref, send_ref):
    value = own_ref[...] + got_ref[...].astype(F32)
    keep_ref[...] = value
    send_ref[...] = value.astype(BF)


def cotangent_kernel(own_ref, got_ref, gates_ref, out_ref):
    rows = gates_ref.shape[0]
    for z in range(own_ref.shape[0] // rows):
        at = slice(z * rows, (z + 1) * rows)
        out_ref[at, :] = (gates_ref[...] * (own_ref[at, :] + got_ref[at, :].astype(F32))).astype(BF)


def gather_blocks(refs, out):
    rows = out.shape[0]
    parts = refs[0].shape[0] // rows
    for k, ref in enumerate(refs):
        for h in range(parts):
            lo = (k * parts + h) * LANES
            out[:, lo : lo + LANES] = ref[h * rows : (h + 1) * rows, :]


def quad_grad_hidden(cot, core, quads, down_w, start, total_ref, outs):
    width = cot.shape[1] // len(quads)
    size = outs[0].shape[1]
    for lo in range(0, size, 2 * LANES):
        here = slice(lo, min(lo + 2 * LANES, size))
        there = slice(start + here.start, start + here.stop)
        value = total_ref[:, there] if total_ref is not None else None
        for k, quad in enumerate(quads):
            cols = pl.ds(pl.multiple_of((4 * core + quad) * width, width), width)
            part = dot_nt(cot[:, k * width : (k + 1) * width], down_w[there, cols])
            value = part if value is None else value + part
        for out in outs:
            out[:, here] = value.astype(out.dtype)


def near_grad_hidden_kernel(flip, flips, place_ref, down_w, *refs):
    got_refs, rest = refs[: len(flips)], refs[len(flips) :]
    *total_ref, out_ref, cot = rest
    core = 1 - core_of(place_ref) if flip else core_of(place_ref)
    quads = [quad_of(place_ref, k) for k in flips]
    gather_blocks(got_refs, cot)
    quad_grad_hidden(cot, core, quads, down_w, 0, total_ref[0] if total_ref else None, (out_ref,))


def first_grad_hidden_kernel(start, place_ref, first_ref, second_ref, third_ref, down_w, total_ref, cot, own_out, send_out):
    gather_blocks((first_ref, second_ref, third_ref), cot)
    quads = [quad_of(place_ref, k) for k in (1, 2, 3)]
    quad_grad_hidden(cot, 1 - core_of(place_ref), quads, down_w, start, total_ref, (own_out, send_out))


def more_grad_hidden_kernel(start, place_ref, cot, down_w, total_ref, own_out, send_out):
    quads = [quad_of(place_ref, k) for k in (1, 2, 3)]
    quad_grad_hidden(cot, 1 - core_of(place_ref), quads, down_w, start, total_ref, (own_out, send_out))


def row_grad_kernel(dims, start, last, place_ref, own_ref, got_ref, up_deriv, act_ref, gate_w, up_w, *refs):
    n_dp, half, cap, blocks, unit = dims
    sources = 2 * n_dp * half
    refs = list(refs)
    total_ref = refs.pop(0) if last else None
    gate_out, up_out, *out_refs = refs
    grad_hidden = own_ref[...] + got_ref[...].astype(F32)
    gate_out[...] = (grad_hidden * up_deriv[...]).astype(BF)
    up_out[...] = (grad_hidden * act_ref[...]).astype(BF)
    hid = gate_out.shape[1]
    wide = out_refs[-1]

    def column(j, _):
        at = pl.ds(pl.multiple_of(j * 2 * LANES, 2 * LANES), 2 * LANES)
        value = dot_nt(gate_out[...], gate_w[at, start : start + hid])
        value = value + dot_nt(up_out[...], up_w[at, start : start + hid])
        if total_ref is not None:
            value = value + total_ref[:, at]
        if not last:
            wide[:, at] = value
            return 0
        for k in range(2):
            for c in range(cap):
                piece = value[c * sources : (c + 1) * sources, k * LANES : (k + 1) * LANES]
                wide[pl.ds((2 * j + k) * cap + c, sources, stride=blocks * cap), :] = piece
        return 0

    lax.fori_loop(0, blocks // 2, column, 0, unroll=True)
    if last:
        keep_ref, send_ref, _ = out_refs
        size = keep_ref.shape[0]
        core = core_of(place_ref)
        keep_ref[...] = wide[pl.ds(pl.multiple_of(core * size, size), size), :]
        send_ref[...] = wide[pl.ds(pl.multiple_of((1 - core) * size, size), size), :].astype(BF)


def weight_grad_kernel(parts, tile, turned_ref, *refs):
    grads = (refs[:parts], refs[parts : 2 * parts])
    outs, values, sems = refs[2 * parts : 2 * parts + 2], refs[2 * parts + 2 : 2 * parts + 4], refs[-1]
    copies = []
    for t in range(turned_ref.shape[0] // tile):
        at = slice(t * tile, (t + 1) * tile)
        for side in range(2):
            lo = 0
            for ref in grads[side]:
                size = ref.shape[1]
                values[side][at, lo : lo + size] = dot_nn(turned_ref[at, :], ref[...]).astype(BF)
                lo += size
            copies.append(pltpu.make_async_copy(values[side].at[at, :], outs[side].at[at, :], sems.at[t, side]))
            copies[-1].start()
    for copy in copies:
        copy.wait()


def token_grad_kernel(dims, pick_ref, got_ref, out_hbm, rows, out, sems):
    n_dp, half, cap, blocks, unit = dims
    size = blocks * cap
    width = blocks * LANES
    pick = pick_ref[...]
    rows[...] = jnp.zeros_like(rows)
    copies = []
    for d in range(n_dp):
        total = got_ref[d * half * size : (d * half + 1) * size, :].astype(F32)
        for h in range(1, half):
            base = (d * half + h) * size
            total = total + got_ref[base : base + size, :].astype(F32)
        for q in range(blocks):
            rows[0:cap, q * LANES : (q + 1) * LANES] = total[q * cap : (q + 1) * cap, :]
        cols = slice(d * width, (d + 1) * width)
        out[:, cols] = dot_tn(pick, rows[...].astype(BF)).astype(out.dtype)
        copies.append(pltpu.make_async_copy(out.at[:, cols], out_hbm.at[:, cols], sems.at[d]))
        copies[-1].start()
    for copy in copies:
        copy.wait()


def fast_shards(n_dp, n_expert, cap, tokens, expert_ids, gate_values, w_gate, w_up, w_down, target):
    tok_rows, features = tokens.shape
    width, hid = w_gate.shape
    half = n_expert // 2
    blocks = width // LANES
    peers = n_dp * half
    sources = 2 * peers
    rows = cap * sources
    unit = -(-(blocks + 2 + GATE_PIECES) * cap // 16) * 16
    dims = (n_dp, half, cap, blocks, unit)
    place = lax.axis_index("expert").astype(jnp.int32).reshape(1)
    ids = expert_ids.T
    slice_groups = [
        [d * n_expert + 2 * h + c for d in range(n_dp) for h in range(half)] for c in range(2)
    ]

    def other(x, mask):
        return lax.ppermute(x, "expert", [(i, i ^ mask) for i in range(n_expert)])

    def other_core(x):
        return other(x, 1)

    def other_dp(x):
        return lax.ppermute(x, "dp", [(0, 1), (1, 0)])

    def over_slice(x):
        return lax.all_to_all(x, ("dp", "expert"), 0, 0, axis_index_groups=slice_groups, tiled=True)

    outgoing, pick = call(
        functools.partial(route_kernel, dims),
        (sds((peers * unit, LANES), BF), sds((16, tok_rows), BF)),
        in_hbm(ids, gate_values.T, tokens, target),
        [HBM] * 4,
        [
            pltpu.VMEM(ids.shape, ids.dtype),
            pltpu.VMEM(ids.shape, F32),
            pltpu.VMEM(tokens.shape, tokens.dtype),
            pltpu.VMEM(target.shape, target.dtype),
            pltpu.VMEM((16, width), F32),
            pltpu.VMEM((16, width), F32),
            pltpu.VMEM((blocks * cap, LANES), F32),
            pltpu.VMEM((unit - blocks * cap, LANES), F32),
            pltpu.SemaphoreType.DMA((2 + 2 * n_dp,)),
        ],
        name="route",
    )
    first = -(-hid // (2 * LANES)) * LANES
    head = 2 * LANES

    def columns(size):
        return sds((width, size), w_gate.dtype), sds((width, size), w_up.dtype)

    def column_sems(size):
        return pltpu.SemaphoreType.DMA((-(-size // (2 * LANES)), 2))

    loaded, *weights = call(
        load_kernel,
        (sds((8, LANES), F32), *columns(head)),
        in_hbm(w_gate, w_up),
        [HBM] * 2,
        [column_sems(head)],
        flops=1_000_000_000,
        moved=8 * width * head,
        name="load_weights",
    )
    own, loaded = lax.optimization_barrier((over_slice(outgoing), loaded))
    *more, own_rows, own_target, own_gates = call(
        functools.partial(load_more_kernel, dims, head),
        (
            *columns(first - head),
            sds((cap * peers, width), BF),
            sds((cap * peers, LANES), F32),
            sds((cap * peers, LANES), F32),
        ),
        (place, own, *in_hbm(w_gate, w_up)),
        [SMEM, VMEM] + [HBM] * 2,
        [pltpu.VMEM((peers * unit, LANES), F32), column_sems(first - head)],
        flops=1_000_000_000,
        moved=8 * width * head,
        name="load_weights",
    )
    weights += more
    neighbour = other_core(own)
    chunks = [(0, first), (first, hid - first)]
    pres = []
    for start, size in chunks:
        outs = (sds((2, rows, size), F32), sds((2, rows, size), BF))
        cost = dict(flops=8 * rows * width * size, moved=4 * width * size)
        fetched = [
            pltpu.VMEM((width, size), w_gate.dtype),
            pltpu.VMEM((width, size), w_up.dtype),
            column_sems(size),
        ]
        if start == 0:
            all_rows, all_target, all_gates, *pre = call(
                functools.partial(first_pre_kernel, dims),
                (sds((rows, width), BF), sds((rows, LANES), F32), sds((rows, LANES), F32), *outs),
                (place, loaded, own_rows, own_target, own_gates, neighbour, *weights),
                [SMEM] + [VMEM] * 9,
                [pltpu.VMEM((peers * unit, LANES), F32)],
                name="pre_activations",
                **cost,
            )
        else:
            turned, *pre = call(
                functools.partial(more_pre_kernel, start),
                (sds((width, rows), BF), *outs),
                (all_rows, *in_hbm(w_gate, w_up)),
                [VMEM] + [HBM] * 2,
                fetched,
                name="pre_activations",
                **cost,
            )
        pres.append((pre[0], other_dp(pre[1])))
    (start, size), (start_b, size_b) = chunks
    half_rows = half * rows
    cost = dict(flops=4 * rows * width * size, moved=2 * width * size)
    up_deriv, act, total = call(
        functools.partial(first_down_kernel, dims, start),
        (sds((rows, size), F32), sds((rows, size), F32), sds((2 * half_rows, LANES), F32)),
        (place, *pres[0], w_down),
        [SMEM] + [VMEM] * 3,
        [pltpu.VMEM((rows, size), BF)],
        name="down",
        **cost,
    )
    up_deriv_b, act_b, hidden_b, send = call(
        functools.partial(send_down_kernel, dims, start_b),
        (
            sds((rows, size_b), F32),
            sds((rows, size_b), F32),
            sds((rows, size_b), BF),
            sds((half_rows, LANES), BF),
        ),
        (place, *pres[1], w_down, total),
        [SMEM] + [VMEM] * 4,
        name="down_send",
        **cost,
    )
    sent = other_core(send)
    keep = call(
        functools.partial(keep_down_kernel, dims, start_b),
        sds((half_rows, LANES), F32),
        (place, hidden_b, w_down, total),
        [SMEM] + [VMEM] * 3,
        name="down_keep",
        **cost,
    )
    saved = [(up_deriv, act), (up_deriv_b, act_b)]
    quad_rows = half_rows // 4
    kept, sent_on = sds((quad_rows, LANES), F32), sds((quad_rows, LANES), BF)
    keep, *sends = call(chip_sum_kernel, (kept, *[sent_on] * 3), (keep, sent), [VMEM] * 2, name="chip_sum")
    keep, send = call(
        residual_kernel,
        (kept, sent_on),
        (place, keep, *[other(sends[k], 2 * (k + 1)) for k in (2, 0, 1)], all_gates, all_target),
        [SMEM] + [VMEM] * 6,
        name="residual",
    )
    step = 8
    while 2 * step < n_expert:
        keep, send = call(line_sum_kernel, (kept, sent_on), (keep, other(send, step)), [VMEM] * 2, name="line_sum")
        step *= 2
    cot = call(
        cotangent_kernel,
        sent_on,
        (keep, other(send, step), all_gates),
        [VMEM] * 3,
        name="cotangent",
    )
    from_quad = [other(cot, 2 * k) for k in (1, 2, 3)]
    from_core = other_core(cot)

    def near(flip, flips, got, *total):
        return call(
            functools.partial(near_grad_hidden_kernel, flip, flips),
            sds((rows, hid), F32),
            (place, w_down, *got, *total),
            [SMEM] + [VMEM] * (1 + len(got) + len(total)),
            [pltpu.VMEM((rows, len(got) * quad_rows // rows * LANES), BF)],
            flops=len(got) * rows * width * hid // 4,
            moved=len(got) * width * hid // 4,
            name="grad_hidden_near",
        )

    own_total = near(0, (0,), (cot,))
    own_total = near(1, (0,), (from_core,), own_total)
    from_quad[2], own_total = lax.optimization_barrier((from_quad[2], own_total))
    from_both = [other_core(x) for x in from_quad]
    own_total = near(0, (1, 2, 3), from_quad, own_total)
    grads = []
    order = [1, 0]
    for k in order:
        start, size = chunks[k]
        outs = (sds((rows, size), F32), sds((rows, size), BF))
        cost = dict(flops=2 * rows * width * size, moved=2 * width * size)
        if k == order[0]:
            cot, *grad = call(
                functools.partial(first_grad_hidden_kernel, start),
                (sds((rows, 3 * width // 8), BF), *outs),
                (place, *from_both, w_down, own_total),
                [SMEM] + [VMEM] * 5,
                name="grad_hidden",
                **cost,
            )
        else:
            grad = call(
                functools.partial(more_grad_hidden_kernel, start),
                outs,
                (place, cot, w_down, own_total),
                [SMEM] + [VMEM] * 3,
                name="grad_hidden",
                **cost,
            )
        grads.append((grad[0], other_dp(grad[1])))
    pre_grads = [None] * len(chunks)
    total = ()
    peer_rows = peers * blocks * cap
    for k, grad in zip(order, grads):
        start, size = chunks[k]
        outs, scratch = (sds((rows, width), F32),), []
        if k == order[-1]:
            outs = (sds((peer_rows, LANES), F32), sds((peer_rows, LANES), BF))
            scratch = [pltpu.VMEM((2 * peer_rows, LANES), F32)]
        gate_pre_grad, up_pre_grad, *total = call(
            functools.partial(row_grad_kernel, dims, start, k == order[-1]),
            (sds((rows, size), BF), sds((rows, size), BF), *outs),
            (place, *grad, *saved[k], w_gate, w_up, *total),
            [SMEM] + [VMEM] * (6 + len(total)),
            scratch,
            flops=8 * rows * width * size,
            moved=4 * width * size,
            name="row_grad",
        )
        pre_grads[k] = (gate_pre_grad, up_pre_grad)
    keep, send = total
    chip_rows = add_cores(keep, other_core(send))
    got_rows = over_slice(chip_rows)
    pre_grads = [pair[0] for pair in pre_grads] + [pair[1] for pair in pre_grads]
    tile = 256
    gate_grad, up_grad = call(
        functools.partial(weight_grad_kernel, len(chunks), tile),
        (sds((width, hid), BF), sds((width, hid), BF)),
        (turned, *pre_grads),
        [VMEM] * (1 + len(pre_grads)),
        [
            pltpu.VMEM((width, hid), BF),
            pltpu.VMEM((width, hid), BF),
            pltpu.SemaphoreType.DMA((width // tile, 2)),
        ],
        flops=4 * rows * width * hid,
        moved=4 * width * hid,
        out_spec=HBM,
        name="weight_grads",
    )
    token_grad = call(
        functools.partial(token_grad_kernel, dims),
        sds((tok_rows, features), tokens.dtype),
        (pick, got_rows),
        [VMEM] * 2,
        [
            pltpu.VMEM((16, width), F32),
            pltpu.VMEM((tok_rows, features), tokens.dtype),
            pltpu.SemaphoreType.DMA((n_dp,)),
        ],
        out_spec=HBM,
        name="token_grad",
    )
    return token_grad, gate_grad, up_grad


def contract_last(matrix_a, matrix_b):
    return lax.dot_general(
        matrix_a, matrix_b, (((1,), (1,)), ((), ())), preferred_element_type=jnp.float32
    )


def rounded_terms(column_blocks, grad_blocks):
    terms = jnp.einsum(
        "krd,krh->kdh", column_blocks, grad_blocks, preferred_element_type=jnp.float32
    )
    terms = lax.optimization_barrier(terms.astype(jnp.bfloat16))
    return jnp.sum(terms.astype(jnp.float32), axis=0)


def spread_rows(rows, group_size, capacity, features):
    flat = rows.reshape(EXPERTS, 1, capacity * features)
    wide = jnp.broadcast_to(flat, (EXPERTS, group_size, capacity * features))
    return wide.reshape(EXPERTS * group_size * capacity, features)


def fold_group(rows, group_size, capacity, features):
    shaped = rows.reshape(EXPERTS, group_size, capacity * features).astype(jnp.float32)
    return jnp.sum(shaped, axis=1).reshape(EXPERTS * capacity, features)


def general_shards(tokens, expert_ids, gate_values, w_gate, w_up, w_down, target):
    devices_along = lax.axis_size("expert")
    group_size = devices_along // EXPERTS
    tok_rows = tokens.shape[0]
    features = tokens.shape[1]
    hid_local = w_gate.shape[1]
    capacity = max(2, 3 * tok_rows // 128)
    slot_total = EXPERTS * capacity
    flat_ids = expert_ids.reshape(-1)
    pair_count = flat_ids.shape[0]
    window = flat_ids < EXPERTS
    onehot = (flat_ids[:, None] == jnp.arange(EXPERTS, dtype=jnp.int32)[None, :]).astype(jnp.int32)
    slot_index = jnp.sum((jnp.cumsum(onehot, axis=0) - onehot) * onehot, axis=1)
    position = jnp.where(window, flat_ids * capacity + slot_index, slot_total)
    owning = jnp.arange(pair_count, dtype=jnp.int32) // 2
    slot_token = jnp.zeros((slot_total + 1,), jnp.int32).at[position].set(owning)[:slot_total]
    slot_live = jnp.zeros((slot_total + 1,), jnp.bool_).at[position].set(True)[:slot_total]
    slot_gate = (
        jnp.zeros((slot_total + 1,), jnp.float32)
        .at[position]
        .set(gate_values.reshape(-1))[:slot_total]
    )
    safe_pairs = jnp.minimum(position, slot_total - 1).reshape(tok_rows, 2)
    live_pairs = window.reshape(tok_rows, 2)

    def pick(table, column):
        return jnp.where(live_pairs[:, column : column + 1], table[safe_pairs[:, column]], 0.0)

    outgoing = jnp.where(slot_live[:, None], tokens[slot_token], jnp.zeros((), tokens.dtype))
    outgoing = spread_rows(outgoing, group_size, capacity, features)
    received = lax.all_to_all(outgoing, "expert", split_axis=0, concat_axis=0, tiled=True)
    rows_count = received.shape[0]
    full_gate, full_up, full_down = (
        lax.all_gather(w_gate, "dp", axis=0, tiled=True),
        lax.all_gather(w_up, "dp", axis=0, tiled=True),
        lax.all_gather(w_down, "dp", axis=1, tiled=True),
    )
    gate_pre = jnp.dot(received, full_gate, preferred_element_type=jnp.float32)
    up_pre = jnp.dot(received, full_up, preferred_element_type=jnp.float32)
    sigmoid_gate = jax.nn.sigmoid(gate_pre)
    activated = sigmoid_gate * gate_pre
    hidden = (activated * up_pre).astype(jnp.bfloat16)
    partial_out = jnp.dot(hidden, full_down, preferred_element_type=jnp.float32).astype(
        jnp.bfloat16
    )
    returned_out = lax.all_to_all(partial_out, "expert", split_axis=0, concat_axis=0, tiled=True)
    expert_out = fold_group(returned_out, group_size, capacity, features)
    combined = gate_values[:, 0:1] * pick(expert_out, 0) + gate_values[:, 1:2] * pick(expert_out, 1)
    residual = combined - target.astype(jnp.float32)
    outgoing_grad = jnp.where(
        slot_live[:, None], slot_gate[:, None] * residual[slot_token], 0.0
    ).astype(jnp.bfloat16)
    outgoing_grad = spread_rows(outgoing_grad, group_size, capacity, features)
    cotangent = lax.all_to_all(outgoing_grad, "expert", split_axis=0, concat_axis=0, tiled=True)
    grad_hidden = contract_last(cotangent, full_down)
    derivative = sigmoid_gate * (1.0 + gate_pre * (1.0 - sigmoid_gate))
    grad_gate_pre = (grad_hidden * up_pre * derivative).astype(jnp.bfloat16)
    grad_up_pre = (grad_hidden * activated).astype(jnp.bfloat16)
    row_part = (
        contract_last(grad_gate_pre, full_gate) + contract_last(grad_up_pre, full_up)
    ).astype(jnp.bfloat16)
    back_rows = lax.all_to_all(row_part, "expert", split_axis=0, concat_axis=0, tiled=True)
    row_grad = fold_group(back_rows, group_size, capacity, features)
    token_grad = (pick(row_grad, 0) + pick(row_grad, 1)).astype(jnp.bfloat16)
    shard_columns = lax.all_to_all(received, "dp", split_axis=1, concat_axis=0, tiled=True)
    shard_width = shard_columns.shape[1]
    dp_count = lax.axis_size("dp")
    every_gate, every_up = (
        lax.all_gather(grad_gate_pre, "dp", axis=0, tiled=True),
        lax.all_gather(grad_up_pre, "dp", axis=0, tiled=True),
    )
    column_blocks = shard_columns.reshape(dp_count, rows_count, shard_width)
    gate_sum = rounded_terms(column_blocks, every_gate.reshape(dp_count, rows_count, hid_local))
    up_sum = rounded_terms(column_blocks, every_up.reshape(dp_count, rows_count, hid_local))
    return (token_grad, gate_sum.astype(jnp.bfloat16), up_sum.astype(jnp.bfloat16))


def solution(mesh):
    n_dp, n_expert = mesh.shape["dp"], mesh.shape["expert"]

    def shards(*args):
        tok_rows, features = args[0].shape
        width, hid = args[3].shape
        cap = max(2, 3 * tok_rows // 128)
        whole_blocks = (
            n_dp == 2
            and n_expert % 16 == 0
            and n_expert & (n_expert - 1) == 0
            and width == n_expert * LANES
            and hid % LANES == 0
            and hid > 4 * LANES
            and cap <= 8
            and tok_rows % LANES == 0
        )
        if whole_blocks:
            return fast_shards(n_dp, n_expert, cap, *args)
        return general_shards(*args)

    placed = (
        P(("dp", "expert"), None),
        P(("dp", "expert"), None),
        P(("dp", "expert"), None),
        P("dp", "expert"),
        P("dp", "expert"),
        P("expert", "dp"),
        P(("dp", "expert"), None),
    )
    return jax.shard_map(
        shards,
        mesh=mesh,
        in_specs=placed,
        out_specs=(P(("dp", "expert"), None), P("dp", "expert"), P("dp", "expert")),
        check_vma=False,
    )
```

```python
import functools

import jax
import jax.numpy as jnp
from jax import lax
from jax.experimental import pallas as pl
from jax.experimental.pallas import tpu as pltpu
from jax.sharding import PartitionSpec as P

EXPERTS = 1
LANES = 128
GATE_PIECES = 3
BF = jnp.bfloat16
F32 = jnp.float32
VMEM = pl.BlockSpec(memory_space=pltpu.VMEM)
HBM = pl.BlockSpec(memory_space=pltpu.HBM)
SMEM = pl.BlockSpec(memory_space=pltpu.SMEM)


def sds(shape, dtype):
    return jax.ShapeDtypeStruct(shape, dtype)


def dot_nn(a, b):
    return lax.dot_general(a, b, (((1,), (0,)), ((), ())), preferred_element_type=F32)


def dot_nt(a, b):
    return lax.dot_general(a, b, (((1,), (1,)), ((), ())), preferred_element_type=F32)


def dot_tn(a, b):
    return lax.dot_general(a, b, (((0,), (0,)), ((), ())), preferred_element_type=F32)


def in_hbm(*arrays):
    return tuple(pltpu.with_memory_space_constraint(x, pltpu.HBM) for x in arrays)


def core_of(place_ref):
    return place_ref[0] & 1


def quad_of(place_ref, k=0):
    x, low = (place_ref[0] >> 1) & 1, (place_ref[0] >> 2) & 1
    return (1 - x if k & 1 else x) + 2 * (1 - low if k & 2 else low)


def rest_of(place_ref):
    return place_ref[0] >> 3


def call(body, outs, args, specs, scratch=(), limit=16, flops=0, moved=0, name=None, out_spec=VMEM):
    return pl.pallas_call(
        body,
        out_shape=outs,
        in_specs=specs,
        out_specs=jax.tree.map(lambda _: out_spec, outs),
        scratch_shapes=list(scratch),
        compiler_params=pltpu.CompilerParams(vmem_limit_bytes=limit << 20),
        cost_estimate=pl.CostEstimate(flops=flops, bytes_accessed=moved, transcendentals=0),
        name=name,
    )(*args)


def select_rows(ids_ref):
    tok_rows = ids_ref.shape[1]
    live = jnp.sum((ids_ref[...] < EXPERTS).astype(F32), axis=0, keepdims=True)
    before = lax.broadcasted_iota(jnp.int32, (tok_rows, tok_rows), 0)
    after = lax.broadcasted_iota(jnp.int32, (tok_rows, tok_rows), 1)
    earlier = (before < after).astype(BF)
    wide = jnp.broadcast_to(live, (16, tok_rows))
    slot = dot_nn(wide.astype(BF), earlier)
    wanted = lax.broadcasted_iota(jnp.int32, (16, tok_rows), 0).astype(F32)
    return jnp.where(slot == wanted, wide, 0.0)


def add_kernel(own_ref, got_ref, out_ref):
    out_ref[...] = (own_ref[...] + got_ref[...].astype(F32)).astype(out_ref.dtype)


def add_cores(own, got):
    return call(add_kernel, sds(got.shape, got.dtype), (own, got), [VMEM] * 2, name="add_cores")


def route_kernel(dims, ids_hbm, gates_hbm, tokens_hbm, target_hbm, out_ref, pick_ref,
                 ids_ref, gates_ref, tokens_ref, target_ref, tok, tgt, head, tail, sems):
    n_dp, half, cap, blocks, unit = dims
    width = blocks * LANES
    pairs = [(ids_hbm, ids_ref), (gates_hbm, gates_ref)]
    for hbm, ref in ((tokens_hbm, tokens_ref), (target_hbm, target_ref)):
        for d in range(n_dp):
            cols = slice(d * width, (d + 1) * width)
            pairs.append((hbm.at[:, cols], ref.at[:, cols]))
    copies = [pltpu.make_async_copy(src, dst, sems.at[i]) for i, (src, dst) in enumerate(pairs)]
    for copy in copies:
        copy.start()
    tail[...] = jnp.zeros_like(tail)
    copies[0].wait()
    copies[1].wait()
    chosen = select_rows(ids_ref)
    live_gates = jnp.sum(jnp.where(ids_ref[...] < EXPERTS, gates_ref[...], 0.0), axis=0, keepdims=True)
    gate = jnp.sum(chosen * live_gates, axis=1, keepdims=True)
    pick = chosen.astype(BF)
    pick_ref[...] = pick
    rest = gate
    for piece in range(GATE_PIECES):
        part = rest.astype(BF).astype(F32)
        rest = rest - part
        at = (2 + piece) * cap
        tail[at : at + cap, :] = jnp.broadcast_to(part[0:cap], (cap, LANES))
    lead = blocks * cap
    for d in range(n_dp):
        cols = slice(d * width, (d + 1) * width)
        copies[2 + d].wait()
        tok[...] = dot_nn(pick, tokens_ref[:, cols])
        for q in range(blocks):
            head[q * cap : (q + 1) * cap, :] = tok[0:cap, q * LANES : (q + 1) * LANES]
        packed = head[...].astype(BF)
        for h in range(half):
            base = (d * half + h) * unit
            out_ref[base : base + lead, :] = packed
    for d in range(n_dp):
        cols = slice(d * width, (d + 1) * width)
        copies[2 + n_dp + d].wait()
        tgt[...] = dot_nn(pick, target_ref[:, cols])
        for h in range(half):
            for core in range(2):
                lo = (core * half + h % 4 * (half // 4) + h // 4) * LANES
                tail[core * cap : (core + 1) * cap, :] = tgt[0:cap, lo : lo + LANES]
            base = (d * half + h) * unit
            out_ref[base + lead : base + unit, :] = tail[...].astype(BF)


def lay_out(dims, place_ref, src_ref, wide, begin, rows_ref, target_ref, gates_ref):
    n_dp, half, cap, blocks, unit = dims
    peers = n_dp * half
    wide[...] = src_ref[...].astype(F32)

    def one(k):
        return wide[pl.ds(k, peers, stride=unit), :]

    for c in range(cap):
        at = begin(c)
        for q in range(blocks):
            rows_ref[at, q * LANES : (q + 1) * LANES] = one(q * cap + c).astype(BF)
        base = blocks * cap
        target_ref[at, :] = jnp.where(core_of(place_ref) == 0, one(base + c), one(base + cap + c))
        gates_ref[at, :] = sum(one(base + (2 + piece) * cap + c) for piece in range(GATE_PIECES))


def fetch_columns(starts, gate_hbm, up_hbm, gate_w, up_w, sems):
    lo, hi = starts
    copies = []
    for k, at in enumerate(range(lo, hi, 2 * LANES)):
        count = min(2 * LANES, hi - at)
        pair = []
        for side, (src, dst) in enumerate(((gate_hbm, gate_w), (up_hbm, up_w))):
            part = src.at[:, pl.ds(at, count)]
            pair.append(pltpu.make_async_copy(part, dst.at[:, pl.ds(at - lo, count)], sems.at[k, side]))
            pair[-1].start()
        copies.append(pair)
    return copies


def load_kernel(gate_hbm, up_hbm, done_ref, gate_w, up_w, sems):
    copies = fetch_columns((0, gate_w.shape[1]), gate_hbm, up_hbm, gate_w, up_w, sems)
    done_ref[...] = jnp.zeros_like(done_ref)
    for pair in copies:
        for copy in pair:
            copy.wait()


def load_more_kernel(dims, start, place_ref, own_ref, gate_hbm, up_hbm, gate_w, up_w,
                     rows_ref, target_ref, gates_ref, wide, sems):
    peers = dims[0] * dims[1]
    copies = fetch_columns((start, start + gate_w.shape[1]), gate_hbm, up_hbm, gate_w, up_w, sems)
    begin = lambda c: slice(c * peers, (c + 1) * peers)
    lay_out(dims, place_ref, own_ref, wide, begin, rows_ref, target_ref, gates_ref)
    for pair in copies:
        for copy in pair:
            copy.wait()


def partial_pre(rows_ref, gate_w, up_w, copies, first, own_pre, send_pre):
    for j in range(gate_w.shape[1] // LANES):
        if copies and j % 2 == 0:
            for copy in copies[j // 2]:
                copy.wait()
        here = slice(j * LANES, (j + 1) * LANES)
        cols = slice(first + j * LANES, first + (j + 1) * LANES)
        pair = jnp.concatenate([gate_w[:, here], up_w[:, here]], axis=1)
        both = dot_nn(rows_ref[...], pair)
        for side in range(2):
            value = both[:, side * LANES : (side + 1) * LANES]
            own_pre[side, :, cols] = value
            send_pre[side, :, cols] = value.astype(BF)


def first_pre_kernel(dims, place_ref, loaded_ref, own_rows, own_target, own_gates, other_ref,
                     gate_head, up_head, gate_rest, up_rest,
                     rows_ref, target_ref, gates_ref, own_pre, send_pre, wide):
    n_dp, half, cap, blocks, unit = dims
    peers = n_dp * half
    core = core_of(place_ref)

    def begin(c, side):
        return pl.ds(pl.multiple_of((2 * c + side) * peers, peers), peers)

    for c in range(cap):
        here = slice(c * peers, (c + 1) * peers)
        for own, full in ((own_rows, rows_ref), (own_target, target_ref), (own_gates, gates_ref)):
            full[begin(c, core), :] = own[here, :]
    there = lambda c: begin(c, 1 - core)
    lay_out(dims, place_ref, other_ref, wide, there, rows_ref, target_ref, gates_ref)
    partial_pre(rows_ref, gate_head, up_head, (), 0, own_pre, send_pre)
    partial_pre(rows_ref, gate_rest, up_rest, (), gate_head.shape[1], own_pre, send_pre)


def more_pre_kernel(start, rows_ref, gate_hbm, up_hbm, turned_ref, own_pre, send_pre, gate_w, up_w, sems):
    copies = fetch_columns((start, start + own_pre.shape[2]), gate_hbm, up_hbm, gate_w, up_w, sems)
    turned_ref[...] = rows_ref[...].T
    partial_pre(rows_ref, gate_w, up_w, copies, 0, own_pre, send_pre)


def down_side(dims, start, place_ref, hidden, down_w, total_ref, side, out_ref):
    n_dp, half, cap, blocks, unit = dims
    rows, hid = hidden.shape
    quarter = half // 4
    core = core_of(place_ref) if side == 0 else 1 - core_of(place_ref)
    for k in range(4):
        quad = quad_of(place_ref, k)
        for j in range(0, quarter, 2):
            lo = (core * half + quad * quarter + j) * LANES
            cols = pl.ds(pl.multiple_of(lo, 2 * LANES), 2 * LANES)
            value = dot_nn(hidden[...], down_w[start : start + hid, cols])
            for n in range(2):
                part = value[:, n * LANES : (n + 1) * LANES]
                block = k * quarter + j + n
                if total_ref is not None:
                    both = side * half + block
                    part = part + total_ref[both * rows : (both + 1) * rows, :]
                out_ref[block * rows : (block + 1) * rows, :] = part.astype(out_ref.dtype)


def activate(own_ref, got_ref, up_deriv, act_ref, hidden):
    gate_pre = own_ref[0] + got_ref[0].astype(F32)
    up_pre = own_ref[1] + got_ref[1].astype(F32)
    sig = jax.nn.sigmoid(gate_pre)
    act = sig * gate_pre
    act_ref[...] = act
    up_deriv[...] = up_pre * (sig * (1.0 + gate_pre * (1.0 - sig)))
    hidden[...] = (act * up_pre).astype(BF)


def first_down_kernel(dims, start, place_ref, own_ref, got_ref, down_w, up_deriv, act_ref, total_ref, hidden):
    activate(own_ref, got_ref, up_deriv, act_ref, hidden)
    size = dims[1] * hidden.shape[0]
    for side in range(2):
        part = total_ref.at[side * size : (side + 1) * size]
        down_side(dims, start, place_ref, hidden, down_w, None, side, part)


def send_down_kernel(dims, start, place_ref, own_ref, got_ref, down_w, total_ref, up_deriv, act_ref, hidden, send_ref):
    activate(own_ref, got_ref, up_deriv, act_ref, hidden)
    down_side(dims, start, place_ref, hidden, down_w, total_ref, 1, send_ref)


def keep_down_kernel(dims, start, place_ref, hidden, down_w, total_ref, keep_ref):
    down_side(dims, start, place_ref, hidden, down_w, total_ref, 0, keep_ref)


def chip_sum_kernel(own_ref, got_ref, keep_ref, *send_refs):
    size = keep_ref.shape[0]
    for k, ref in enumerate((keep_ref, *send_refs)):
        at = slice(k * size, (k + 1) * size)
        ref[...] = (own_ref[at, :] + got_ref[at, :].astype(F32)).astype(ref.dtype)


def residual_kernel(place_ref, own_ref, first_ref, second_ref, third_ref, gates_ref, target_ref, keep_ref, send_ref):
    rows = target_ref.shape[0]
    for z in range(own_ref.shape[0] // rows):
        at = slice(z * rows, (z + 1) * rows)
        value = own_ref[at, :] + first_ref[at, :].astype(F32)
        value = value + (second_ref[at, :].astype(F32) + third_ref[at, :].astype(F32))
        value = gates_ref[...] * value
        value = jnp.where(rest_of(place_ref) == z, value - target_ref[...], value)
        keep_ref[at, :] = value
        send_ref[at, :] = value.astype(BF)


def line_sum_kernel(own_ref, got_ref, keep_ref, send_ref):
    value = own_ref[...] + got_ref[...].astype(F32)
    keep_ref[...] = value
    send_ref[...] = value.astype(BF)


def cotangent_kernel(own_ref, got_ref, gates_ref, out_ref):
    rows = gates_ref.shape[0]
    for z in range(own_ref.shape[0] // rows):
        at = slice(z * rows, (z + 1) * rows)
        out_ref[at, :] = (gates_ref[...] * (own_ref[at, :] + got_ref[at, :].astype(F32))).astype(BF)


def gather_blocks(refs, out):
    rows = out.shape[0]
    parts = refs[0].shape[0] // rows
    for k, ref in enumerate(refs):
        for h in range(parts):
            lo = (k * parts + h) * LANES
            out[:, lo : lo + LANES] = ref[h * rows : (h + 1) * rows, :]


def quad_grad_hidden(cot, core, quads, down_w, start, total_ref, outs):
    width = cot.shape[1] // len(quads)
    size = outs[0].shape[1]
    for lo in range(0, size, 2 * LANES):
        here = slice(lo, min(lo + 2 * LANES, size))
        there = slice(start + here.start, start + here.stop)
        value = total_ref[:, there] if total_ref is not None else None
        for k, quad in enumerate(quads):
            cols = pl.ds(pl.multiple_of((4 * core + quad) * width, width), width)
            part = dot_nt(cot[:, k * width : (k + 1) * width], down_w[there, cols])
            value = part if value is None else value + part
        for out in outs:
            out[:, here] = value.astype(out.dtype)


def near_grad_hidden_kernel(flip, flips, place_ref, down_w, *refs):
    got_refs, rest = refs[: len(flips)], refs[len(flips) :]
    *total_ref, out_ref, cot = rest
    core = 1 - core_of(place_ref) if flip else core_of(place_ref)
    quads = [quad_of(place_ref, k) for k in flips]
    gather_blocks(got_refs, cot)
    quad_grad_hidden(cot, core, quads, down_w, 0, total_ref[0] if total_ref else None, (out_ref,))


def first_grad_hidden_kernel(start, place_ref, first_ref, second_ref, third_ref, down_w, total_ref, cot, own_out, send_out):
    gather_blocks((first_ref, second_ref, third_ref), cot)
    quads = [quad_of(place_ref, k) for k in (1, 2, 3)]
    quad_grad_hidden(cot, 1 - core_of(place_ref), quads, down_w, start, total_ref, (own_out, send_out))


def more_grad_hidden_kernel(start, place_ref, cot, down_w, total_ref, own_out, send_out):
    quads = [quad_of(place_ref, k) for k in (1, 2, 3)]
    quad_grad_hidden(cot, 1 - core_of(place_ref), quads, down_w, start, total_ref, (own_out, send_out))


def row_grad_kernel(dims, start, last, place_ref, own_ref, got_ref, up_deriv, act_ref, gate_w, up_w, *refs):
    n_dp, half, cap, blocks, unit = dims
    sources = 2 * n_dp * half
    refs = list(refs)
    total_ref = refs.pop(0) if last else None
    gate_out, up_out, *out_refs = refs
    grad_hidden = own_ref[...] + got_ref[...].astype(F32)
    gate_out[...] = (grad_hidden * up_deriv[...]).astype(BF)
    up_out[...] = (grad_hidden * act_ref[...]).astype(BF)
    hid = gate_out.shape[1]
    wide = out_refs[-1]

    def column(j, _):
        at = pl.ds(pl.multiple_of(j * 2 * LANES, 2 * LANES), 2 * LANES)
        value = dot_nt(gate_w[at, start : start + hid], gate_out[...])
        value = (value + dot_nt(up_w[at, start : start + hid], up_out[...])).T
        if total_ref is not None:
            value = value + total_ref[:, at]
        if not last:
            wide[:, at] = value
            return 0
        for k in range(2):
            for c in range(cap):
                piece = value[c * sources : (c + 1) * sources, k * LANES : (k + 1) * LANES]
                wide[pl.ds((2 * j + k) * cap + c, sources, stride=blocks * cap), :] = piece
        return 0

    lax.fori_loop(0, blocks // 2, column, 0, unroll=True)
    if last:
        keep_ref, send_ref, _ = out_refs
        size = keep_ref.shape[0]
        core = core_of(place_ref)
        keep_ref[...] = wide[pl.ds(pl.multiple_of(core * size, size), size), :]
        send_ref[...] = wide[pl.ds(pl.multiple_of((1 - core) * size, size), size), :].astype(BF)


def weight_grad_kernel(parts, tile, turned_ref, *refs):
    grads = (refs[:parts], refs[parts : 2 * parts])
    outs, values, sems = refs[2 * parts : 2 * parts + 2], refs[2 * parts + 2 : 2 * parts + 4], refs[-1]
    copies = []
    for t in range(turned_ref.shape[0] // tile):
        at = slice(t * tile, (t + 1) * tile)
        for side in range(2):
            lo = 0
            for ref in grads[side]:
                size = ref.shape[1]
                values[side][at, lo : lo + size] = dot_nn(turned_ref[at, :], ref[...]).astype(BF)
                lo += size
            copies.append(pltpu.make_async_copy(values[side].at[at, :], outs[side].at[at, :], sems.at[t, side]))
            copies[-1].start()
    for copy in copies:
        copy.wait()


def token_grad_kernel(dims, pick_ref, got_ref, out_hbm, rows, out, sems):
    n_dp, half, cap, blocks, unit = dims
    size = blocks * cap
    width = blocks * LANES
    pick = pick_ref[...]
    rows[...] = jnp.zeros_like(rows)
    copies = []
    for d in range(n_dp):
        total = got_ref[d * half * size : (d * half + 1) * size, :].astype(F32)
        for h in range(1, half):
            base = (d * half + h) * size
            total = total + got_ref[base : base + size, :].astype(F32)
        for q in range(blocks):
            rows[0:cap, q * LANES : (q + 1) * LANES] = total[q * cap : (q + 1) * cap, :]
        cols = slice(d * width, (d + 1) * width)
        out[:, cols] = dot_tn(pick, rows[...].astype(BF)).astype(out.dtype)
        copies.append(pltpu.make_async_copy(out.at[:, cols], out_hbm.at[:, cols], sems.at[d]))
        copies[-1].start()
    for copy in copies:
        copy.wait()


def fast_shards(n_dp, n_expert, cap, tokens, expert_ids, gate_values, w_gate, w_up, w_down, target):
    tok_rows, features = tokens.shape
    width, hid = w_gate.shape
    half = n_expert // 2
    blocks = width // LANES
    peers = n_dp * half
    sources = 2 * peers
    rows = cap * sources
    unit = -(-(blocks + 2 + GATE_PIECES) * cap // 16) * 16
    dims = (n_dp, half, cap, blocks, unit)
    place = lax.axis_index("expert").astype(jnp.int32).reshape(1)
    ids = expert_ids.T
    slice_groups = [
        [d * n_expert + 2 * h + c for d in range(n_dp) for h in range(half)] for c in range(2)
    ]

    def other(x, mask):
        return lax.ppermute(x, "expert", [(i, i ^ mask) for i in range(n_expert)])

    def other_core(x):
        return other(x, 1)

    def other_dp(x):
        return lax.ppermute(x, "dp", [(0, 1), (1, 0)])

    def over_slice(x):
        return lax.all_to_all(x, ("dp", "expert"), 0, 0, axis_index_groups=slice_groups, tiled=True)

    outgoing, pick = call(
        functools.partial(route_kernel, dims),
        (sds((peers * unit, LANES), BF), sds((16, tok_rows), BF)),
        in_hbm(ids, gate_values.T, tokens, target),
        [HBM] * 4,
        [
            pltpu.VMEM(ids.shape, ids.dtype),
            pltpu.VMEM(ids.shape, F32),
            pltpu.VMEM(tokens.shape, tokens.dtype),
            pltpu.VMEM(target.shape, target.dtype),
            pltpu.VMEM((16, width), F32),
            pltpu.VMEM((16, width), F32),
            pltpu.VMEM((blocks * cap, LANES), F32),
            pltpu.VMEM((unit - blocks * cap, LANES), F32),
            pltpu.SemaphoreType.DMA((2 + 2 * n_dp,)),
        ],
        name="route",
    )
    first = -(-hid // (2 * LANES)) * LANES
    head = 2 * LANES

    def columns(size):
        return sds((width, size), w_gate.dtype), sds((width, size), w_up.dtype)

    def column_sems(size):
        return pltpu.SemaphoreType.DMA((-(-size // (2 * LANES)), 2))

    loaded, *weights = call(
        load_kernel,
        (sds((8, LANES), F32), *columns(head)),
        in_hbm(w_gate, w_up),
        [HBM] * 2,
        [column_sems(head)],
        flops=1_000_000_000,
        moved=8 * width * head,
        name="load_weights",
    )
    own, loaded = lax.optimization_barrier((over_slice(outgoing), loaded))
    *more, own_rows, own_target, own_gates = call(
        functools.partial(load_more_kernel, dims, head),
        (
            *columns(first - head),
            sds((cap * peers, width), BF),
            sds((cap * peers, LANES), F32),
            sds((cap * peers, LANES), F32),
        ),
        (place, own, *in_hbm(w_gate, w_up)),
        [SMEM, VMEM] + [HBM] * 2,
        [pltpu.VMEM((peers * unit, LANES), F32), column_sems(first - head)],
        flops=1_000_000_000,
        moved=8 * width * head,
        name="load_weights",
    )
    weights += more
    neighbour = other_core(own)
    chunks = [(0, first), (first, hid - first)]
    pres = []
    for start, size in chunks:
        outs = (sds((2, rows, size), F32), sds((2, rows, size), BF))
        cost = dict(flops=8 * rows * width * size, moved=4 * width * size)
        fetched = [
            pltpu.VMEM((width, size), w_gate.dtype),
            pltpu.VMEM((width, size), w_up.dtype),
            column_sems(size),
        ]
        if start == 0:
            all_rows, all_target, all_gates, *pre = call(
                functools.partial(first_pre_kernel, dims),
                (sds((rows, width), BF), sds((rows, LANES), F32), sds((rows, LANES), F32), *outs),
                (place, loaded, own_rows, own_target, own_gates, neighbour, *weights),
                [SMEM] + [VMEM] * 9,
                [pltpu.VMEM((peers * unit, LANES), F32)],
                name="pre_activations",
                **cost,
            )
        else:
            turned, *pre = call(
                functools.partial(more_pre_kernel, start),
                (sds((width, rows), BF), *outs),
                (all_rows, *in_hbm(w_gate, w_up)),
                [VMEM] + [HBM] * 2,
                fetched,
                name="pre_activations",
                **cost,
            )
        pres.append((pre[0], other_dp(pre[1])))
    (start, size), (start_b, size_b) = chunks
    half_rows = half * rows
    cost = dict(flops=4 * rows * width * size, moved=2 * width * size)
    up_deriv, act, total = call(
        functools.partial(first_down_kernel, dims, start),
        (sds((rows, size), F32), sds((rows, size), F32), sds((2 * half_rows, LANES), F32)),
        (place, *pres[0], w_down),
        [SMEM] + [VMEM] * 3,
        [pltpu.VMEM((rows, size), BF)],
        name="down",
        **cost,
    )
    up_deriv_b, act_b, hidden_b, send = call(
        functools.partial(send_down_kernel, dims, start_b),
        (
            sds((rows, size_b), F32),
            sds((rows, size_b), F32),
            sds((rows, size_b), BF),
            sds((half_rows, LANES), BF),
        ),
        (place, *pres[1], w_down, total),
        [SMEM] + [VMEM] * 4,
        name="down_send",
        **cost,
    )
    sent = other_core(send)
    keep = call(
        functools.partial(keep_down_kernel, dims, start_b),
        sds((half_rows, LANES), F32),
        (place, hidden_b, w_down, total),
        [SMEM] + [VMEM] * 3,
        name="down_keep",
        **cost,
    )
    saved = [(up_deriv, act), (up_deriv_b, act_b)]
    quad_rows = half_rows // 4
    kept, sent_on = sds((quad_rows, LANES), F32), sds((quad_rows, LANES), BF)
    keep, *sends = call(chip_sum_kernel, (kept, *[sent_on] * 3), (keep, sent), [VMEM] * 2, name="chip_sum")
    keep, send = call(
        residual_kernel,
        (kept, sent_on),
        (place, keep, *[other(sends[k], 2 * (k + 1)) for k in (2, 0, 1)], all_gates, all_target),
        [SMEM] + [VMEM] * 6,
        name="residual",
    )
    step = 8
    while 2 * step < n_expert:
        keep, send = call(line_sum_kernel, (kept, sent_on), (keep, other(send, step)), [VMEM] * 2, name="line_sum")
        step *= 2
    cot = call(
        cotangent_kernel,
        sent_on,
        (keep, other(send, step), all_gates),
        [VMEM] * 3,
        name="cotangent",
    )
    from_quad = [other(cot, 2 * k) for k in (1, 2, 3)]
    from_core = other_core(cot)

    def near(flip, flips, got, *total):
        return call(
            functools.partial(near_grad_hidden_kernel, flip, flips),
            sds((rows, hid), F32),
            (place, w_down, *got, *total),
            [SMEM] + [VMEM] * (1 + len(got) + len(total)),
            [pltpu.VMEM((rows, len(got) * quad_rows // rows * LANES), BF)],
            flops=len(got) * rows * width * hid // 4,
            moved=len(got) * width * hid // 4,
            name="grad_hidden_near",
        )

    own_total = near(0, (0,), (cot,))
    own_total = near(1, (0,), (from_core,), own_total)
    from_quad[2], own_total = lax.optimization_barrier((from_quad[2], own_total))
    from_both = [other_core(x) for x in from_quad]
    own_total = near(0, (1, 2, 3), from_quad, own_total)
    grads = []
    order = [1, 0]
    for k in order:
        start, size = chunks[k]
        outs = (sds((rows, size), F32), sds((rows, size), BF))
        cost = dict(flops=2 * rows * width * size, moved=2 * width * size)
        if k == order[0]:
            cot, *grad = call(
                functools.partial(first_grad_hidden_kernel, start),
                (sds((rows, 3 * width // 8), BF), *outs),
                (place, *from_both, w_down, own_total),
                [SMEM] + [VMEM] * 5,
                name="grad_hidden",
                **cost,
            )
        else:
            grad = call(
                functools.partial(more_grad_hidden_kernel, start),
                outs,
                (place, cot, w_down, own_total),
                [SMEM] + [VMEM] * 3,
                name="grad_hidden",
                **cost,
            )
        grads.append((grad[0], other_dp(grad[1])))
    pre_grads = [None] * len(chunks)
    total = ()
    peer_rows = peers * blocks * cap
    for k, grad in zip(order, grads):
        start, size = chunks[k]
        outs, scratch = (sds((rows, width), F32),), []
        if k == order[-1]:
            outs = (sds((peer_rows, LANES), F32), sds((peer_rows, LANES), BF))
            scratch = [pltpu.VMEM((2 * peer_rows, LANES), F32)]
        gate_pre_grad, up_pre_grad, *total = call(
            functools.partial(row_grad_kernel, dims, start, k == order[-1]),
            (sds((rows, size), BF), sds((rows, size), BF), *outs),
            (place, *grad, *saved[k], w_gate, w_up, *total),
            [SMEM] + [VMEM] * (6 + len(total)),
            scratch,
            flops=8 * rows * width * size,
            moved=4 * width * size,
            name="row_grad",
        )
        pre_grads[k] = (gate_pre_grad, up_pre_grad)
    keep, send = total
    chip_rows = add_cores(keep, other_core(send))
    got_rows = over_slice(chip_rows)
    pre_grads = [pair[0] for pair in pre_grads] + [pair[1] for pair in pre_grads]
    tile = 256
    gate_grad, up_grad = call(
        functools.partial(weight_grad_kernel, len(chunks), tile),
        (sds((width, hid), BF), sds((width, hid), BF)),
        (turned, *pre_grads),
        [VMEM] * (1 + len(pre_grads)),
        [
            pltpu.VMEM((width, hid), BF),
            pltpu.VMEM((width, hid), BF),
            pltpu.SemaphoreType.DMA((width // tile, 2)),
        ],
        flops=4 * rows * width * hid,
        moved=4 * width * hid,
        out_spec=HBM,
        name="weight_grads",
    )
    token_grad = call(
        functools.partial(token_grad_kernel, dims),
        sds((tok_rows, features), tokens.dtype),
        (pick, got_rows),
        [VMEM] * 2,
        [
            pltpu.VMEM((16, width), F32),
            pltpu.VMEM((tok_rows, features), tokens.dtype),
            pltpu.SemaphoreType.DMA((n_dp,)),
        ],
        out_spec=HBM,
        name="token_grad",
    )
    return token_grad, gate_grad, up_grad


def contract_last(matrix_a, matrix_b):
    return lax.dot_general(
        matrix_a, matrix_b, (((1,), (1,)), ((), ())), preferred_element_type=jnp.float32
    )


def rounded_terms(column_blocks, grad_blocks):
    terms = jnp.einsum(
        "krd,krh->kdh", column_blocks, grad_blocks, preferred_element_type=jnp.float32
    )
    terms = lax.optimization_barrier(terms.astype(jnp.bfloat16))
    return jnp.sum(terms.astype(jnp.float32), axis=0)


def spread_rows(rows, group_size, capacity, features):
    flat = rows.reshape(EXPERTS, 1, capacity * features)
    wide = jnp.broadcast_to(flat, (EXPERTS, group_size, capacity * features))
    return wide.reshape(EXPERTS * group_size * capacity, features)


def fold_group(rows, group_size, capacity, features):
    shaped = rows.reshape(EXPERTS, group_size, capacity * features).astype(jnp.float32)
    return jnp.sum(shaped, axis=1).reshape(EXPERTS * capacity, features)


def general_shards(tokens, expert_ids, gate_values, w_gate, w_up, w_down, target):
    devices_along = lax.axis_size("expert")
    group_size = devices_along // EXPERTS
    tok_rows = tokens.shape[0]
    features = tokens.shape[1]
    hid_local = w_gate.shape[1]
    capacity = max(2, 3 * tok_rows // 128)
    slot_total = EXPERTS * capacity
    flat_ids = expert_ids.reshape(-1)
    pair_count = flat_ids.shape[0]
    window = flat_ids < EXPERTS
    onehot = (flat_ids[:, None] == jnp.arange(EXPERTS, dtype=jnp.int32)[None, :]).astype(jnp.int32)
    slot_index = jnp.sum((jnp.cumsum(onehot, axis=0) - onehot) * onehot, axis=1)
    position = jnp.where(window, flat_ids * capacity + slot_index, slot_total)
    owning = jnp.arange(pair_count, dtype=jnp.int32) // 2
    slot_token = jnp.zeros((slot_total + 1,), jnp.int32).at[position].set(owning)[:slot_total]
    slot_live = jnp.zeros((slot_total + 1,), jnp.bool_).at[position].set(True)[:slot_total]
    slot_gate = (
        jnp.zeros((slot_total + 1,), jnp.float32)
        .at[position]
        .set(gate_values.reshape(-1))[:slot_total]
    )
    safe_pairs = jnp.minimum(position, slot_total - 1).reshape(tok_rows, 2)
    live_pairs = window.reshape(tok_rows, 2)

    def pick(table, column):
        return jnp.where(live_pairs[:, column : column + 1], table[safe_pairs[:, column]], 0.0)

    outgoing = jnp.where(slot_live[:, None], tokens[slot_token], jnp.zeros((), tokens.dtype))
    outgoing = spread_rows(outgoing, group_size, capacity, features)
    received = lax.all_to_all(outgoing, "expert", split_axis=0, concat_axis=0, tiled=True)
    rows_count = received.shape[0]
    full_gate, full_up, full_down = (
        lax.all_gather(w_gate, "dp", axis=0, tiled=True),
        lax.all_gather(w_up, "dp", axis=0, tiled=True),
        lax.all_gather(w_down, "dp", axis=1, tiled=True),
    )
    gate_pre = jnp.dot(received, full_gate, preferred_element_type=jnp.float32)
    up_pre = jnp.dot(received, full_up, preferred_element_type=jnp.float32)
    sigmoid_gate = jax.nn.sigmoid(gate_pre)
    activated = sigmoid_gate * gate_pre
    hidden = (activated * up_pre).astype(jnp.bfloat16)
    partial_out = jnp.dot(hidden, full_down, preferred_element_type=jnp.float32).astype(
        jnp.bfloat16
    )
    returned_out = lax.all_to_all(partial_out, "expert", split_axis=0, concat_axis=0, tiled=True)
    expert_out = fold_group(returned_out, group_size, capacity, features)
    combined = gate_values[:, 0:1] * pick(expert_out, 0) + gate_values[:, 1:2] * pick(expert_out, 1)
    residual = combined - target.astype(jnp.float32)
    outgoing_grad = jnp.where(
        slot_live[:, None], slot_gate[:, None] * residual[slot_token], 0.0
    ).astype(jnp.bfloat16)
    outgoing_grad = spread_rows(outgoing_grad, group_size, capacity, features)
    cotangent = lax.all_to_all(outgoing_grad, "expert", split_axis=0, concat_axis=0, tiled=True)
    grad_hidden = contract_last(cotangent, full_down)
    derivative = sigmoid_gate * (1.0 + gate_pre * (1.0 - sigmoid_gate))
    grad_gate_pre = (grad_hidden * up_pre * derivative).astype(jnp.bfloat16)
    grad_up_pre = (grad_hidden * activated).astype(jnp.bfloat16)
    row_part = (
        contract_last(grad_gate_pre, full_gate) + contract_last(grad_up_pre, full_up)
    ).astype(jnp.bfloat16)
    back_rows = lax.all_to_all(row_part, "expert", split_axis=0, concat_axis=0, tiled=True)
    row_grad = fold_group(back_rows, group_size, capacity, features)
    token_grad = (pick(row_grad, 0) + pick(row_grad, 1)).astype(jnp.bfloat16)
    shard_columns = lax.all_to_all(received, "dp", split_axis=1, concat_axis=0, tiled=True)
    shard_width = shard_columns.shape[1]
    dp_count = lax.axis_size("dp")
    every_gate, every_up = (
        lax.all_gather(grad_gate_pre, "dp", axis=0, tiled=True),
        lax.all_gather(grad_up_pre, "dp", axis=0, tiled=True),
    )
    column_blocks = shard_columns.reshape(dp_count, rows_count, shard_width)
    gate_sum = rounded_terms(column_blocks, every_gate.reshape(dp_count, rows_count, hid_local))
    up_sum = rounded_terms(column_blocks, every_up.reshape(dp_count, rows_count, hid_local))
    return (token_grad, gate_sum.astype(jnp.bfloat16), up_sum.astype(jnp.bfloat16))


def solution(mesh):
    n_dp, n_expert = mesh.shape["dp"], mesh.shape["expert"]

    def shards(*args):
        tok_rows, features = args[0].shape
        width, hid = args[3].shape
        cap = max(2, 3 * tok_rows // 128)
        whole_blocks = (
            n_dp == 2
            and n_expert % 16 == 0
            and n_expert & (n_expert - 1) == 0
            and width == n_expert * LANES
            and hid % LANES == 0
            and hid > 4 * LANES
            and cap <= 8
            and tok_rows % LANES == 0
        )
        if whole_blocks:
            return fast_shards(n_dp, n_expert, cap, *args)
        return general_shards(*args)

    placed = (
        P(("dp", "expert"), None),
        P(("dp", "expert"), None),
        P(("dp", "expert"), None),
        P("dp", "expert"),
        P("dp", "expert"),
        P("expert", "dp"),
        P(("dp", "expert"), None),
    )
    return jax.shard_map(
        shards,
        mesh=mesh,
        in_specs=placed,
        out_specs=(P(("dp", "expert"), None), P("dp", "expert"), P("dp", "expert")),
        check_vma=False,
    )
```

```python
import functools

import jax
import jax.numpy as jnp
from jax import lax
from jax.experimental import pallas as pl
from jax.experimental.pallas import tpu as pltpu
from jax.sharding import PartitionSpec as P

EXPERTS = 1
LANES = 128
GATE_PIECES = 3
BF = jnp.bfloat16
F32 = jnp.float32
VMEM = pl.BlockSpec(memory_space=pltpu.VMEM)
HBM = pl.BlockSpec(memory_space=pltpu.HBM)
SMEM = pl.BlockSpec(memory_space=pltpu.SMEM)


def sds(shape, dtype):
    return jax.ShapeDtypeStruct(shape, dtype)


def dot_nn(a, b):
    return lax.dot_general(a, b, (((1,), (0,)), ((), ())), preferred_element_type=F32)


def dot_nt(a, b):
    return lax.dot_general(a, b, (((1,), (1,)), ((), ())), preferred_element_type=F32)


def dot_tn(a, b):
    return lax.dot_general(a, b, (((0,), (0,)), ((), ())), preferred_element_type=F32)


def in_hbm(*arrays):
    return tuple(pltpu.with_memory_space_constraint(x, pltpu.HBM) for x in arrays)


def core_of(place_ref):
    return place_ref[0] & 1


def quad_of(place_ref, k=0):
    x, low = (place_ref[0] >> 1) & 1, (place_ref[0] >> 2) & 1
    return (1 - x if k & 1 else x) + 2 * (1 - low if k & 2 else low)


def rest_of(place_ref):
    return place_ref[0] >> 3


def call(body, outs, args, specs, scratch=(), limit=16, flops=0, moved=0, name=None, out_spec=VMEM):
    return pl.pallas_call(
        body,
        out_shape=outs,
        in_specs=specs,
        out_specs=jax.tree.map(lambda _: out_spec, outs),
        scratch_shapes=list(scratch),
        compiler_params=pltpu.CompilerParams(vmem_limit_bytes=limit << 20),
        cost_estimate=pl.CostEstimate(flops=flops, bytes_accessed=moved, transcendentals=0),
        name=name,
    )(*args)


def select_rows(ids_ref):
    tok_rows = ids_ref.shape[1]
    live = jnp.sum((ids_ref[...] < EXPERTS).astype(F32), axis=0, keepdims=True)
    before = lax.broadcasted_iota(jnp.int32, (tok_rows, tok_rows), 0)
    after = lax.broadcasted_iota(jnp.int32, (tok_rows, tok_rows), 1)
    earlier = (before < after).astype(BF)
    wide = jnp.broadcast_to(live, (16, tok_rows))
    slot = dot_nn(wide.astype(BF), earlier)
    wanted = lax.broadcasted_iota(jnp.int32, (16, tok_rows), 0).astype(F32)
    return jnp.where(slot == wanted, wide, 0.0)


def add_kernel(own_ref, got_ref, out_ref):
    out_ref[...] = (own_ref[...] + got_ref[...].astype(F32)).astype(out_ref.dtype)


def add_cores(own, got):
    return call(add_kernel, sds(got.shape, got.dtype), (own, got), [VMEM] * 2, name="add_cores")


def route_kernel(dims, ids_hbm, gates_hbm, tokens_hbm, target_hbm, out_ref, pick_ref,
                 ids_ref, gates_ref, tokens_ref, target_ref, tok, tgt, head, tail, sems):
    n_dp, half, cap, blocks, unit = dims
    width = blocks * LANES
    pairs = [(ids_hbm, ids_ref), (gates_hbm, gates_ref)]
    for hbm, ref in ((tokens_hbm, tokens_ref), (target_hbm, target_ref)):
        for d in range(n_dp):
            cols = slice(d * width, (d + 1) * width)
            pairs.append((hbm.at[:, cols], ref.at[:, cols]))
    copies = [pltpu.make_async_copy(src, dst, sems.at[i]) for i, (src, dst) in enumerate(pairs)]
    for copy in copies:
        copy.start()
    tail[...] = jnp.zeros_like(tail)
    copies[0].wait()
    copies[1].wait()
    chosen = select_rows(ids_ref)
    live_gates = jnp.sum(jnp.where(ids_ref[...] < EXPERTS, gates_ref[...], 0.0), axis=0, keepdims=True)
    gate = jnp.sum(chosen * live_gates, axis=1, keepdims=True)
    pick = chosen.astype(BF)
    pick_ref[...] = pick
    rest = gate
    for piece in range(GATE_PIECES):
        part = rest.astype(BF).astype(F32)
        rest = rest - part
        at = (2 + piece) * cap
        tail[at : at + cap, :] = jnp.broadcast_to(part[0:cap], (cap, LANES))
    lead = blocks * cap
    for d in range(n_dp):
        cols = slice(d * width, (d + 1) * width)
        copies[2 + d].wait()
        tok[...] = dot_nn(pick, tokens_ref[:, cols])
        for q in range(blocks):
            head[q * cap : (q + 1) * cap, :] = tok[0:cap, q * LANES : (q + 1) * LANES]
        packed = head[...].astype(BF)
        for h in range(half):
            base = (d * half + h) * unit
            out_ref[base : base + lead, :] = packed
    for d in range(n_dp):
        cols = slice(d * width, (d + 1) * width)
        copies[2 + n_dp + d].wait()
        tgt[...] = dot_nn(pick, target_ref[:, cols])
        for h in range(half):
            for core in range(2):
                lo = (core * half + h % 4 * (half // 4) + h // 4) * LANES
                tail[core * cap : (core + 1) * cap, :] = tgt[0:cap, lo : lo + LANES]
            base = (d * half + h) * unit
            out_ref[base + lead : base + unit, :] = tail[...].astype(BF)


def lay_out(dims, place_ref, src_ref, wide, begin, rows_ref, target_ref, gates_ref):
    n_dp, half, cap, blocks, unit = dims
    peers = n_dp * half
    wide[...] = src_ref[...].astype(F32)

    def one(k):
        return wide[pl.ds(k, peers, stride=unit), :]

    for c in range(cap):
        at = begin(c)
        for q in range(blocks):
            rows_ref[at, q * LANES : (q + 1) * LANES] = one(q * cap + c).astype(BF)
        base = blocks * cap
        target_ref[at, :] = jnp.where(core_of(place_ref) == 0, one(base + c), one(base + cap + c))
        gates_ref[at, :] = sum(one(base + (2 + piece) * cap + c) for piece in range(GATE_PIECES))


def fetch_columns(starts, gate_hbm, up_hbm, gate_w, up_w, sems):
    lo, hi = starts
    copies = []
    for k, at in enumerate(range(lo, hi, 2 * LANES)):
        count = min(2 * LANES, hi - at)
        pair = []
        for side, (src, dst) in enumerate(((gate_hbm, gate_w), (up_hbm, up_w))):
            part = src.at[:, pl.ds(at, count)]
            pair.append(pltpu.make_async_copy(part, dst.at[:, pl.ds(at - lo, count)], sems.at[k, side]))
            pair[-1].start()
        copies.append(pair)
    return copies


def load_kernel(gate_hbm, up_hbm, done_ref, gate_w, up_w, sems):
    copies = fetch_columns((0, gate_w.shape[1]), gate_hbm, up_hbm, gate_w, up_w, sems)
    done_ref[...] = jnp.zeros_like(done_ref)
    for pair in copies:
        for copy in pair:
            copy.wait()


def load_more_kernel(dims, start, place_ref, own_ref, gate_hbm, up_hbm, gate_w, up_w,
                     rows_ref, target_ref, gates_ref, wide, sems):
    peers = dims[0] * dims[1]
    copies = fetch_columns((start, start + gate_w.shape[1]), gate_hbm, up_hbm, gate_w, up_w, sems)
    begin = lambda c: slice(c * peers, (c + 1) * peers)
    lay_out(dims, place_ref, own_ref, wide, begin, rows_ref, target_ref, gates_ref)
    for pair in copies:
        for copy in pair:
            copy.wait()


def partial_pre(rows_ref, gate_w, up_w, copies, first, own_pre, send_pre):
    for j in range(gate_w.shape[1] // LANES):
        if copies and j % 2 == 0:
            for copy in copies[j // 2]:
                copy.wait()
        here = slice(j * LANES, (j + 1) * LANES)
        cols = slice(first + j * LANES, first + (j + 1) * LANES)
        pair = jnp.concatenate([gate_w[:, here], up_w[:, here]], axis=1)
        both = dot_nn(rows_ref[...], pair)
        for side in range(2):
            value = both[:, side * LANES : (side + 1) * LANES]
            own_pre[side, :, cols] = value
            send_pre[side, :, cols] = value.astype(BF)


def first_pre_kernel(dims, place_ref, loaded_ref, own_rows, own_target, own_gates, other_ref,
                     gate_head, up_head, gate_rest, up_rest,
                     rows_ref, target_ref, gates_ref, own_pre, send_pre, wide):
    n_dp, half, cap, blocks, unit = dims
    peers = n_dp * half
    core = core_of(place_ref)

    def begin(c, side):
        return pl.ds(pl.multiple_of((2 * c + side) * peers, peers), peers)

    for c in range(cap):
        here = slice(c * peers, (c + 1) * peers)
        for own, full in ((own_rows, rows_ref), (own_target, target_ref), (own_gates, gates_ref)):
            full[begin(c, core), :] = own[here, :]
    there = lambda c: begin(c, 1 - core)
    lay_out(dims, place_ref, other_ref, wide, there, rows_ref, target_ref, gates_ref)
    partial_pre(rows_ref, gate_head, up_head, (), 0, own_pre, send_pre)
    partial_pre(rows_ref, gate_rest, up_rest, (), gate_head.shape[1], own_pre, send_pre)


def more_pre_kernel(start, rows_ref, gate_hbm, up_hbm, turned_ref, own_pre, send_pre, gate_w, up_w, sems):
    copies = fetch_columns((start, start + own_pre.shape[2]), gate_hbm, up_hbm, gate_w, up_w, sems)
    turned_ref[...] = rows_ref[...].T
    partial_pre(rows_ref, gate_w, up_w, copies, 0, own_pre, send_pre)


def down_side(dims, start, place_ref, hidden, down_w, total_ref, side, out_ref):
    n_dp, half, cap, blocks, unit = dims
    rows, hid = hidden.shape
    quarter = half // 4
    core = core_of(place_ref) if side == 0 else 1 - core_of(place_ref)
    for k in range(4):
        quad = quad_of(place_ref, k)
        for j in range(0, quarter, 2):
            lo = (core * half + quad * quarter + j) * LANES
            cols = pl.ds(pl.multiple_of(lo, 2 * LANES), 2 * LANES)
            value = dot_nn(hidden[...], down_w[start : start + hid, cols])
            for n in range(2):
                part = value[:, n * LANES : (n + 1) * LANES]
                block = k * quarter + j + n
                if total_ref is not None:
                    both = side * half + block
                    part = part + total_ref[both * rows : (both + 1) * rows, :]
                out_ref[block * rows : (block + 1) * rows, :] = part.astype(out_ref.dtype)


def activate(own_ref, got_ref, up_deriv, act_ref, hidden):
    gate_pre = own_ref[0] + got_ref[0].astype(F32)
    up_pre = own_ref[1] + got_ref[1].astype(F32)
    sig = jax.nn.sigmoid(gate_pre)
    act = sig * gate_pre
    act_ref[...] = act
    up_deriv[...] = up_pre * (sig * (1.0 + gate_pre * (1.0 - sig)))
    hidden[...] = (act * up_pre).astype(BF)


def first_down_kernel(dims, start, place_ref, own_ref, got_ref, down_w, up_deriv, act_ref, total_ref, hidden):
    activate(own_ref, got_ref, up_deriv, act_ref, hidden)
    size = dims[1] * hidden.shape[0]
    for side in range(2):
        part = total_ref.at[side * size : (side + 1) * size]
        down_side(dims, start, place_ref, hidden, down_w, None, side, part)


def send_down_kernel(dims, start, place_ref, own_ref, got_ref, down_w, total_ref, up_deriv, act_ref, hidden, send_ref):
    activate(own_ref, got_ref, up_deriv, act_ref, hidden)
    down_side(dims, start, place_ref, hidden, down_w, total_ref, 1, send_ref)


def keep_down_kernel(dims, start, place_ref, hidden, down_w, total_ref, keep_ref):
    down_side(dims, start, place_ref, hidden, down_w, total_ref, 0, keep_ref)


def chip_sum_kernel(own_ref, got_ref, keep_ref, *send_refs):
    size = keep_ref.shape[0]
    for k, ref in enumerate((keep_ref, *send_refs)):
        at = slice(k * size, (k + 1) * size)
        ref[...] = (own_ref[at, :] + got_ref[at, :].astype(F32)).astype(ref.dtype)


def residual_kernel(place_ref, own_ref, first_ref, second_ref, third_ref, gates_ref, target_ref, keep_ref, send_ref):
    rows = target_ref.shape[0]
    for z in range(own_ref.shape[0] // rows):
        at = slice(z * rows, (z + 1) * rows)
        value = own_ref[at, :] + first_ref[at, :].astype(F32)
        value = value + (second_ref[at, :].astype(F32) + third_ref[at, :].astype(F32))
        value = gates_ref[...] * value
        value = jnp.where(rest_of(place_ref) == z, value - target_ref[...], value)
        keep_ref[at, :] = value
        send_ref[at, :] = value.astype(BF)


def line_sum_kernel(own_ref, got_ref, keep_ref, send_ref):
    value = own_ref[...] + got_ref[...].astype(F32)
    keep_ref[...] = value
    send_ref[...] = value.astype(BF)


def cotangent_kernel(own_ref, got_ref, gates_ref, out_ref):
    rows = gates_ref.shape[0]
    for z in range(own_ref.shape[0] // rows):
        at = slice(z * rows, (z + 1) * rows)
        out_ref[at, :] = (gates_ref[...] * (own_ref[at, :] + got_ref[at, :].astype(F32))).astype(BF)


def gather_blocks(refs, out):
    rows = out.shape[0]
    parts = refs[0].shape[0] // rows
    for k, ref in enumerate(refs):
        for h in range(parts):
            lo = (k * parts + h) * LANES
            out[:, lo : lo + LANES] = ref[h * rows : (h + 1) * rows, :]


def quad_grad_hidden(cot, core, quads, down_w, start, total_ref, outs):
    width = cot.shape[1] // len(quads)
    size = outs[0].shape[1]
    for lo in range(0, size, 2 * LANES):
        here = slice(lo, min(lo + 2 * LANES, size))
        there = slice(start + here.start, start + here.stop)
        value = total_ref[:, there] if total_ref is not None else None
        for k, quad in enumerate(quads):
            cols = pl.ds(pl.multiple_of((4 * core + quad) * width, width), width)
            part = dot_nt(cot[:, k * width : (k + 1) * width], down_w[there, cols])
            value = part if value is None else value + part
        for out in outs:
            out[:, here] = value.astype(out.dtype)


def near_grad_hidden_kernel(flip, flips, place_ref, down_w, *refs):
    got_refs, rest = refs[: len(flips)], refs[len(flips) :]
    *total_ref, out_ref, cot = rest
    core = 1 - core_of(place_ref) if flip else core_of(place_ref)
    quads = [quad_of(place_ref, k) for k in flips]
    gather_blocks(got_refs, cot)
    quad_grad_hidden(cot, core, quads, down_w, 0, total_ref[0] if total_ref else None, (out_ref,))


def first_grad_hidden_kernel(start, place_ref, first_ref, second_ref, third_ref, down_w, total_ref, cot, own_out, send_out):
    gather_blocks((first_ref, second_ref, third_ref), cot)
    quads = [quad_of(place_ref, k) for k in (1, 2, 3)]
    quad_grad_hidden(cot, 1 - core_of(place_ref), quads, down_w, start, total_ref, (own_out, send_out))


def more_grad_hidden_kernel(start, place_ref, cot, down_w, total_ref, own_out, send_out):
    quads = [quad_of(place_ref, k) for k in (1, 2, 3)]
    quad_grad_hidden(cot, 1 - core_of(place_ref), quads, down_w, start, total_ref, (own_out, send_out))


def row_grad_kernel(dims, start, last, place_ref, own_ref, got_ref, up_deriv, act_ref, gate_w, up_w, *refs):
    n_dp, half, cap, blocks, unit = dims
    sources = 2 * n_dp * half
    refs = list(refs)
    total_ref = refs.pop(0) if last else None
    gate_out, up_out, *out_refs = refs
    grad_hidden = own_ref[...] + got_ref[...].astype(F32)
    gate_out[...] = (grad_hidden * up_deriv[...]).astype(BF)
    up_out[...] = (grad_hidden * act_ref[...]).astype(BF)
    hid = gate_out.shape[1]
    wide = out_refs[-1]

    def column(j, _):
        at = pl.ds(pl.multiple_of(j * 2 * LANES, 2 * LANES), 2 * LANES)
        value = dot_nt(gate_w[at, start : start + hid], gate_out[...])
        value = (value + dot_nt(up_w[at, start : start + hid], up_out[...])).T
        if total_ref is not None:
            value = value + total_ref[:, at]
        if not last:
            wide[:, at] = value
            return 0
        for k in range(2):
            for c in range(cap):
                piece = value[c * sources : (c + 1) * sources, k * LANES : (k + 1) * LANES]
                wide[pl.ds((2 * j + k) * cap + c, sources, stride=blocks * cap), :] = piece
        return 0

    lax.fori_loop(0, blocks // 2, column, 0, unroll=True)
    if last:
        keep_ref, send_ref, _ = out_refs
        size = keep_ref.shape[0]
        core = core_of(place_ref)
        keep_ref[...] = wide[pl.ds(pl.multiple_of(core * size, size), size), :]
        send_ref[...] = wide[pl.ds(pl.multiple_of((1 - core) * size, size), size), :].astype(BF)


def weight_grad_kernel(parts, tile, turned_ref, *refs):
    grads = (refs[:parts], refs[parts : 2 * parts])
    outs, values, sems = refs[2 * parts : 2 * parts + 2], refs[2 * parts + 2 : 2 * parts + 4], refs[-1]
    copies = []
    for t in range(turned_ref.shape[0] // tile):
        at = slice(t * tile, (t + 1) * tile)
        for side in range(2):
            lo = 0
            for ref in grads[side]:
                size = ref.shape[1]
                values[side][at, lo : lo + size] = dot_nn(turned_ref[at, :], ref[...]).astype(BF)
                lo += size
            copies.append(pltpu.make_async_copy(values[side].at[at, :], outs[side].at[at, :], sems.at[t, side]))
            copies[-1].start()
    for copy in copies:
        copy.wait()


def token_grad_kernel(dims, pick_ref, got_ref, out_hbm, rows, out, sems):
    n_dp, half, cap, blocks, unit = dims
    size = blocks * cap
    width = blocks * LANES
    pick = pick_ref[...]
    rows[...] = jnp.zeros_like(rows)
    copies = []
    for d in range(n_dp):
        total = got_ref[d * half * size : (d * half + 1) * size, :].astype(F32)
        for h in range(1, half):
            base = (d * half + h) * size
            total = total + got_ref[base : base + size, :].astype(F32)
        for k in range(4):
            here = slice(k * width // 4, (k + 1) * width // 4)
            for q in range(k * blocks // 4, (k + 1) * blocks // 4):
                rows[0:cap, q * LANES : (q + 1) * LANES] = total[q * cap : (q + 1) * cap, :]
            cols = slice(d * width + here.start, d * width + here.stop)
            out[:, cols] = dot_tn(pick, rows[:, here].astype(BF)).astype(out.dtype)
            copies.append(pltpu.make_async_copy(out.at[:, cols], out_hbm.at[:, cols], sems.at[d, k]))
            copies[-1].start()
    for copy in copies:
        copy.wait()


def fast_shards(n_dp, n_expert, cap, tokens, expert_ids, gate_values, w_gate, w_up, w_down, target):
    tok_rows, features = tokens.shape
    width, hid = w_gate.shape
    half = n_expert // 2
    blocks = width // LANES
    peers = n_dp * half
    sources = 2 * peers
    rows = cap * sources
    unit = -(-(blocks + 2 + GATE_PIECES) * cap // 16) * 16
    dims = (n_dp, half, cap, blocks, unit)
    place = lax.axis_index("expert").astype(jnp.int32).reshape(1)
    ids = expert_ids.T
    slice_groups = [
        [d * n_expert + 2 * h + c for d in range(n_dp) for h in range(half)] for c in range(2)
    ]

    def other(x, mask):
        return lax.ppermute(x, "expert", [(i, i ^ mask) for i in range(n_expert)])

    def other_core(x):
        return other(x, 1)

    def other_dp(x):
        return lax.ppermute(x, "dp", [(0, 1), (1, 0)])

    def over_slice(x):
        return lax.all_to_all(x, ("dp", "expert"), 0, 0, axis_index_groups=slice_groups, tiled=True)

    outgoing, pick = call(
        functools.partial(route_kernel, dims),
        (sds((peers * unit, LANES), BF), sds((16, tok_rows), BF)),
        in_hbm(ids, gate_values.T, tokens, target),
        [HBM] * 4,
        [
            pltpu.VMEM(ids.shape, ids.dtype),
            pltpu.VMEM(ids.shape, F32),
            pltpu.VMEM(tokens.shape, tokens.dtype),
            pltpu.VMEM(target.shape, target.dtype),
            pltpu.VMEM((16, width), F32),
            pltpu.VMEM((16, width), F32),
            pltpu.VMEM((blocks * cap, LANES), F32),
            pltpu.VMEM((unit - blocks * cap, LANES), F32),
            pltpu.SemaphoreType.DMA((2 + 2 * n_dp,)),
        ],
        name="route",
    )
    first = -(-hid // (2 * LANES)) * LANES
    head = 2 * LANES

    def columns(size):
        return sds((width, size), w_gate.dtype), sds((width, size), w_up.dtype)

    def column_sems(size):
        return pltpu.SemaphoreType.DMA((-(-size // (2 * LANES)), 2))

    loaded, *weights = call(
        load_kernel,
        (sds((8, LANES), F32), *columns(head)),
        in_hbm(w_gate, w_up),
        [HBM] * 2,
        [column_sems(head)],
        flops=1_000_000_000,
        moved=8 * width * head,
        name="load_weights",
    )
    own, loaded = lax.optimization_barrier((over_slice(outgoing), loaded))
    *more, own_rows, own_target, own_gates = call(
        functools.partial(load_more_kernel, dims, head),
        (
            *columns(first - head),
            sds((cap * peers, width), BF),
            sds((cap * peers, LANES), F32),
            sds((cap * peers, LANES), F32),
        ),
        (place, own, *in_hbm(w_gate, w_up)),
        [SMEM, VMEM] + [HBM] * 2,
        [pltpu.VMEM((peers * unit, LANES), F32), column_sems(first - head)],
        flops=1_000_000_000,
        moved=8 * width * head,
        name="load_weights",
    )
    weights += more
    neighbour = other_core(own)
    chunks = [(0, first), (first, hid - first)]
    pres = []
    for start, size in chunks:
        outs = (sds((2, rows, size), F32), sds((2, rows, size), BF))
        cost = dict(flops=8 * rows * width * size, moved=4 * width * size)
        fetched = [
            pltpu.VMEM((width, size), w_gate.dtype),
            pltpu.VMEM((width, size), w_up.dtype),
            column_sems(size),
        ]
        if start == 0:
            all_rows, all_target, all_gates, *pre = call(
                functools.partial(first_pre_kernel, dims),
                (sds((rows, width), BF), sds((rows, LANES), F32), sds((rows, LANES), F32), *outs),
                (place, loaded, own_rows, own_target, own_gates, neighbour, *weights),
                [SMEM] + [VMEM] * 9,
                [pltpu.VMEM((peers * unit, LANES), F32)],
                name="pre_activations",
                **cost,
            )
        else:
            turned, *pre = call(
                functools.partial(more_pre_kernel, start),
                (sds((width, rows), BF), *outs),
                (all_rows, *in_hbm(w_gate, w_up)),
                [VMEM] + [HBM] * 2,
                fetched,
                name="pre_activations",
                **cost,
            )
        pres.append((pre[0], other_dp(pre[1])))
    (start, size), (start_b, size_b) = chunks
    half_rows = half * rows
    cost = dict(flops=4 * rows * width * size, moved=2 * width * size)
    up_deriv, act, total = call(
        functools.partial(first_down_kernel, dims, start),
        (sds((rows, size), F32), sds((rows, size), F32), sds((2 * half_rows, LANES), F32)),
        (place, *pres[0], w_down),
        [SMEM] + [VMEM] * 3,
        [pltpu.VMEM((rows, size), BF)],
        name="down",
        **cost,
    )
    up_deriv_b, act_b, hidden_b, send = call(
        functools.partial(send_down_kernel, dims, start_b),
        (
            sds((rows, size_b), F32),
            sds((rows, size_b), F32),
            sds((rows, size_b), BF),
            sds((half_rows, LANES), BF),
        ),
        (place, *pres[1], w_down, total),
        [SMEM] + [VMEM] * 4,
        name="down_send",
        **cost,
    )
    sent = other_core(send)
    keep = call(
        functools.partial(keep_down_kernel, dims, start_b),
        sds((half_rows, LANES), F32),
        (place, hidden_b, w_down, total),
        [SMEM] + [VMEM] * 3,
        name="down_keep",
        **cost,
    )
    saved = [(up_deriv, act), (up_deriv_b, act_b)]
    quad_rows = half_rows // 4
    kept, sent_on = sds((quad_rows, LANES), F32), sds((quad_rows, LANES), BF)
    keep, *sends = call(chip_sum_kernel, (kept, *[sent_on] * 3), (keep, sent), [VMEM] * 2, name="chip_sum")
    keep, send = call(
        residual_kernel,
        (kept, sent_on),
        (place, keep, *[other(sends[k], 2 * (k + 1)) for k in (2, 0, 1)], all_gates, all_target),
        [SMEM] + [VMEM] * 6,
        name="residual",
    )
    step = 8
    while 2 * step < n_expert:
        keep, send = call(line_sum_kernel, (kept, sent_on), (keep, other(send, step)), [VMEM] * 2, name="line_sum")
        step *= 2
    cot = call(
        cotangent_kernel,
        sent_on,
        (keep, other(send, step), all_gates),
        [VMEM] * 3,
        name="cotangent",
    )
    from_quad = [other(cot, 2 * k) for k in (1, 2, 3)]
    from_core = other_core(cot)

    def near(flip, flips, got, *total):
        return call(
            functools.partial(near_grad_hidden_kernel, flip, flips),
            sds((rows, hid), F32),
            (place, w_down, *got, *total),
            [SMEM] + [VMEM] * (1 + len(got) + len(total)),
            [pltpu.VMEM((rows, len(got) * quad_rows // rows * LANES), BF)],
            flops=len(got) * rows * width * hid // 4,
            moved=len(got) * width * hid // 4,
            name="grad_hidden_near",
        )

    own_total = near(0, (0,), (cot,))
    own_total = near(1, (0,), (from_core,), own_total)
    from_quad[2], own_total = lax.optimization_barrier((from_quad[2], own_total))
    from_both = [other_core(x) for x in from_quad]
    own_total = near(0, (1, 2, 3), from_quad, own_total)
    grads = []
    order = [1, 0]
    for k in order:
        start, size = chunks[k]
        outs = (sds((rows, size), F32), sds((rows, size), BF))
        cost = dict(flops=2 * rows * width * size, moved=2 * width * size)
        if k == order[0]:
            cot, *grad = call(
                functools.partial(first_grad_hidden_kernel, start),
                (sds((rows, 3 * width // 8), BF), *outs),
                (place, *from_both, w_down, own_total),
                [SMEM] + [VMEM] * 5,
                name="grad_hidden",
                **cost,
            )
        else:
            grad = call(
                functools.partial(more_grad_hidden_kernel, start),
                outs,
                (place, cot, w_down, own_total),
                [SMEM] + [VMEM] * 3,
                name="grad_hidden",
                **cost,
            )
        grads.append((grad[0], other_dp(grad[1])))
    pre_grads = [None] * len(chunks)
    total = ()
    peer_rows = peers * blocks * cap
    for k, grad in zip(order, grads):
        start, size = chunks[k]
        outs, scratch = (sds((rows, width), F32),), []
        if k == order[-1]:
            outs = (sds((peer_rows, LANES), F32), sds((peer_rows, LANES), BF))
            scratch = [pltpu.VMEM((2 * peer_rows, LANES), F32)]
        gate_pre_grad, up_pre_grad, *total = call(
            functools.partial(row_grad_kernel, dims, start, k == order[-1]),
            (sds((rows, size), BF), sds((rows, size), BF), *outs),
            (place, *grad, *saved[k], w_gate, w_up, *total),
            [SMEM] + [VMEM] * (6 + len(total)),
            scratch,
            flops=8 * rows * width * size,
            moved=4 * width * size,
            name="row_grad",
        )
        pre_grads[k] = (gate_pre_grad, up_pre_grad)
    keep, send = total
    chip_rows = add_cores(keep, other_core(send))
    got_rows = over_slice(chip_rows)
    pre_grads = [pair[0] for pair in pre_grads] + [pair[1] for pair in pre_grads]
    tile = 256
    gate_grad, up_grad = call(
        functools.partial(weight_grad_kernel, len(chunks), tile),
        (sds((width, hid), BF), sds((width, hid), BF)),
        (turned, *pre_grads),
        [VMEM] * (1 + len(pre_grads)),
        [
            pltpu.VMEM((width, hid), BF),
            pltpu.VMEM((width, hid), BF),
            pltpu.SemaphoreType.DMA((width // tile, 2)),
        ],
        flops=4 * rows * width * hid,
        moved=4 * width * hid,
        out_spec=HBM,
        name="weight_grads",
    )
    token_grad = call(
        functools.partial(token_grad_kernel, dims),
        sds((tok_rows, features), tokens.dtype),
        (pick, got_rows),
        [VMEM] * 2,
        [
            pltpu.VMEM((16, width), F32),
            pltpu.VMEM((tok_rows, features), tokens.dtype),
            pltpu.SemaphoreType.DMA((n_dp, 4)),
        ],
        out_spec=HBM,
        name="token_grad",
    )
    return token_grad, gate_grad, up_grad


def contract_last(matrix_a, matrix_b):
    return lax.dot_general(
        matrix_a, matrix_b, (((1,), (1,)), ((), ())), preferred_element_type=jnp.float32
    )


def rounded_terms(column_blocks, grad_blocks):
    terms = jnp.einsum(
        "krd,krh->kdh", column_blocks, grad_blocks, preferred_element_type=jnp.float32
    )
    terms = lax.optimization_barrier(terms.astype(jnp.bfloat16))
    return jnp.sum(terms.astype(jnp.float32), axis=0)


def spread_rows(rows, group_size, capacity, features):
    flat = rows.reshape(EXPERTS, 1, capacity * features)
    wide = jnp.broadcast_to(flat, (EXPERTS, group_size, capacity * features))
    return wide.reshape(EXPERTS * group_size * capacity, features)


def fold_group(rows, group_size, capacity, features):
    shaped = rows.reshape(EXPERTS, group_size, capacity * features).astype(jnp.float32)
    return jnp.sum(shaped, axis=1).reshape(EXPERTS * capacity, features)


def general_shards(tokens, expert_ids, gate_values, w_gate, w_up, w_down, target):
    devices_along = lax.axis_size("expert")
    group_size = devices_along // EXPERTS
    tok_rows = tokens.shape[0]
    features = tokens.shape[1]
    hid_local = w_gate.shape[1]
    capacity = max(2, 3 * tok_rows // 128)
    slot_total = EXPERTS * capacity
    flat_ids = expert_ids.reshape(-1)
    pair_count = flat_ids.shape[0]
    window = flat_ids < EXPERTS
    onehot = (flat_ids[:, None] == jnp.arange(EXPERTS, dtype=jnp.int32)[None, :]).astype(jnp.int32)
    slot_index = jnp.sum((jnp.cumsum(onehot, axis=0) - onehot) * onehot, axis=1)
    position = jnp.where(window, flat_ids * capacity + slot_index, slot_total)
    owning = jnp.arange(pair_count, dtype=jnp.int32) // 2
    slot_token = jnp.zeros((slot_total + 1,), jnp.int32).at[position].set(owning)[:slot_total]
    slot_live = jnp.zeros((slot_total + 1,), jnp.bool_).at[position].set(True)[:slot_total]
    slot_gate = (
        jnp.zeros((slot_total + 1,), jnp.float32)
        .at[position]
        .set(gate_values.reshape(-1))[:slot_total]
    )
    safe_pairs = jnp.minimum(position, slot_total - 1).reshape(tok_rows, 2)
    live_pairs = window.reshape(tok_rows, 2)

    def pick(table, column):
        return jnp.where(live_pairs[:, column : column + 1], table[safe_pairs[:, column]], 0.0)

    outgoing = jnp.where(slot_live[:, None], tokens[slot_token], jnp.zeros((), tokens.dtype))
    outgoing = spread_rows(outgoing, group_size, capacity, features)
    received = lax.all_to_all(outgoing, "expert", split_axis=0, concat_axis=0, tiled=True)
    rows_count = received.shape[0]
    full_gate, full_up, full_down = (
        lax.all_gather(w_gate, "dp", axis=0, tiled=True),
        lax.all_gather(w_up, "dp", axis=0, tiled=True),
        lax.all_gather(w_down, "dp", axis=1, tiled=True),
    )
    gate_pre = jnp.dot(received, full_gate, preferred_element_type=jnp.float32)
    up_pre = jnp.dot(received, full_up, preferred_element_type=jnp.float32)
    sigmoid_gate = jax.nn.sigmoid(gate_pre)
    activated = sigmoid_gate * gate_pre
    hidden = (activated * up_pre).astype(jnp.bfloat16)
    partial_out = jnp.dot(hidden, full_down, preferred_element_type=jnp.float32).astype(
        jnp.bfloat16
    )
    returned_out = lax.all_to_all(partial_out, "expert", split_axis=0, concat_axis=0, tiled=True)
    expert_out = fold_group(returned_out, group_size, capacity, features)
    combined = gate_values[:, 0:1] * pick(expert_out, 0) + gate_values[:, 1:2] * pick(expert_out, 1)
    residual = combined - target.astype(jnp.float32)
    outgoing_grad = jnp.where(
        slot_live[:, None], slot_gate[:, None] * residual[slot_token], 0.0
    ).astype(jnp.bfloat16)
    outgoing_grad = spread_rows(outgoing_grad, group_size, capacity, features)
    cotangent = lax.all_to_all(outgoing_grad, "expert", split_axis=0, concat_axis=0, tiled=True)
    grad_hidden = contract_last(cotangent, full_down)
    derivative = sigmoid_gate * (1.0 + gate_pre * (1.0 - sigmoid_gate))
    grad_gate_pre = (grad_hidden * up_pre * derivative).astype(jnp.bfloat16)
    grad_up_pre = (grad_hidden * activated).astype(jnp.bfloat16)
    row_part = (
        contract_last(grad_gate_pre, full_gate) + contract_last(grad_up_pre, full_up)
    ).astype(jnp.bfloat16)
    back_rows = lax.all_to_all(row_part, "expert", split_axis=0, concat_axis=0, tiled=True)
    row_grad = fold_group(back_rows, group_size, capacity, features)
    token_grad = (pick(row_grad, 0) + pick(row_grad, 1)).astype(jnp.bfloat16)
    shard_columns = lax.all_to_all(received, "dp", split_axis=1, concat_axis=0, tiled=True)
    shard_width = shard_columns.shape[1]
    dp_count = lax.axis_size("dp")
    every_gate, every_up = (
        lax.all_gather(grad_gate_pre, "dp", axis=0, tiled=True),
        lax.all_gather(grad_up_pre, "dp", axis=0, tiled=True),
    )
    column_blocks = shard_columns.reshape(dp_count, rows_count, shard_width)
    gate_sum = rounded_terms(column_blocks, every_gate.reshape(dp_count, rows_count, hid_local))
    up_sum = rounded_terms(column_blocks, every_up.reshape(dp_count, rows_count, hid_local))
    return (token_grad, gate_sum.astype(jnp.bfloat16), up_sum.astype(jnp.bfloat16))


def solution(mesh):
    n_dp, n_expert = mesh.shape["dp"], mesh.shape["expert"]

    def shards(*args):
        tok_rows, features = args[0].shape
        width, hid = args[3].shape
        cap = max(2, 3 * tok_rows // 128)
        whole_blocks = (
            n_dp == 2
            and n_expert % 16 == 0
            and n_expert & (n_expert - 1) == 0
            and width == n_expert * LANES
            and hid % LANES == 0
            and hid > 4 * LANES
            and cap <= 8
            and tok_rows % LANES == 0
        )
        if whole_blocks:
            return fast_shards(n_dp, n_expert, cap, *args)
        return general_shards(*args)

    placed = (
        P(("dp", "expert"), None),
        P(("dp", "expert"), None),
        P(("dp", "expert"), None),
        P("dp", "expert"),
        P("dp", "expert"),
        P("expert", "dp"),
        P(("dp", "expert"), None),
    )
    return jax.shard_map(
        shards,
        mesh=mesh,
        in_specs=placed,
        out_specs=(P(("dp", "expert"), None), P("dp", "expert"), P("dp", "expert")),
        check_vma=False,
    )
```
